256 devices in a mesh: dp: 64 (over z, y_lo, x), split: 4 (over y_hi, core).
Axes of the slice: x: 4, y: 4 (y_hi: 2, y_lo: 2; y = y_hi * 2 + y_lo), z: 8, core: 2. Of those that a mesh axis runs over, the one named last changes fastest.
Arguments:
- picture_vectors: bfloat16 [16384, 1152], P('dp'), may hold values from -0.59765625 to 0.59765625
- caption_vectors: bfloat16 [16384, 1152], P('dp'), may hold values from -0.59765625 to 0.59765625
- sharpness_entry: float32 [1], replicated, may hold values from 4 to 16
- offset_shift: float32 [1], replicated, may hold values from -4 to -1
Outputs:
- picture_derivative: float32 [16384, 1152], P('dp')
- text_grad: float32 [16384, 1152], P('dp')
- image_loss: float32 [16384], P('dp')
The draws below stay inside these ranges and needn't reach their ends.
All inputs are finite; a program needn't handle non-finite values.
Results may differ from the reference program's by a relative error of at most 0.0058.
Values may be sent and summed in bfloat16 or wider, within the bound.
A program may use at most 64 MiB of HBM per device.

```python
import math
import jax
import jax.numpy as jnp
from jax import lax

D = 1152
ROWS_DEV = 256
PAIRS = 16384


def block_levels(own_key, extent, shards, low, top_value):
    loudness, own = 1.0, jax.random.fold_in(own_key, 6)
    for position, shards_of in shards:
        draws = jnp.exp(jax.random.uniform(jax.random.fold_in(own, position), (shards_of,), jnp.float32, low / len(shards), top_value / len(shards)))
        loudness = loudness * jnp.repeat(draws, extent[position] // shards_of).reshape([-1 if axis == position else 1 for axis in range(len(extent))])
    return loudness


def gaussian(key, extent, spread, bound, cuts=(), kind=jnp.bfloat16):
    array = spread * jax.random.normal(key, extent, jnp.float32)
    if cuts:
        array = array * block_levels(key, extent, cuts, -0.22, 0.18)
    return jnp.clip(array, -bound, bound).astype(kind)


def setup_inputs(seed: int = 0) -> dict:
    keys = jax.random.split(jax.random.key(seed), 5)
    return {
        "picture_vectors": gaussian(keys[0], (PAIRS, D), 0.1, 0.59765625, ((0, 64),)),
        "caption_vectors": gaussian(keys[1], (PAIRS, D), 0.1, 0.59765625, ((0, 64),)),
        "sharpness_entry": jnp.clip(jnp.exp(jax.random.uniform(keys[2], (1,), jnp.float32, math.log(4.0), math.log(16.0))), 4.0, 16.0),
        "offset_shift": jnp.clip(jax.random.uniform(keys[3], (1,), jnp.float32, -4.0, -1.0), -4.0, -1.0),
    }


def rescale_to_length(rows):
    values = rows.astype(jnp.float32)
    inverse = lax.rsqrt(lax.optimization_barrier(jnp.sum(values * values, axis=1, keepdims=True)) + 1e-06)
    return (inverse, values * inverse)

def unit_back(unit, inverse, grad):
    return (grad - unit * lax.optimization_barrier(jnp.sum(unit * grad, axis=1, keepdims=True))) * inverse

def reference(picture_vectors, caption_vectors, sharpness_entry, offset_shift):
    img_inv, image_unit = rescale_to_length(picture_vectors)
    txt_inv, text_unit = rescale_to_length(caption_vectors)
    img_b = image_unit.astype(jnp.bfloat16)
    txt_b = text_unit.astype(jnp.bfloat16)
    sharpness_factor = sharpness_entry[0]
    offset = offset_shift[0]
    blocks = PAIRS // ROWS_DEV
    columns = jnp.arange(PAIRS, dtype=jnp.int32)

    def one_block(carry, index):
        start = (index * ROWS_DEV).astype(jnp.int32)
        block = lax.dynamic_slice_in_dim(img_b, start, ROWS_DEV, 0)
        logits = sharpness_factor * lax.dot_general(block, txt_b, (((1,), (1,)), ((), ())), preferred_element_type=jnp.float32) + offset
        row_ids = start + jnp.arange(ROWS_DEV, dtype=jnp.int32)
        label = jnp.where(row_ids[:, None] == columns[None, :], 1.0, -1.0).astype(jnp.float32)
        pair_loss = jax.nn.softplus(-label * logits)
        coef_b = (-label * jax.nn.sigmoid(-label * logits)).astype(jnp.bfloat16)
        img_part = jnp.dot(coef_b, txt_b, preferred_element_type=jnp.float32)
        text_partial = lax.dot_general(coef_b, block, (((0,), (0,)), ((), ())), preferred_element_type=jnp.float32)
        return (carry + text_partial, (img_part, lax.optimization_barrier(jnp.sum(pair_loss, axis=1))))
    zeros = jnp.zeros((PAIRS, D), jnp.float32)
    txt_sum, (img_parts, losses) = lax.scan(one_block, zeros, jnp.arange(blocks, dtype=jnp.int32))
    img_sum = img_parts.reshape(PAIRS, D)
    image_loss = losses.reshape(PAIRS) / PAIRS
    picture_derivative = unit_back(image_unit, img_inv, sharpness_factor * img_sum)
    text_grad = unit_back(text_unit, txt_inv, sharpness_factor * txt_sum)
    return (picture_derivative, text_grad, image_loss)
```

```python
import jax
import jax.numpy as jnp
from jax import lax
from jax.experimental import pallas as pl
from jax.experimental.pallas import tpu as pltpu
from jax.sharding import PartitionSpec as P

MESH = pl.DeviceIdType.MESH
F32 = jnp.float32
BF16 = jnp.bfloat16

NX, NY, NZ = 4, 4, 8
ROWS, WIDTH = 256, 1152
HALF, QUARTER, EIGHTH = 128, 64, 32
PAIRS = 16384


def unit_rows(values):
    values = values.astype(F32)
    inverse = lax.rsqrt(jnp.sum(values * values, axis=1, keepdims=True) + 1e-06)
    return inverse, values * inverse


def unit_back(unit, inverse, grad):
    return (grad - unit * jnp.sum(unit * grad, axis=1, keepdims=True)) * inverse


def contract(a, b, dims):
    return lax.dot_general(a, b, (dims, ((), ())), preferred_element_type=F32)


def kernel(
    pic_hbm, cap_hbm, sharp_ref, off_ref,
    img_out, txt_out, loss_out,
    pic, cap, ibuf, jbuf, cbuf, ctbuf, pacc, tacc, lacc,
    pb, xr1, x2, rb, qr,
    ts, tr, vs, vr,
    ls, lx, rl, lq,
    hop,
    in_sem, i_s, i_r, t_s, t_r, d_s, d_r, x1_s, x1_r, x2_s, x2_r, y_s, y_r,
    ly_s, ly_r, lx_s, lx_r, e_s, e_r, v_s, v_r, g_s, g_r,
):
    dp, split = lax.axis_index("dp"), lax.axis_index("split")
    x = lax.rem(dp, NX)
    yl = lax.rem(dp // NX, 2)
    z = dp // (2 * NX)
    yh, core = split // 2, lax.rem(split, 2)
    y = 2 * yh + yl
    other = 1 - core
    first = core == 0
    second = core == 1

    def at(px, py, pz, pc):
        px, py, pz = lax.rem(px, NX), lax.rem(py, NY), lax.rem(pz, NZ)
        return ((pz * 2 + lax.rem(py, 2)) * NX + px, (py // 2) * 2 + pc)

    sibling = at(x, y, z, other)
    x_up, x_down, x_far = (at(x + k, y, z, core) for k in (1, 3, 2))
    z_up, z_down = at(x, y, z + 1, core), at(x, y, z + 7, core)
    y_up1, y_down1 = at(x, y + 1, z, 1), at(x, y + 3, z, 1)

    own_text = pl.multiple_of(yh * HALF, HALF)
    fetch_text = pltpu.make_async_copy(cap_hbm.at[pl.ds(own_text, HALF)], cap, in_sem.at[0])
    fetch_image = pltpu.make_async_copy(pic_hbm, pic, in_sem.at[1])
    fetch_text.start()
    fetch_image.start()

    barrier = pltpu.get_barrier_semaphore()
    partners = [sibling, x_up, x_down, x_far, z_up, z_down]
    partners += [at(x, y + k, z, c) for k in (1, 2, 3) for c in (0, 1)]
    for partner in partners:
        pl.semaphore_signal(barrier, inc=1, device_id=partner, device_id_type=MESH)

    pending = []

    def copy(src, dst, send, recv, to):
        return pltpu.make_async_remote_copy(
            src_ref=src, dst_ref=dst, send_sem=send, recv_sem=recv, device_id=to, device_id_type=MESH
        )

    def send(src, dst, ssem, rsem, to):
        one = copy(src, dst, ssem, rsem, to)
        one.start()
        pending.append((None, one))

    def send_when(cond, *copies):
        made = [copy(*c) for c in copies]

        @pl.when(cond)
        def _():
            for one in made:
                one.start()

        pending.extend((cond, one) for one in made)

    def landed(dst, rsem):
        copy(dst, dst, e_s.at[0], rsem, sibling).wait_recv()

    sharp, off = sharp_ref[0], off_ref[0]

    fetch_text.wait()
    jbuf[0:HALF, :] = unit_rows(cap[...])[1].astype(BF16)
    fetch_image.wait()

    @pl.when(first)
    def _():
        ibuf[0:ROWS, :] = unit_rows(pic[...])[1].astype(BF16)

    pl.semaphore_wait(barrier, len(partners))

    def irows(slot, half):
        return ibuf.at[pl.ds(slot * ROWS + half * HALF, HALF)]

    def jrows(slot, c, start=0, count=QUARTER):
        return jbuf.at[pl.ds(pl.multiple_of(slot * HALF + c * QUARTER + start, EIGHTH), count)]

    send(jrows(0, core), jrows(2, core), t_s.at[0, 0], t_r.at[0, 0], z_up)
    send(jrows(0, core), jrows(1, core), t_s.at[1, 0], t_r.at[1, 0], z_down)

    def to_y(slot, half):
        target = y_down1 if half else y_up1
        return (irows(slot, half), irows(slot, half), i_s.at[6 + 2 * slot + half], i_r.at[slot, half], target)

    send_when(
        first,
        (irows(0, 0), irows(1, 0), i_s.at[0], i_r.at[1, 0], x_up),
        (irows(0, 1), irows(2, 1), i_s.at[1], i_r.at[2, 1], x_down),
        to_y(0, 0),
        to_y(0, 1),
        (irows(0, 1), irows(1, 1), i_s.at[2], i_r.at[1, 1], x_up),
        (irows(0, 0), irows(2, 0), i_s.at[3], i_r.at[2, 0], x_down),
    )

    lacc[...] = jnp.zeros_like(lacc)

    def swap(slot):
        send(jrows(slot, core), jrows(slot, core), d_s.at[slot], d_r.at[slot], sibling)

    def swapped(*slots):
        for slot in slots:
            landed(jrows(slot, other), d_r.at[slot])

    def text_hop(d):
        if d < 4:
            landed(jrows(2 * d, core), t_r.at[0, d - 1])
            landed(jrows(2 * d - 1, core), t_r.at[1, d - 1])
        else:
            landed(jrows(7, core, 0, EIGHTH), t_r.at[0, 3])
            landed(jrows(7, core, EIGHTH, EIGHTH), t_r.at[1, 3])
        if d < 3:
            send(jrows(2 * d, core), jrows(2 * d + 2, core), t_s.at[0, d], t_r.at[0, d], z_up)
            send(jrows(2 * d - 1, core), jrows(2 * d + 1, core), t_s.at[1, d], t_r.at[1, d], z_down)
        elif d == 3:
            send(jrows(6, core, 0, EIGHTH), jrows(7, core, 0, EIGHTH), t_s.at[0, 3], t_r.at[0, 3], z_up)
            send(
                jrows(5, core, EIGHTH, EIGHTH), jrows(7, core, EIGHTH, EIGHTH), t_s.at[1, 3], t_r.at[1, 3], z_down
            )
        if d < 4:
            swap(2 * d - 1)
            swap(2 * d)
        else:
            swap(7)

    log2_e = 1.4426950408889634
    sharp2, off2 = sharp * log2_e, off * log2_e

    def logits_block(i, j):
        ri, rj = slice(i * ROWS, (i + 1) * ROWS), slice(j * ROWS, (j + 1) * ROWS)
        logits = sharp2 * contract(ibuf[ri, :], jbuf[rj, :], ((1,), (1,))) + off2
        if (i, j) == (0, 0):
            row = lax.broadcasted_iota(jnp.int32, (ROWS, ROWS), 0)
            col = lax.broadcasted_iota(jnp.int32, (ROWS, ROWS), 1)
            same = jnp.logical_and(jnp.logical_and(row == col + yh * HALF, col < HALF), first)
            logits = jnp.where(same, -logits, logits)
        grown = jnp.exp2(logits)
        total = 1.0 + grown
        rough = pl.reciprocal(total, approx=True)
        inverse = rough * (2.0 - total * rough)
        coef = grown * inverse
        lost = (grown - (total - 1.0)) * inverse
        lacc[ri, :] += jnp.log(total[:, :HALF] * total[:, HALF:]) + (lost[:, :HALF] + lost[:, HALF:])
        if (i, j) == (0, 0):
            coef = jnp.where(same, -coef, coef)
        coef = coef.astype(BF16)
        cbuf[ri, rj] = coef
        ctbuf[rj, ri] = coef.T

    def product(out, left, right, m, k0, k1):
        rows, depth = slice(m * ROWS, (m + 1) * ROWS), slice(k0 * ROWS, k1 * ROWS)
        a = left[rows, depth]
        for n in range(0, WIDTH, 256):
            columns = slice(n, min(n + 256, WIDTH))
            result = contract(a, right[depth, columns], ((1,), (0,)))
            out[rows, columns] = result if k0 == 0 else out[rows, columns] + result

    def image_product(i, j0, j1):
        product(pacc, cbuf, jbuf, i, j0, j1)

    def text_product(j, i0, i1):
        product(tacc, ctbuf, ibuf, j, i0, i1)

    @pl.when(first)
    def _():
        landed(irows(1, 0), i_r.at[1, 0])
        landed(irows(2, 1), i_r.at[2, 1])

    send_when(
        first,
        (irows(1, 0), irows(3, 0), i_s.at[4], i_r.at[3, 0], x_up),
        (irows(2, 1), irows(3, 1), i_s.at[5], i_r.at[3, 1], x_down),
        to_y(1, 0),
        to_y(2, 1),
    )
    text_hop(1)

    @pl.when(second)
    def _():
        landed(irows(0, 0), i_r.at[0, 0])
        landed(irows(0, 1), i_r.at[0, 1])

    swapped(1)
    logits_block(0, 0)

    @pl.when(first)
    def _():
        landed(irows(1, 1), i_r.at[1, 1])
        landed(irows(2, 0), i_r.at[2, 0])

    send_when(first, to_y(1, 1), to_y(2, 0))
    text_hop(2)
    swapped(2, 3)
    logits_block(0, 1)

    @pl.when(first)
    def _():
        landed(irows(3, 0), i_r.at[3, 0])
        landed(irows(3, 1), i_r.at[3, 1])

    send_when(first, to_y(3, 0), to_y(3, 1))
    text_hop(3)

    @pl.when(second)
    def _():
        for slot in (1, 2):
            for half in (0, 1):
                landed(irows(slot, half), i_r.at[slot, half])

    logits_block(1, 0)
    image_product(0, 0, 2)
    logits_block(2, 0)
    logits_block(1, 1)
    text_product(0, 0, 3)
    logits_block(2, 1)
    swapped(4, 5)
    logits_block(0, 2)
    text_product(1, 0, 3)
    logits_block(1, 2)
    image_product(1, 0, 2)
    logits_block(2, 2)
    text_hop(4)
    image_product(2, 0, 3)
    text_product(2, 0, 3)
    swapped(6, 7)
    logits_block(0, 3)
    logits_block(1, 3)
    image_product(1, 2, 4)
    logits_block(2, 3)
    image_product(2, 3, 4)
    text_product(3, 0, 3)

    @pl.when(second)
    def _():
        landed(irows(3, 0), i_r.at[3, 0])
        landed(irows(3, 1), i_r.at[3, 1])

    logits_block(3, 0)
    logits_block(3, 1)
    logits_block(3, 2)
    logits_block(3, 3)
    image_product(3, 0, 4)

    up_hi = lax.rem(y + 1, NY) // 2
    turns = (
        other * 2 * (1 - yh) + core * (2 * up_hi + 1),
        other * (2 * yh + 1) + core * 2 * up_hi,
        other * (2 * (1 - yh) + 1) + core * 2 * (1 - up_hi),
        other * 2 * yh + core * (2 * (1 - up_hi) + 1),
    )

    def seat(k):
        return pl.ds(k * QUARTER, QUARTER)

    def part_rows(slot, k):
        return pl.ds(pl.multiple_of(slot * ROWS + turns[k] * QUARTER, QUARTER), QUARTER)

    def far_turn(k):
        pb[0, seat(k), :] = pacc[part_rows(3, k), :].astype(BF16)
        send(pb.at[0, seat(k)], xr1.at[seat(k)], x1_s.at[k], x1_r.at[k], x_up if k < 2 else x_down)

    def near_turn(slot, k):
        side = 0 if slot == 2 else 1
        rows = pacc[part_rows(slot, k), :]
        if (k < 2) == (slot == 2):
            landed(xr1.at[seat(k)], x1_r.at[k])
            rows = rows + xr1[seat(k), :].astype(F32)
        pb[1 + side, seat(k), :] = rows.astype(BF16)
        send(
            pb.at[1 + side, seat(k)],
            x2.at[side, seat(k)],
            x2_s.at[side, k],
            x2_r.at[side, k],
            x_down if side else x_up,
        )

    def text_over(*slots):
        for slot in slots:
            mine = pl.ds(pl.multiple_of(slot * HALF + other * QUARTER, QUARTER), QUARTER)
            ts[slot] = tacc[mine, :].astype(BF16)
            send(ts.at[slot], tr.at[slot], e_s.at[slot], e_r.at[slot], sibling)

    for k in (0, 2, 1, 3):
        far_turn(k)
    text_product(3, 3, 4)
    text_over(7, 6)
    near_turn(2, 2)
    near_turn(1, 0)
    near_turn(2, 3)
    near_turn(1, 1)
    text_product(2, 3, 4)
    text_over(5, 4)
    text_product(1, 3, 4)
    text_product(0, 3, 4)
    text_over(3, 2, 1, 0)
    image_product(0, 2, 4)

    ones = jnp.ones((8, HALF), F32)
    for i in range(4):
        ls[i] = lax.dot_general(
            ones,
            lacc[i * ROWS : (i + 1) * ROWS, :],
            (((1,), (1,)), ((), ())),
            precision=lax.Precision.HIGHEST,
            preferred_element_type=F32,
        )
    send(ls.at[2], lx.at[0], lx_s.at[0], lx_r.at[0], x_up)
    send(ls.at[1], lx.at[1], lx_s.at[1], lx_r.at[1], x_down)
    send(ls.at[3], lx.at[2], lx_s.at[2], lx_r.at[2], x_far)

    def text_sum(slot):
        landed(tr.at[slot], e_r.at[slot])
        mine = pl.ds(pl.multiple_of(slot * HALF + core * QUARTER, QUARTER), QUARTER)
        return tacc[mine, :] + tr[slot].astype(F32)

    def text_back(d):
        if d == 4:
            both = text_sum(7).astype(BF16)
            for side in (0, 1):
                vs[side, 3, 0:EIGHTH, :] = both[side * EIGHTH : (side + 1) * EIGHTH]
                part = pl.ds(0, EIGHTH)
                send(
                    vs.at[side, 3, part],
                    vr.at[side, 3, part],
                    v_s.at[side, 3],
                    v_r.at[side, 3],
                    z_down if side else z_up,
                )
            return
        for side in (0, 1):
            rows = text_sum(2 * d if side else 2 * d - 1)
            if d == 3:
                part = pl.ds(0, EIGHTH)
                landed(vr.at[side, 3, part], v_r.at[side, 3])
                came = vr[side, 3, 0:EIGHTH, :].astype(F32)
                if side:
                    vs[side, 2, 0:EIGHTH, :] = rows[:EIGHTH].astype(BF16)
                    vs[side, 2, EIGHTH:QUARTER, :] = (rows[EIGHTH:] + came).astype(BF16)
                else:
                    vs[side, 2, 0:EIGHTH, :] = (rows[:EIGHTH] + came).astype(BF16)
                    vs[side, 2, EIGHTH:QUARTER, :] = rows[EIGHTH:].astype(BF16)
            else:
                landed(vr.at[side, d], v_r.at[side, d])
                vs[side, d - 1] = (rows + vr[side, d].astype(F32)).astype(BF16)
            send(
                vs.at[side, d - 1],
                vr.at[side, d - 1],
                v_s.at[side, d - 1],
                v_r.at[side, d - 1],
                z_down if side else z_up,
            )

    text_back(4)
    near_turn(2, 0)
    near_turn(1, 2)
    text_back(3)
    near_turn(2, 1)
    near_turn(1, 3)
    text_back(2)

    source = yh + 2 * core
    block_yl = lax.rem(yl + core, 2)

    def owner_of(q):
        to = at(x, 2 * (q // 2) + block_yl, z, q % 2)
        return to, jnp.logical_and(dp == to[0], split == to[1])

    for k in range(3):
        landed(lx.at[k], lx_r.at[k])
    rl[...] = ls[0] + lx[0] + lx[1] + lx[2]
    for q in range(4):
        to, own = owner_of(q)
        send_when(jnp.logical_not(own), (rl, lq.at[source], ly_s.at[q], ly_r.at[source], to))

        @pl.when(own)
        def _():
            lq[source] = rl[...]

    text_back(1)

    y_up0, y_down0 = at(x, y + 1, z, 0), at(x, y + 3, z, 0)

    def image_sum(k):
        landed(x2.at[0, seat(k)], x2_r.at[0, k])
        landed(x2.at[1, seat(k)], x2_r.at[1, k])
        return pacc[part_rows(0, k), :] + (x2[0, seat(k), :].astype(F32) + x2[1, seat(k), :].astype(F32))

    def image_out(k):
        total = image_sum(k)
        rb[seat(k), :] = total.astype(BF16)
        if k == 0:
            box = other * 3 + core
            send(rb.at[seat(0)], qr.at[box], y_s.at[0], y_r.at[box], y_up1)
        elif k == 2:
            box = other * 4 + core * 2
            send(rb.at[seat(2)], qr.at[box], y_s.at[2], y_r.at[box], (y_down1[0], y_down0[1] + other))
        else:
            carried = 3 if k == 1 else 4
            box, to = (1, y_up0) if k == 1 else (2, y_down1)

            @pl.when(second)
            def _():
                landed(qr.at[carried], y_r.at[carried])
                rb[seat(k), :] = (total + qr[carried].astype(F32)).astype(BF16)

            send_when(second, (rb.at[seat(k)], qr.at[box], y_s.at[k], y_r.at[box], to))
            if k == 1:
                send_when(first, (rb.at[seat(1)], qr.at[0], y_s.at[1], y_r.at[0], sibling))
            else:

                @pl.when(first)
                def _():
                    qr[0] = rb[seat(3), :]

    image_out(0)
    image_out(2)

    mine = yh * 2 + core
    outs = (img_out, txt_out)

    def quarter_rows(q, start=0, count=QUARTER):
        return pl.ds(pl.multiple_of(q * QUARTER + start, EIGHTH), count)

    my_rows = quarter_rows(mine)
    y_up, y_down = at(x, y + 1, z, core), at(x, y + 3, z, core)

    def gather_out(kind, grad, values):
        inverse, unit = unit_rows(values)
        out = outs[kind]
        out[my_rows, :] = unit_back(unit, inverse, sharp * grad).astype(BF16)
        low, high = out.at[quarter_rows(mine, 0, EIGHTH)], out.at[quarter_rows(mine, EIGHTH, EIGHTH)]
        send(low, hop.at[kind, 0], g_s.at[kind, 0], g_r.at[kind, 0], y_up)
        send(high, hop.at[kind, 1], g_s.at[kind, 1], g_r.at[kind, 1], y_down)
        send(out.at[my_rows], out.at[my_rows], g_s.at[kind, 2], g_r.at[kind, 2], sibling)

    def gather_on(kind):
        out = outs[kind]
        landed(hop.at[kind, 0], g_r.at[kind, 0])
        there = out.at[quarter_rows(2 * (1 - up_hi) + core, 0, EIGHTH)]
        send(hop.at[kind, 0], there, g_s.at[kind, 3], g_r.at[kind, 3], y_up)
        landed(hop.at[kind, 1], g_r.at[kind, 1])
        there = out.at[quarter_rows(2 * up_hi + core, EIGHTH, EIGHTH)]
        send(hop.at[kind, 1], there, g_s.at[kind, 4], g_r.at[kind, 4], y_down)

    def gather_over(kind):
        for half in (0, 1):
            here = outs[kind].at[quarter_rows((1 - yh) * 2 + core, half * EIGHTH, EIGHTH)]
            landed(here, g_r.at[kind, 3 + half])
            send(here, here, g_s.at[kind, 5 + half], g_r.at[kind, 5 + half], sibling)

    def gather_end(kind):
        landed(outs[kind].at[quarter_rows(yh * 2 + other)], g_r.at[kind, 2])
        for half in (0, 1):
            here = outs[kind].at[quarter_rows((1 - yh) * 2 + other, half * EIGHTH, EIGHTH)]
            landed(here, g_r.at[kind, 5 + half])

    grad = text_sum(0)
    for side in (0, 1):
        landed(vr.at[side, 0], v_r.at[side, 0])
        grad = grad + vr[side, 0].astype(F32)
    gather_out(1, grad, cap[pl.ds(pl.multiple_of(core * QUARTER, QUARTER), QUARTER), :])

    gather_on(1)
    image_out(1)
    image_out(3)
    gather_over(1)

    for k in range(4):
        here = jnp.logical_and(first, yh == k)

        @pl.when(jnp.logical_not(here))
        def _():
            landed(lq.at[k], ly_r.at[k])

    loss_out[...] = ((lq[0] + lq[1]) + (lq[2] + lq[3])) * (1.0 / PAIRS)

    @pl.when(second)
    def _():
        landed(qr.at[0], y_r.at[0])

    landed(qr.at[1], y_r.at[1])
    landed(qr.at[2], y_r.at[2])
    grad = qr[0].astype(F32) + (qr[1].astype(F32) + qr[2].astype(F32))
    gather_out(0, grad, pic[my_rows, :])
    gather_on(0)
    gather_over(0)
    gather_end(1)
    gather_end(0)

    for cond, one in pending:
        if cond is None:
            one.wait_send()
        else:

            @pl.when(cond)
            def _():
                one.wait_send()


def per_device(picture_vectors, caption_vectors, sharpness_entry, offset_shift):
    dma = pltpu.SemaphoreType.DMA
    vmem = pl.BlockSpec(memory_space=pltpu.VMEM)
    smem = pl.BlockSpec(memory_space=pltpu.SMEM)
    hbm = pl.BlockSpec(memory_space=pltpu.HBM)
    img, txt, loss = pl.pallas_call(
        kernel,
        out_shape=(
            jax.ShapeDtypeStruct((ROWS, WIDTH), BF16),
            jax.ShapeDtypeStruct((ROWS, WIDTH), BF16),
            jax.ShapeDtypeStruct((8, ROWS), F32),
        ),
        in_specs=[hbm, hbm, smem, smem],
        out_specs=(vmem, vmem, vmem),
        scratch_shapes=[
            pltpu.VMEM((ROWS, WIDTH), BF16),
            pltpu.VMEM((HALF, WIDTH), BF16),
            pltpu.VMEM((4 * ROWS, WIDTH), BF16),
            pltpu.VMEM((8 * HALF, WIDTH), BF16),
            pltpu.VMEM((4 * ROWS, 8 * HALF), BF16),
            pltpu.VMEM((8 * HALF, 4 * ROWS), BF16),
            pltpu.VMEM((4 * ROWS, WIDTH), F32),
            pltpu.VMEM((8 * HALF, WIDTH), F32),
            pltpu.VMEM((4 * ROWS, HALF), F32),
            pltpu.VMEM((3, ROWS, WIDTH), BF16),
            pltpu.VMEM((ROWS, WIDTH), BF16),
            pltpu.VMEM((2, ROWS, WIDTH), BF16),
            pltpu.VMEM((ROWS, WIDTH), BF16),
            pltpu.VMEM((5, QUARTER, WIDTH), BF16),
            pltpu.VMEM((8, QUARTER, WIDTH), BF16),
            pltpu.VMEM((8, QUARTER, WIDTH), BF16),
            pltpu.VMEM((2, 4, QUARTER, WIDTH), BF16),
            pltpu.VMEM((2, 4, QUARTER, WIDTH), BF16),
            pltpu.VMEM((4, 8, ROWS), F32),
            pltpu.VMEM((3, 8, ROWS), F32),
            pltpu.VMEM((8, ROWS), F32),
            pltpu.VMEM((4, 8, ROWS), F32),
            pltpu.VMEM((2, 2, EIGHTH, WIDTH), BF16),
            dma((2,)),
            dma((14,)), dma((4, 2)),
            dma((2, 4)), dma((2, 4)),
            dma((8,)), dma((8,)),
            dma((4,)), dma((4,)),
            dma((2, 4)), dma((2, 4)),
            dma((4,)), dma((5,)),
            dma((4,)), dma((4,)),
            dma((3,)), dma((3,)),
            dma((8,)), dma((8,)),
            dma((2, 4)), dma((2, 4)),
            dma((2, 7)), dma((2, 7)),
        ],
        compiler_params=pltpu.CompilerParams(
            collective_id=0, has_side_effects=True, vmem_limit_bytes=48 * 1024 * 1024
        ),
        cost_estimate=pl.CostEstimate(flops=7_300_000_000, bytes_accessed=4_000_000, transcendentals=3_000_000),
    )(
        pltpu.with_memory_space_constraint(picture_vectors, pltpu.HBM),
        pltpu.with_memory_space_constraint(caption_vectors, pltpu.HBM),
        sharpness_entry,
        offset_shift,
    )
    return img.astype(F32), txt.astype(F32), loss[0]


def solution(mesh):
    placed = (P("dp", None), P("dp", None), P(), P())
    return jax.shard_map(
        per_device,
        mesh=mesh,
        in_specs=placed,
        out_specs=(P("dp", None), P("dp", None), P("dp")),
        check_vma=False,
    )
```

```python
import math

import jax
import jax.numpy as jnp
from jax import lax
from jax.experimental import pallas as pl
from jax.experimental.pallas import tpu as pltpu
from jax.sharding import PartitionSpec as P

MESH = pl.DeviceIdType.MESH
F32 = jnp.float32
BF16 = jnp.bfloat16

NX, NY, NZ = 4, 4, 8
ROWS, WIDTH = 256, 1152
HALF, QUARTER, EIGHTH = 128, 64, 32
PAIRS = 16384


def unit_rows(values):
    values = values.astype(F32)
    inverse = lax.rsqrt(jnp.sum(values * values, axis=1, keepdims=True) + 1e-06)
    return inverse, values * inverse


def unit_back(unit, inverse, grad):
    return (grad - unit * jnp.sum(unit * grad, axis=1, keepdims=True)) * inverse


def contract(a, b, dims):
    return lax.dot_general(a, b, (dims, ((), ())), preferred_element_type=F32)


def kernel(
    pic_hbm, cap_hbm, sharp_ref, off_ref,
    img_out, txt_out, loss_out,
    pic, cap, ibuf, jbuf, cbuf, ctbuf, pacc, tacc, lacc,
    pb, xr1, x2, rb, qr,
    ts, tr, vs, vr,
    ls, lx, rl, lq,
    hop,
    in_sem, i_s, i_r, t_s, t_r, d_s, d_r, x1_s, x1_r, x2_s, x2_r, y_s, y_r,
    ly_s, ly_r, lx_s, lx_r, e_s, e_r, v_s, v_r, g_s, g_r,
):
    dp, split = lax.axis_index("dp"), lax.axis_index("split")
    x = lax.rem(dp, NX)
    yl = lax.rem(dp // NX, 2)
    z = dp // (2 * NX)
    yh, core = split // 2, lax.rem(split, 2)
    y = 2 * yh + yl
    other = 1 - core
    first = core == 0
    second = core == 1

    def at(px, py, pz, pc):
        px, py, pz = lax.rem(px, NX), lax.rem(py, NY), lax.rem(pz, NZ)
        return ((pz * 2 + lax.rem(py, 2)) * NX + px, (py // 2) * 2 + pc)

    sibling = at(x, y, z, other)
    x_up, x_down, x_far = (at(x + k, y, z, core) for k in (1, 3, 2))
    z_up, z_down = at(x, y, z + 1, core), at(x, y, z + 7, core)
    y_up1, y_down1 = at(x, y + 1, z, 1), at(x, y + 3, z, 1)

    own_text = pl.multiple_of(yh * HALF, HALF)
    fetch_text = pltpu.make_async_copy(cap_hbm.at[pl.ds(own_text, HALF)], cap, in_sem.at[0])
    fetch_image = pltpu.make_async_copy(pic_hbm, pic, in_sem.at[1])
    fetch_text.start()
    fetch_image.start()

    barrier = pltpu.get_barrier_semaphore()
    partners = [sibling, x_up, x_down, x_far, z_up, z_down]
    partners += [at(x, y + k, z, c) for k in (1, 2, 3) for c in (0, 1)]
    for partner in partners:
        pl.semaphore_signal(barrier, inc=1, device_id=partner, device_id_type=MESH)

    pending = []

    def copy(src, dst, send, recv, to):
        return pltpu.make_async_remote_copy(
            src_ref=src, dst_ref=dst, send_sem=send, recv_sem=recv, device_id=to, device_id_type=MESH
        )

    def send(src, dst, ssem, rsem, to):
        one = copy(src, dst, ssem, rsem, to)
        one.start()
        pending.append((None, one))

    def send_when(cond, *copies):
        made = [copy(*c) for c in copies]

        @pl.when(cond)
        def _():
            for one in made:
                one.start()

        pending.extend((cond, one) for one in made)

    def drain():
        for cond in (None, first, second):
            some = [one for c, one in pending if c is cond]
            if cond is None:
                for one in some:
                    one.wait_send()
            elif some:

                @pl.when(cond)
                def _():
                    for one in some:
                        one.wait_send()

        pending[:] = [(c, one) for c, one in pending if not any(c is k for k in (None, first, second))]

    def landed(dst, rsem):
        copy(dst, dst, e_s.at[0], rsem, sibling).wait_recv()


    fetch_text.wait()
    jbuf[0:HALF, :] = unit_rows(cap[...])[1].astype(BF16)
    fetch_image.wait()

    @pl.when(first)
    def _():
        ibuf[0:ROWS, :] = unit_rows(pic[...])[1].astype(BF16)

    pl.semaphore_wait(barrier, len(partners))

    def irows(slot, half):
        return ibuf.at[pl.ds(slot * ROWS + half * HALF, HALF)]

    def jrows(slot, c, start=0, count=QUARTER):
        return jbuf.at[pl.ds(pl.multiple_of(slot * HALF + c * QUARTER + start, EIGHTH), count)]

    send(jrows(0, core), jrows(2, core), t_s.at[0, 0], t_r.at[0, 0], z_up)
    send(jrows(0, core), jrows(1, core), t_s.at[1, 0], t_r.at[1, 0], z_down)

    def to_y(slot, half):
        target = y_down1 if half else y_up1
        return (irows(slot, half), irows(slot, half), i_s.at[6 + 2 * slot + half], i_r.at[slot, half], target)

    send_when(
        first,
        (irows(0, 0), irows(1, 0), i_s.at[0], i_r.at[1, 0], x_up),
        (irows(0, 1), irows(2, 1), i_s.at[1], i_r.at[2, 1], x_down),
        to_y(0, 0),
        to_y(0, 1),
        (irows(0, 1), irows(1, 1), i_s.at[2], i_r.at[1, 1], x_up),
        (irows(0, 0), irows(2, 0), i_s.at[3], i_r.at[2, 0], x_down),
    )

    lacc[...] = jnp.zeros_like(lacc)

    def swap(slot):
        send(jrows(slot, core), jrows(slot, core), d_s.at[slot], d_r.at[slot], sibling)

    def swapped(*slots):
        for slot in slots:
            landed(jrows(slot, other), d_r.at[slot])

    def text_hop(d):
        if d < 4:
            landed(jrows(2 * d, core), t_r.at[0, d - 1])
            landed(jrows(2 * d - 1, core), t_r.at[1, d - 1])
        else:
            landed(jrows(7, core, 0, EIGHTH), t_r.at[0, 3])
            landed(jrows(7, core, EIGHTH, EIGHTH), t_r.at[1, 3])
        if d < 3:
            send(jrows(2 * d, core), jrows(2 * d + 2, core), t_s.at[0, d], t_r.at[0, d], z_up)
            send(jrows(2 * d - 1, core), jrows(2 * d + 1, core), t_s.at[1, d], t_r.at[1, d], z_down)
        elif d == 3:
            send(jrows(6, core, 0, EIGHTH), jrows(7, core, 0, EIGHTH), t_s.at[0, 3], t_r.at[0, 3], z_up)
            send(
                jrows(5, core, EIGHTH, EIGHTH), jrows(7, core, EIGHTH, EIGHTH), t_s.at[1, 3], t_r.at[1, 3], z_down
            )
        if d < 4:
            swap(2 * d - 1)
            swap(2 * d)
        else:
            swap(7)

    sharp, off = sharp_ref[0], off_ref[0]
    log2_e = 1.4426950408889634
    sharp2, off2 = sharp * log2_e, off * log2_e

    def logits_block(i0, i1, j0, j1):
        ri, rj = slice(i0 * ROWS, i1 * ROWS), slice(j0 * ROWS, j1 * ROWS)
        logits = sharp2 * contract(ibuf[ri, :], jbuf[rj, :], ((1,), (1,))) + off2
        diagonal = i0 == 0 and j0 == 0
        if diagonal:
            row = lax.broadcasted_iota(jnp.int32, logits.shape, 0)
            col = lax.broadcasted_iota(jnp.int32, logits.shape, 1)
            same = jnp.logical_and(jnp.logical_and(row == col + yh * HALF, col < HALF), first)
            logits = jnp.where(same, -logits, logits)
        grown = jnp.exp2(logits)
        total = 1.0 + grown
        rough = pl.reciprocal(total, approx=True)
        inverse = rough * (2.0 - total * rough)
        coef = grown * inverse
        lost = (grown - (total - 1.0)) * inverse
        strips = [slice(n, n + HALF) for n in range(0, (j1 - j0) * ROWS, HALF)]
        loss = lacc[ri, :]
        for n in range(0, len(strips), 4):
            group = strips[n : n + 4]
            loss = loss + (jnp.log(math.prod(total[:, c] for c in group)) + sum(lost[:, c] for c in group))
        lacc[ri, :] = loss
        if diagonal:
            coef = jnp.where(same, -coef, coef)
        coef = coef.astype(BF16)
        cbuf[ri, rj] = coef
        ctbuf[rj, ri] = coef.T

    def product(out, left, right, m0, m1, k0, k1):
        rows, depth = slice(m0 * ROWS, m1 * ROWS), slice(k0 * ROWS, k1 * ROWS)
        result = contract(left[rows, depth], right[depth, :], ((1,), (0,)))
        out[rows, :] = result if k0 == 0 else out[rows, :] + result

    def image_product(i0, i1, j0, j1):
        product(pacc, cbuf, jbuf, i0, i1, j0, j1)

    def text_product(j0, j1, i0, i1):
        product(tacc, ctbuf, ibuf, j0, j1, i0, i1)

    @pl.when(first)
    def _():
        landed(irows(1, 0), i_r.at[1, 0])
        landed(irows(2, 1), i_r.at[2, 1])

    send_when(
        first,
        (irows(1, 0), irows(3, 0), i_s.at[4], i_r.at[3, 0], x_up),
        (irows(2, 1), irows(3, 1), i_s.at[5], i_r.at[3, 1], x_down),
        to_y(1, 0),
        to_y(2, 1),
    )
    text_hop(1)

    @pl.when(second)
    def _():
        landed(irows(0, 0), i_r.at[0, 0])
        landed(irows(0, 1), i_r.at[0, 1])

    swapped(1)
    logits_block(0, 1, 0, 1)

    @pl.when(first)
    def _():
        landed(irows(1, 1), i_r.at[1, 1])
        landed(irows(2, 0), i_r.at[2, 0])

    send_when(first, to_y(1, 1), to_y(2, 0))
    text_hop(2)
    swapped(2, 3)
    logits_block(0, 1, 1, 2)

    @pl.when(first)
    def _():
        landed(irows(3, 0), i_r.at[3, 0])
        landed(irows(3, 1), i_r.at[3, 1])

    send_when(first, to_y(3, 0), to_y(3, 1))
    text_hop(3)

    @pl.when(second)
    def _():
        for slot in (1, 2):
            for half in (0, 1):
                landed(irows(slot, half), i_r.at[slot, half])

    logits_block(1, 3, 0, 2)
    swapped(4, 5)
    logits_block(0, 3, 2, 3)
    image_product(0, 3, 0, 3)
    text_hop(4)
    text_product(0, 3, 0, 3)
    swapped(6, 7)
    logits_block(0, 3, 3, 4)
    image_product(1, 3, 3, 4)
    text_product(3, 4, 0, 3)

    @pl.when(second)
    def _():
        landed(irows(3, 0), i_r.at[3, 0])
        landed(irows(3, 1), i_r.at[3, 1])

    logits_block(3, 4, 0, 4)
    image_product(3, 4, 0, 4)

    up_hi = lax.rem(y + 1, NY) // 2
    turns = (
        other * 2 * (1 - yh) + core * (2 * up_hi + 1),
        other * (2 * yh + 1) + core * 2 * up_hi,
        other * (2 * (1 - yh) + 1) + core * 2 * (1 - up_hi),
        other * 2 * yh + core * (2 * (1 - up_hi) + 1),
    )

    def seat(k):
        return pl.ds(k * QUARTER, QUARTER)

    def part_rows(slot, k):
        return pl.ds(pl.multiple_of(slot * ROWS + turns[k] * QUARTER, QUARTER), QUARTER)

    def far_turn(k):
        pb[0, seat(k), :] = pacc[part_rows(3, k), :].astype(BF16)
        send(pb.at[0, seat(k)], xr1.at[seat(k)], x1_s.at[k], x1_r.at[k], x_up if k < 2 else x_down)

    def near_turn(slot, k):
        side = 0 if slot == 2 else 1
        rows = pacc[part_rows(slot, k), :]
        if (k < 2) == (slot == 2):
            landed(xr1.at[seat(k)], x1_r.at[k])
            rows = rows + xr1[seat(k), :].astype(F32)
        pb[1 + side, seat(k), :] = rows.astype(BF16)
        send(
            pb.at[1 + side, seat(k)],
            x2.at[side, seat(k)],
            x2_s.at[side, k],
            x2_r.at[side, k],
            x_down if side else x_up,
        )

    def text_over(low, count):
        for slot in range(low, low + count):
            mine = pl.ds(pl.multiple_of(slot * HALF + other * QUARTER, QUARTER), QUARTER)
            ts[slot] = tacc[mine, :].astype(BF16)
        slots = pl.ds(low, count)
        send(ts.at[slots], tr.at[slots], e_s.at[low], e_r.at[low], sibling)

    def text_came(low, count):
        landed(tr.at[pl.ds(low, count)], e_r.at[low])

    for k in (0, 2, 1, 3):
        far_turn(k)
    text_product(3, 4, 3, 4)
    text_over(6, 2)
    near_turn(2, 2)
    near_turn(1, 0)
    near_turn(2, 3)
    near_turn(1, 1)
    text_product(2, 3, 3, 4)
    text_over(4, 2)
    text_product(0, 2, 3, 4)
    text_over(0, 4)
    image_product(0, 1, 3, 4)

    ones = jnp.ones((8, HALF), F32)
    for i in range(4):
        ls[i] = lax.dot_general(
            ones,
            lacc[i * ROWS : (i + 1) * ROWS, :],
            (((1,), (1,)), ((), ())),
            precision=lax.Precision.HIGHEST,
            preferred_element_type=F32,
        )
    send(ls.at[2], lx.at[0], lx_s.at[0], lx_r.at[0], x_up)
    send(ls.at[1], lx.at[1], lx_s.at[1], lx_r.at[1], x_down)
    send(ls.at[3], lx.at[2], lx_s.at[2], lx_r.at[2], x_far)

    def text_sum(slot):
        mine = pl.ds(pl.multiple_of(slot * HALF + core * QUARTER, QUARTER), QUARTER)
        return tacc[mine, :] + tr[slot].astype(F32)

    def text_back(d):
        if d == 4:
            both = text_sum(7).astype(BF16)
            for side in (0, 1):
                vs[side, 3, 0:EIGHTH, :] = both[side * EIGHTH : (side + 1) * EIGHTH]
                part = pl.ds(0, EIGHTH)
                send(
                    vs.at[side, 3, part],
                    vr.at[side, 3, part],
                    v_s.at[side, 3],
                    v_r.at[side, 3],
                    z_down if side else z_up,
                )
            return
        for side in (0, 1):
            rows = text_sum(2 * d if side else 2 * d - 1)
            if d == 3:
                part = pl.ds(0, EIGHTH)
                landed(vr.at[side, 3, part], v_r.at[side, 3])
                came = vr[side, 3, 0:EIGHTH, :].astype(F32)
                if side:
                    vs[side, 2, 0:EIGHTH, :] = rows[:EIGHTH].astype(BF16)
                    vs[side, 2, EIGHTH:QUARTER, :] = (rows[EIGHTH:] + came).astype(BF16)
                else:
                    vs[side, 2, 0:EIGHTH, :] = (rows[:EIGHTH] + came).astype(BF16)
                    vs[side, 2, EIGHTH:QUARTER, :] = rows[EIGHTH:].astype(BF16)
            else:
                landed(vr.at[side, d], v_r.at[side, d])
                vs[side, d - 1] = (rows + vr[side, d].astype(F32)).astype(BF16)
            send(
                vs.at[side, d - 1],
                vr.at[side, d - 1],
                v_s.at[side, d - 1],
                v_r.at[side, d - 1],
                z_down if side else z_up,
            )

    text_came(6, 2)
    text_back(4)
    near_turn(2, 0)
    near_turn(1, 2)
    text_came(4, 2)
    text_back(3)
    near_turn(2, 1)
    near_turn(1, 3)
    text_came(0, 4)
    text_back(2)

    source = yh + 2 * core
    block_yl = lax.rem(yl + core, 2)

    def owner_of(q):
        to = at(x, 2 * (q // 2) + block_yl, z, q % 2)
        return to, jnp.logical_and(dp == to[0], split == to[1])

    for k in range(3):
        landed(lx.at[k], lx_r.at[k])
    rl[...] = ls[0] + lx[0] + lx[1] + lx[2]
    for q in range(4):
        to, own = owner_of(q)
        send_when(jnp.logical_not(own), (rl, lq.at[source], ly_s.at[q], ly_r.at[source], to))

        @pl.when(own)
        def _():
            lq[source] = rl[...]

    text_back(1)
    drain()

    y_up0, y_down0 = at(x, y + 1, z, 0), at(x, y + 3, z, 0)

    def image_sum(k):
        landed(x2.at[0, seat(k)], x2_r.at[0, k])
        landed(x2.at[1, seat(k)], x2_r.at[1, k])
        return pacc[part_rows(0, k), :] + (x2[0, seat(k), :].astype(F32) + x2[1, seat(k), :].astype(F32))

    def image_out(k):
        total = image_sum(k)
        rb[seat(k), :] = total.astype(BF16)
        if k == 0:
            box = other * 3 + core
            send(rb.at[seat(0)], qr.at[box], y_s.at[0], y_r.at[box], y_up1)
        elif k == 2:
            box = other * 4 + core * 2
            send(rb.at[seat(2)], qr.at[box], y_s.at[2], y_r.at[box], (y_down1[0], y_down0[1] + other))
        else:
            carried = 3 if k == 1 else 4
            box, to = (1, y_up0) if k == 1 else (2, y_down1)

            @pl.when(second)
            def _():
                landed(qr.at[carried], y_r.at[carried])
                rb[seat(k), :] = (total + qr[carried].astype(F32)).astype(BF16)

            send_when(second, (rb.at[seat(k)], qr.at[box], y_s.at[k], y_r.at[box], to))
            if k == 1:
                send_when(first, (rb.at[seat(1)], qr.at[0], y_s.at[1], y_r.at[0], sibling))
            else:

                @pl.when(first)
                def _():
                    qr[0] = rb[seat(3), :]

    image_out(0)
    image_out(2)

    mine = yh * 2 + core
    outs = (img_out, txt_out)

    def quarter_rows(q, start=0, count=QUARTER):
        return pl.ds(pl.multiple_of(q * QUARTER + start, EIGHTH), count)

    my_rows = quarter_rows(mine)
    y_up, y_down = at(x, y + 1, z, core), at(x, y + 3, z, core)

    def gather_out(kind, grad, values):
        inverse, unit = unit_rows(values)
        out = outs[kind]
        out[my_rows, :] = unit_back(unit, inverse, sharp * grad).astype(BF16)
        low, high = out.at[quarter_rows(mine, 0, EIGHTH)], out.at[quarter_rows(mine, EIGHTH, EIGHTH)]
        send(low, hop.at[kind, 0], g_s.at[kind, 0], g_r.at[kind, 0], y_up)
        send(high, hop.at[kind, 1], g_s.at[kind, 1], g_r.at[kind, 1], y_down)
        send(out.at[my_rows], out.at[my_rows], g_s.at[kind, 2], g_r.at[kind, 2], sibling)

    def gather_on(kind):
        out = outs[kind]
        landed(hop.at[kind, 0], g_r.at[kind, 0])
        there = out.at[quarter_rows(2 * (1 - up_hi) + core, 0, EIGHTH)]
        send(hop.at[kind, 0], there, g_s.at[kind, 3], g_r.at[kind, 3], y_up)
        landed(hop.at[kind, 1], g_r.at[kind, 1])
        there = out.at[quarter_rows(2 * up_hi + core, EIGHTH, EIGHTH)]
        send(hop.at[kind, 1], there, g_s.at[kind, 4], g_r.at[kind, 4], y_down)

    def gather_over(kind):
        for half in (0, 1):
            here = outs[kind].at[quarter_rows((1 - yh) * 2 + core, half * EIGHTH, EIGHTH)]
            landed(here, g_r.at[kind, 3 + half])
            send(here, here, g_s.at[kind, 5 + half], g_r.at[kind, 5 + half], sibling)

    def gather_end(kind):
        landed(outs[kind].at[quarter_rows(yh * 2 + other)], g_r.at[kind, 2])
        for half in (0, 1):
            here = outs[kind].at[quarter_rows((1 - yh) * 2 + other, half * EIGHTH, EIGHTH)]
            landed(here, g_r.at[kind, 5 + half])

    grad = text_sum(0)
    for side in (0, 1):
        landed(vr.at[side, 0], v_r.at[side, 0])
        grad = grad + vr[side, 0].astype(F32)
    gather_out(1, grad, cap[pl.ds(pl.multiple_of(core * QUARTER, QUARTER), QUARTER), :])

    image_out(1)
    image_out(3)
    gather_on(1)

    for k in range(4):
        here = jnp.logical_and(first, yh == k)

        @pl.when(jnp.logical_not(here))
        def _():
            landed(lq.at[k], ly_r.at[k])

    loss_out[...] = ((lq[0] + lq[1]) + (lq[2] + lq[3])) * (1.0 / PAIRS)

    @pl.when(second)
    def _():
        landed(qr.at[0], y_r.at[0])

    landed(qr.at[1], y_r.at[1])
    landed(qr.at[2], y_r.at[2])
    grad = qr[0].astype(F32) + (qr[1].astype(F32) + qr[2].astype(F32))
    gather_out(0, grad, pic[my_rows, :])
    gather_over(1)
    drain()
    gather_on(0)
    gather_over(0)
    gather_end(1)
    gather_end(0)

    for cond, one in pending:
        if cond is None:
            one.wait_send()
        else:

            @pl.when(cond)
            def _():
                one.wait_send()


def per_device(picture_vectors, caption_vectors, sharpness_entry, offset_shift):
    dma = pltpu.SemaphoreType.DMA
    vmem = pl.BlockSpec(memory_space=pltpu.VMEM)
    smem = pl.BlockSpec(memory_space=pltpu.SMEM)
    hbm = pl.BlockSpec(memory_space=pltpu.HBM)
    img, txt, loss = pl.pallas_call(
        kernel,
        out_shape=(
            jax.ShapeDtypeStruct((ROWS, WIDTH), BF16),
            jax.ShapeDtypeStruct((ROWS, WIDTH), BF16),
            jax.ShapeDtypeStruct((8, ROWS), F32),
        ),
        in_specs=[hbm, hbm, smem, smem],
        out_specs=(vmem, vmem, vmem),
        scratch_shapes=[
            pltpu.VMEM((ROWS, WIDTH), BF16),
            pltpu.VMEM((HALF, WIDTH), BF16),
            pltpu.VMEM((4 * ROWS, WIDTH), BF16),
            pltpu.VMEM((8 * HALF, WIDTH), BF16),
            pltpu.VMEM((4 * ROWS, 8 * HALF), BF16),
            pltpu.VMEM((8 * HALF, 4 * ROWS), BF16),
            pltpu.VMEM((4 * ROWS, WIDTH), F32),
            pltpu.VMEM((8 * HALF, WIDTH), F32),
            pltpu.VMEM((4 * ROWS, HALF), F32),
            pltpu.VMEM((3, ROWS, WIDTH), BF16),
            pltpu.VMEM((ROWS, WIDTH), BF16),
            pltpu.VMEM((2, ROWS, WIDTH), BF16),
            pltpu.VMEM((ROWS, WIDTH), BF16),
            pltpu.VMEM((5, QUARTER, WIDTH), BF16),
            pltpu.VMEM((8, QUARTER, WIDTH), BF16),
            pltpu.VMEM((8, QUARTER, WIDTH), BF16),
            pltpu.VMEM((2, 4, QUARTER, WIDTH), BF16),
            pltpu.VMEM((2, 4, QUARTER, WIDTH), BF16),
            pltpu.VMEM((4, 8, ROWS), F32),
            pltpu.VMEM((3, 8, ROWS), F32),
            pltpu.VMEM((8, ROWS), F32),
            pltpu.VMEM((4, 8, ROWS), F32),
            pltpu.VMEM((2, 2, EIGHTH, WIDTH), BF16),
            dma((2,)),
            dma((14,)), dma((4, 2)),
            dma((2, 4)), dma((2, 4)),
            dma((8,)), dma((8,)),
            dma((4,)), dma((4,)),
            dma((2, 4)), dma((2, 4)),
            dma((4,)), dma((5,)),
            dma((4,)), dma((4,)),
            dma((3,)), dma((3,)),
            dma((8,)), dma((8,)),
            dma((2, 4)), dma((2, 4)),
            dma((2, 7)), dma((2, 7)),
        ],
        compiler_params=pltpu.CompilerParams(
            collective_id=0, has_side_effects=True, vmem_limit_bytes=48 * 1024 * 1024
        ),
        cost_estimate=pl.CostEstimate(flops=7_300_000_000, bytes_accessed=4_000_000, transcendentals=3_000_000),
    )(
        pltpu.with_memory_space_constraint(picture_vectors, pltpu.HBM),
        pltpu.with_memory_space_constraint(caption_vectors, pltpu.HBM),
        sharpness_entry,
        offset_shift,
    )
    return img.astype(F32), txt.astype(F32), loss[0]


def solution(mesh):
    placed = (P("dp", None), P("dp", None), P(), P())
    return jax.shard_map(
        per_device,
        mesh=mesh,
        in_specs=placed,
        out_specs=(P("dp", None), P("dp", None), P("dp")),
        check_vma=False,
    )
```

```python
import jax
import jax.numpy as jnp
from jax import lax
from jax.experimental import pallas as pl
from jax.experimental.pallas import tpu as pltpu
from jax.sharding import PartitionSpec as P

MESH = pl.DeviceIdType.MESH
F32 = jnp.float32
BF16 = jnp.bfloat16

NX, NY, NZ = 4, 4, 8
ROWS, WIDTH = 256, 1152
HALF, QUARTER, EIGHTH = 128, 64, 32
PAIRS = 16384


def unit_rows(values):
    values = values.astype(F32)
    inverse = lax.rsqrt(jnp.sum(values * values, axis=1, keepdims=True) + 1e-06)
    return inverse, values * inverse


def unit_back(unit, inverse, grad):
    return (grad - unit * jnp.sum(unit * grad, axis=1, keepdims=True)) * inverse


def contract(a, b, dims):
    return lax.dot_general(a, b, (dims, ((), ())), preferred_element_type=F32)


def kernel(
    pic_hbm, cap_hbm, sharp_ref, off_ref,
    both_out, loss_out,
    pic, cap, ibuf, jbuf, cbuf, ctbuf, pacc, tacc, lacc,
    pb, xr1, x2, rb, qr, ys, yr,
    ts, tr, vs, vr,
    ls, lx, rl, lq,
    hop,
    in_sem, i_s, i_r, t_s, t_r, d_s, d_r, x1_s, x1_r, x2_s, x2_r, y_s, y_r, yc_s, yc_r,
    ly_s, ly_r, lx_s, lx_r, e_s, e_r, v_s, v_r, g_s, g_r,
):
    dp, split = lax.axis_index("dp"), lax.axis_index("split")
    x = lax.rem(dp, NX)
    yl = lax.rem(dp // NX, 2)
    z = dp // (2 * NX)
    yh, core = split // 2, lax.rem(split, 2)
    y = 2 * yh + yl
    other = 1 - core
    first = core == 0
    second = core == 1

    def at(px, py, pz, pc):
        px, py, pz = lax.rem(px, NX), lax.rem(py, NY), lax.rem(pz, NZ)
        return ((pz * 2 + lax.rem(py, 2)) * NX + px, (py // 2) * 2 + pc)

    sibling = at(x, y, z, other)
    x_up, x_down, x_far = (at(x + k, y, z, core) for k in (1, 3, 2))
    z_up, z_down = at(x, y, z + 1, core), at(x, y, z + 7, core)
    y_up1, y_down1 = at(x, y + 1, z, 1), at(x, y + 3, z, 1)

    own_text = pl.multiple_of(yh * HALF, HALF)
    fetch_text = pltpu.make_async_copy(cap_hbm.at[pl.ds(own_text, HALF)], cap, in_sem.at[0])
    fetch_image = pltpu.make_async_copy(pic_hbm, pic, in_sem.at[1])
    fetch_text.start()
    fetch_image.start()

    barrier = pltpu.get_barrier_semaphore()
    partners = [sibling, x_up, x_down, x_far, z_up, z_down]
    partners += [at(x, y + k, z, c) for k in (1, 2, 3) for c in (0, 1)]
    for partner in partners:
        pl.semaphore_signal(barrier, inc=1, device_id=partner, device_id_type=MESH)

    pending = []

    def copy(src, dst, send, recv, to):
        return pltpu.make_async_remote_copy(
            src_ref=src, dst_ref=dst, send_sem=send[0].at[send[1:]], recv_sem=recv, device_id=to, device_id_type=MESH
        )

    def note(cond, src, ssem):
        rows = 0 if src.dtype == F32 else src.shape[0] * (src.shape[1] if len(src.shape) == 3 else 1)
        pending.append((cond, rows, ssem))

    def sent(rows, ssem):
        ref = ibuf.at[pl.ds(0, rows)] if rows else ls.at[0]
        copy(ref, ref, ssem, e_r.at[0], sibling).wait_send()

    branch = [None]

    def on(cond):
        def run(body):
            branch[0] = cond
            pl.when(cond)(body)
            branch[0] = None

        return run

    def send(src, dst, ssem, rsem, to):
        copy(src, dst, ssem, rsem, to).start()
        note(branch[0], src, ssem)

    def send_when(cond, *copies):
        @pl.when(cond)
        def _():
            for one in copies:
                copy(*one).start()

        for one in copies:
            note(cond, one[0], one[2])

    def drain(of=None):
        later = [entry for entry in pending if of is not None and not any(entry[2][0] is sem for sem in of)]
        pending[:] = [entry for entry in pending if not any(entry is k for k in later)]
        for cond in (None, first, second):
            some = [entry[1:] for entry in pending if entry[0] is cond]
            if cond is None:
                for entry in some:
                    sent(*entry)
            elif some:

                @pl.when(cond)
                def _():
                    for entry in some:
                        sent(*entry)

        pending[:] = later + [entry for entry in pending if not any(entry[0] is k for k in (None, first, second))]

    def landed(dst, rsem):
        copy(dst, dst, (e_s, 0), rsem, sibling).wait_recv()


    fetch_text.wait()
    jbuf[0:HALF, :] = unit_rows(cap[...])[1].astype(BF16)
    fetch_image.wait()

    @pl.when(first)
    def _():
        ibuf[0:ROWS, :] = unit_rows(pic[...])[1].astype(BF16)

    pl.semaphore_wait(barrier, len(partners))

    def irows(slot, piece):
        return ibuf.at[pl.ds(slot * ROWS + piece * QUARTER, QUARTER)]

    def jrows(slot, c, start=0, count=QUARTER):
        return jbuf.at[pl.ds(pl.multiple_of(slot * HALF + c * QUARTER + start, EIGHTH), count)]

    def text_piece(slot, piece):
        return jrows(slot, core, piece * EIGHTH, EIGHTH)

    def text_send(side, d, piece, source, target):
        send(
            text_piece(source, piece),
            text_piece(target, piece),
            (t_s, side, d, piece),
            t_r.at[side, d, piece],
            z_down if side else z_up,
        )

    for piece in (0, 1):
        text_send(0, 0, piece, 0, 2)
        text_send(1, 0, piece, 0, 1)

    def to_y(slot, piece):
        target = y_up1 if piece < 2 else y_down1
        return (irows(slot, piece), irows(slot, piece), (i_s, 2 + slot, piece), i_r.at[slot, piece], target)

    def to_x(source, slot, piece, kind):
        target = x_up if slot == 1 or (slot == 3 and piece < 2) else x_down
        return (irows(source, piece), irows(slot, piece), (i_s, kind, piece), i_r.at[slot, piece], target)

    send_when(
        first,
        to_x(0, 1, 0, 0), to_x(0, 2, 2, 1), to_y(0, 0), to_y(0, 2),
        to_x(0, 1, 1, 0), to_x(0, 2, 3, 1), to_y(0, 1), to_y(0, 3),
        to_x(0, 1, 2, 0), to_x(0, 2, 0, 1), to_x(0, 1, 3, 0), to_x(0, 2, 1, 1),
    )

    def pass_near(up, down, onward):
        landed(irows(1, up), i_r.at[1, up])
        if onward:
            send(*to_x(1, 3, up, 6))
        send(*to_y(1, up))
        landed(irows(2, down), i_r.at[2, down])
        if onward:
            send(*to_x(2, 3, down, 6))
        send(*to_y(2, down))

    def pass_far(*pieces):
        for piece in pieces:
            landed(irows(3, piece), i_r.at[3, piece])
            send(*to_y(3, piece))

    def images_in(*slots):
        for slot in slots:
            for piece in range(4):
                landed(irows(slot, piece), i_r.at[slot, piece])

    for zeroed in (lacc,):

        def clear(n, carry):
            rows = pl.ds(pl.multiple_of(n * QUARTER, QUARTER), QUARTER)
            zeroed[rows, :] = jnp.zeros((QUARTER, zeroed.shape[1]), F32)
            return carry

        lax.fori_loop(0, 16, clear, 0)

    def swap(slot):
        send(jrows(slot, core), jrows(slot, core), (d_s, slot), d_r.at[slot], sibling)

    def swapped(*slots):
        for slot in slots:
            landed(jrows(slot, other), d_r.at[slot])

    def text_hop(d, pieces=(0, 1)):
        for piece in pieces:
            for side in (0, 1):
                if d == 4:
                    if piece == side:
                        landed(text_piece(7, piece), t_r.at[side, 3, piece])
                    continue
                here = 2 * d - side
                landed(text_piece(here, piece), t_r.at[side, d - 1, piece])
                if d < 3:
                    text_send(side, d, piece, here, here + 2)
                elif piece == side:
                    text_send(side, 3, piece, here, 7)
        if pieces[-1] == 0:
            return
        if d < 4:
            swap(2 * d - 1)
            swap(2 * d)
        else:
            swap(7)

    sharp, off = sharp_ref[0], off_ref[0]
    log2_e = 1.4426950408889634
    sharp2, off2 = sharp * log2_e, off * log2_e

    def logits_block(i, j, diagonal=False):
        ri, rj = slice(i * ROWS, (i + 1) * ROWS), slice(j * ROWS, (j + 1) * ROWS)
        logits = sharp2 * contract(ibuf[ri, :], jbuf[rj, :], ((1,), (1,))) + off2
        if diagonal:
            row = lax.broadcasted_iota(jnp.int32, (ROWS, ROWS), 0)
            col = lax.broadcasted_iota(jnp.int32, (ROWS, ROWS), 1)
            same = jnp.logical_and(row == col + yh * HALF, col < HALF)
            logits = jnp.where(same, -logits, logits)
        grown = jnp.exp2(logits)
        total = 1.0 + grown
        rough = pl.reciprocal(total, approx=True)
        inverse = rough * (2.0 - total * rough)
        coef = grown * inverse
        lost = (grown - (total - 1.0)) * inverse
        lacc[ri, :] += jnp.log(total[:, :HALF] * total[:, HALF:]) + (lost[:, :HALF] + lost[:, HALF:])
        if diagonal:
            coef = jnp.where(same, -coef, coef)
        coef = coef.astype(BF16)
        cbuf[ri, rj] = coef
        ctbuf[rj, ri] = coef.T

    def product(out, left, right, m, k0, k1):
        rows, depth = slice(m * ROWS, (m + 1) * ROWS), slice(k0 * ROWS, k1 * ROWS)
        a = left[rows, depth]
        for n in range(0, WIDTH, 256):
            columns = slice(n, min(n + 256, WIDTH))
            result = contract(a, right[depth, columns], ((1,), (0,)))
            out[rows, columns] = result if k0 == 0 else out[rows, columns] + result

    def image_product(i, j0, j1):
        product(pacc, cbuf, jbuf, i, j0, j1)

    def text_product(j, i0, i1):
        product(tacc, ctbuf, ibuf, j, i0, i1)

    up_hi = lax.rem(y + 1, NY) // 2
    turns = (
        other * 2 * (1 - yh) + core * 2 * up_hi,
        core * (2 * up_hi + 1),
        other * 2 * yh + core * 2 * (1 - up_hi),
        core * (2 * (1 - up_hi) + 1),
    )

    def hand_over(slot):
        for side, q, to in ((0, 2 * yh + 1, y_up1), (1, 2 * (1 - yh) + 1, y_down1)):
            rows = pl.ds(pl.multiple_of(slot * ROWS + q * QUARTER, QUARTER), QUARTER)
            ys[side, slot] = pacc[rows, :].astype(BF16)
            send(ys.at[side, slot], yr.at[side, slot], (yc_s, side, slot), yc_r.at[side, slot], to)

    def handed(slot):
        rows = part_rows(slot, 3)
        for side in (0, 1):
            landed(yr.at[side, slot], yc_r.at[side, slot])
        pacc[rows, :] += yr[0, slot].astype(F32) + yr[1, slot].astype(F32)

    def seat(k):
        return pl.ds(k * QUARTER, QUARTER)

    def part_rows(slot, k):
        return pl.ds(pl.multiple_of(slot * ROWS + turns[k] * QUARTER, QUARTER), QUARTER)

    def far_turn(k):
        pb[0, seat(k), :] = pacc[part_rows(3, k), :].astype(BF16)
        send(pb.at[0, seat(k)], xr1.at[seat(k)], (x1_s, k), x1_r.at[k], x_up if k < 2 else x_down)

    def near_turn(slot, k):
        side = 0 if slot == 2 else 1
        rows = pacc[part_rows(slot, k), :]
        if (k < 2) == (slot == 2):
            landed(xr1.at[seat(k)], x1_r.at[k])
            rows = rows + xr1[seat(k), :].astype(F32)
        pb[1 + side, seat(k), :] = rows.astype(BF16)
        send(
            pb.at[1 + side, seat(k)],
            x2.at[side, seat(k)],
            (x2_s, side, k),
            x2_r.at[side, k],
            x_down if side else x_up,
        )

    def text_over(low, count):
        for slot in range(low, low + count):
            mine = pl.ds(pl.multiple_of(slot * HALF + other * QUARTER, QUARTER), QUARTER)
            ts[slot] = tacc[mine, :].astype(BF16)
        slots = pl.ds(low, count)
        send(ts.at[slots], tr.at[slots], (e_s, low), e_r.at[low], sibling)

    def text_came(low, count):
        landed(tr.at[pl.ds(low, count)], e_r.at[low])

    @on(first)
    def _():
        text_hop(1, (0,))
        pass_near(0, 2, True)
        text_hop(1, (1,))
        pass_near(1, 3, True)
        swapped(1)
        logits_block(0, 0, True)
        pass_near(2, 0, False)
        text_hop(2, (0,))
        text_hop(2, (1,))
        pass_near(3, 1, False)
        swapped(2, 3)
        logits_block(0, 1)
        pass_far(0, 2)
        logits_block(1, 0)
        logits_block(2, 0)
        image_product(0, 0, 2)
        text_hop(3)
        pass_far(1, 3)
        logits_block(1, 1)
        logits_block(2, 1)
        image_product(1, 0, 2)
        logits_block(3, 0)
        image_product(2, 0, 2)
        logits_block(3, 1)
        swapped(4, 5)
        text_hop(4)
        text_product(0, 0, 4)
        logits_block(0, 2)
        text_product(1, 0, 4)
        logits_block(1, 2)
        image_product(3, 0, 2)
        logits_block(2, 2)
        logits_block(3, 2)
        swapped(6, 7)
        logits_block(3, 3)
        text_product(2, 0, 4)
        logits_block(1, 3)
        image_product(3, 2, 4)
        logits_block(2, 3)
        image_product(1, 2, 4)
        logits_block(0, 3)
        text_product(3, 0, 4)
        text_over(6, 2)
        text_over(4, 2)
        text_over(0, 4)
        far_turn(0)
        far_turn(2)
        hand_over(3)
        near_turn(1, 0)
        hand_over(1)
        image_product(2, 2, 4)
        near_turn(2, 2)
        hand_over(2)
        image_product(0, 2, 4)
        hand_over(0)

    @on(second)
    def _():
        text_hop(1)
        images_in(0)
        swapped(1)
        logits_block(0, 0)
        text_hop(2)
        swapped(2, 3)
        logits_block(0, 1)
        text_hop(3)
        swapped(4, 5)
        logits_block(0, 2)
        image_product(0, 0, 3)
        text_hop(4)
        images_in(1, 2)
        logits_block(1, 0)
        logits_block(2, 0)
        logits_block(1, 1)
        text_product(0, 0, 3)
        logits_block(2, 1)
        logits_block(1, 2)
        text_product(1, 0, 3)
        logits_block(2, 2)
        swapped(6, 7)
        logits_block(1, 3)
        text_product(2, 0, 3)
        logits_block(2, 3)
        image_product(1, 0, 4)
        logits_block(0, 3)
        image_product(2, 0, 4)
        text_product(3, 0, 3)
        near_turn(1, 0)
        near_turn(2, 2)
        near_turn(1, 1)
        images_in(3)
        logits_block(3, 3)
        logits_block(3, 2)
        text_product(3, 3, 4)
        logits_block(3, 0)
        logits_block(3, 1)
        text_over(6, 2)
        text_product(2, 3, 4)
        text_over(4, 2)
        text_product(1, 3, 4)
        text_product(0, 3, 4)
        text_over(0, 4)
        image_product(3, 0, 4)
        far_turn(0)
        far_turn(2)
        far_turn(1)
        handed(3)
        far_turn(3)
        handed(2)
        near_turn(2, 3)
        image_product(0, 3, 4)

    ones = jnp.ones((8, HALF), F32)
    for i in range(4):
        ls[i] = lax.dot_general(
            ones,
            lacc[i * ROWS : (i + 1) * ROWS, :],
            (((1,), (1,)), ((), ())),
            precision=lax.Precision.HIGHEST,
            preferred_element_type=F32,
        )
    send(ls.at[2], lx.at[0], (lx_s, 0), lx_r.at[0], x_up)
    send(ls.at[1], lx.at[1], (lx_s, 1), lx_r.at[1], x_down)
    send(ls.at[3], lx.at[2], (lx_s, 2), lx_r.at[2], x_far)

    def piece_rows(piece):
        return pl.ds(piece * EIGHTH, EIGHTH)

    def text_sum(slot, piece):
        start = slot * HALF + core * QUARTER + piece * EIGHTH
        return tacc[pl.ds(pl.multiple_of(start, EIGHTH), EIGHTH), :] + tr[slot, piece_rows(piece), :].astype(F32)

    def text_back(d, steps=(0, 1)):
        for step in steps:
            for side in (0, 1):
                piece = step if side else 1 - step
                if d == 4 and piece != side:
                    continue
                rows = text_sum(7 if d == 4 else 2 * d - 1 + side, piece)
                part = piece_rows(piece)
                if d < 3 or (d == 3 and piece == side):
                    landed(vr.at[side, d, part], v_r.at[side, d, piece])
                    rows = rows + vr[side, d, part, :].astype(F32)
                vs[side, d - 1, part, :] = rows.astype(BF16)
                send(
                    vs.at[side, d - 1, part],
                    vr.at[side, d - 1, part],
                    (v_s, side, d - 1, piece),
                    v_r.at[side, d - 1, piece],
                    z_down if side else z_up,
                )

    text_came(6, 2)
    text_back(4)
    text_came(4, 2)
    text_back(3, (0,))
    near_turn(2, 0)
    near_turn(1, 2)
    text_back(3, (1,))
    text_came(0, 4)
    text_back(2, (0,))

    @on(second)
    def _():
        near_turn(2, 1)
        handed(1)
        near_turn(1, 3)

    text_back(2, (1,))
    text_back(1, (0,))

    source = yh + 2 * core
    block_yl = lax.rem(yl + core, 2)

    def owner_of(q):
        to = at(x, 2 * (q // 2) + block_yl, z, q % 2)
        return to, jnp.logical_and(dp == to[0], split == to[1])

    for k in range(3):
        landed(lx.at[k], lx_r.at[k])
    rl[...] = ls[0] + lx[0] + lx[1] + lx[2]
    for q in range(4):
        to, own = owner_of(q)
        send_when(jnp.logical_not(own), (rl, lq.at[source], (ly_s, q), ly_r.at[source], to))

        @pl.when(own)
        def _():
            lq[source] = rl[...]

    text_back(1, (1,))
    drain((i_s, t_s, d_s))

    y_up0, y_down0 = at(x, y + 1, z, 0), at(x, y + 3, z, 0)

    def image_sum(k):
        landed(x2.at[0, seat(k)], x2_r.at[0, k])
        landed(x2.at[1, seat(k)], x2_r.at[1, k])
        return pacc[part_rows(0, k), :] + (x2[0, seat(k), :].astype(F32) + x2[1, seat(k), :].astype(F32))

    def image_out(k, box, to):
        total = image_sum(k)
        if core_of[0] == 1 and k == 0:
            landed(qr.at[3], y_r.at[3])
            total = total + qr[3].astype(F32)
        rb[seat(k), :] = total.astype(BF16)
        send(rb.at[seat(k)], qr.at[box], (y_s, k), y_r.at[box], to)

    core_of = [0]

    @on(first)
    def _():
        image_out(0, 3, y_up1)
        qr[0] = image_sum(2).astype(BF16)

    core_of[0] = 1

    @on(second)
    def _():
        qr[0] = jnp.zeros((QUARTER, WIDTH), BF16)
        image_out(2, 2, y_down0)
        image_out(0, 1, y_up0)

    mine = yh * 2 + core
    outs = (both_out.at[pl.ds(0, ROWS)], both_out.at[pl.ds(ROWS, ROWS)])

    def quarter_rows(q, start=0, count=QUARTER):
        return pl.ds(pl.multiple_of(q * QUARTER + start, EIGHTH), count)

    my_rows = quarter_rows(mine)
    y_up, y_down = at(x, y + 1, z, core), at(x, y + 3, z, core)

    def gather_out(kind, grad, values):
        inverse, unit = unit_rows(values)
        out = outs[kind]
        out[my_rows, :] = unit_back(unit, inverse, sharp * grad).astype(BF16)
        low, high = out.at[quarter_rows(mine, 0, EIGHTH)], out.at[quarter_rows(mine, EIGHTH, EIGHTH)]
        send(low, hop.at[kind, 0], (g_s, kind, 0), g_r.at[kind, 0], y_up)
        send(high, hop.at[kind, 1], (g_s, kind, 1), g_r.at[kind, 1], y_down)
        send(out.at[my_rows], out.at[my_rows], (g_s, kind, 2), g_r.at[kind, 2], sibling)

    def gather_on(kind):
        out = outs[kind]
        landed(hop.at[kind, 0], g_r.at[kind, 0])
        there = out.at[quarter_rows(2 * (1 - up_hi) + core, 0, EIGHTH)]
        send(hop.at[kind, 0], there, (g_s, kind, 3), g_r.at[kind, 3], y_up)
        landed(hop.at[kind, 1], g_r.at[kind, 1])
        there = out.at[quarter_rows(2 * up_hi + core, EIGHTH, EIGHTH)]
        send(hop.at[kind, 1], there, (g_s, kind, 4), g_r.at[kind, 4], y_down)

    def gather_over(kind):
        for half in (0, 1):
            here = outs[kind].at[quarter_rows((1 - yh) * 2 + core, half * EIGHTH, EIGHTH)]
            landed(here, g_r.at[kind, 3 + half])
            send(here, here, (g_s, kind, 5 + half), g_r.at[kind, 5 + half], sibling)

    def gather_end(kind):
        landed(outs[kind].at[quarter_rows(yh * 2 + other)], g_r.at[kind, 2])
        for half in (0, 1):
            here = outs[kind].at[quarter_rows((1 - yh) * 2 + other, half * EIGHTH, EIGHTH)]
            landed(here, g_r.at[kind, 5 + half])

    grads = []
    for piece in (0, 1):
        grad = text_sum(0, piece)
        for side in (0, 1):
            landed(vr.at[side, 0, piece_rows(piece)], v_r.at[side, 0, piece])
            grad = grad + vr[side, 0, piece_rows(piece), :].astype(F32)
        grads.append(grad)
    grad = jnp.concatenate(grads, axis=0)
    gather_out(1, grad, cap[pl.ds(pl.multiple_of(core * QUARTER, QUARTER), QUARTER), :])

    @on(second)
    def _():
        image_out(1, 1, y_up1)
        handed(0)
        image_out(3, 2, y_down1)

    gather_on(1)

    for k in range(4):
        here = jnp.logical_and(first, yh == k)

        @pl.when(jnp.logical_not(here))
        def _():
            landed(lq.at[k], ly_r.at[k])

    loss_out[...] = ((lq[0] + lq[1]) + (lq[2] + lq[3])) * (1.0 / PAIRS)

    landed(qr.at[1], y_r.at[1])
    landed(qr.at[2], y_r.at[2])
    grad = qr[0].astype(F32) + (qr[1].astype(F32) + qr[2].astype(F32))
    gather_out(0, grad, pic[my_rows, :])
    gather_over(1)
    drain()
    gather_on(0)
    gather_over(0)
    gather_end(1)
    gather_end(0)

    drain()
    for cond, rows, ssem in pending:

        @pl.when(cond)
        def _():
            sent(rows, ssem)


def per_device(picture_vectors, caption_vectors, sharpness_entry, offset_shift):
    dma = pltpu.SemaphoreType.DMA
    vmem = pl.BlockSpec(memory_space=pltpu.VMEM)
    smem = pl.BlockSpec(memory_space=pltpu.SMEM)
    hbm = pl.BlockSpec(memory_space=pltpu.HBM)
    both, loss = pl.pallas_call(
        kernel,
        out_shape=(
            jax.ShapeDtypeStruct((2 * ROWS, WIDTH), BF16),
            jax.ShapeDtypeStruct((8, ROWS), F32),
        ),
        in_specs=[hbm, hbm, smem, smem],
        out_specs=(vmem, vmem),
        scratch_shapes=[
            pltpu.VMEM((ROWS, WIDTH), BF16),
            pltpu.VMEM((HALF, WIDTH), BF16),
            pltpu.VMEM((4 * ROWS, WIDTH), BF16),
            pltpu.VMEM((8 * HALF, WIDTH), BF16),
            pltpu.VMEM((4 * ROWS, 8 * HALF), BF16),
            pltpu.VMEM((8 * HALF, 4 * ROWS), BF16),
            pltpu.VMEM((4 * ROWS, WIDTH), F32),
            pltpu.VMEM((8 * HALF, WIDTH), F32),
            pltpu.VMEM((4 * ROWS, HALF), F32),
            pltpu.VMEM((3, ROWS, WIDTH), BF16),
            pltpu.VMEM((ROWS, WIDTH), BF16),
            pltpu.VMEM((2, ROWS, WIDTH), BF16),
            pltpu.VMEM((ROWS, WIDTH), BF16),
            pltpu.VMEM((4, QUARTER, WIDTH), BF16),
            pltpu.VMEM((2, 4, QUARTER, WIDTH), BF16),
            pltpu.VMEM((2, 4, QUARTER, WIDTH), BF16),
            pltpu.VMEM((8, QUARTER, WIDTH), BF16),
            pltpu.VMEM((8, QUARTER, WIDTH), BF16),
            pltpu.VMEM((2, 4, QUARTER, WIDTH), BF16),
            pltpu.VMEM((2, 4, QUARTER, WIDTH), BF16),
            pltpu.VMEM((4, 8, ROWS), F32),
            pltpu.VMEM((3, 8, ROWS), F32),
            pltpu.VMEM((8, ROWS), F32),
            pltpu.VMEM((4, 8, ROWS), F32),
            pltpu.VMEM((2, 2, EIGHTH, WIDTH), BF16),
            dma((2,)),
            dma((7, 4)), dma((4, 4)),
            dma((2, 4, 2)), dma((2, 4, 2)),
            dma((8,)), dma((8,)),
            dma((4,)), dma((4,)),
            dma((2, 4)), dma((2, 4)),
            dma((4,)), dma((4,)),
            dma((2, 4)), dma((2, 4)),
            dma((4,)), dma((4,)),
            dma((3,)), dma((3,)),
            dma((8,)), dma((8,)),
            dma((2, 4, 2)), dma((2, 4, 2)),
            dma((2, 7)), dma((2, 7)),
        ],
        compiler_params=pltpu.CompilerParams(
            collective_id=0, has_side_effects=True, vmem_limit_bytes=48 * 1024 * 1024
        ),
        cost_estimate=pl.CostEstimate(flops=7_300_000_000, bytes_accessed=4_000_000, transcendentals=3_000_000),
    )(
        pltpu.with_memory_space_constraint(picture_vectors, pltpu.HBM),
        pltpu.with_memory_space_constraint(caption_vectors, pltpu.HBM),
        sharpness_entry,
        offset_shift,
    )
    return both[:ROWS].astype(F32), both[ROWS:].astype(F32), loss[0]


def solution(mesh):
    placed = (P("dp", None), P("dp", None), P(), P())
    return jax.shard_map(
        per_device,
        mesh=mesh,
        in_specs=placed,
        out_specs=(P("dp", None), P("dp", None), P("dp")),
        check_vma=False,
    )
```

```python
import jax
import jax.numpy as jnp
from jax import lax
from jax.experimental import pallas as pl
from jax.experimental.pallas import tpu as pltpu
from jax.sharding import PartitionSpec as P

MESH = pl.DeviceIdType.MESH
F32 = jnp.float32
BF16 = jnp.bfloat16

NX, NY, NZ = 4, 4, 8
ROWS, WIDTH = 256, 1152
HALF, QUARTER, EIGHTH = 128, 64, 32
PAIRS = 16384


def unit_rows(values):
    values = values.astype(F32)
    inverse = lax.rsqrt(jnp.sum(values * values, axis=1, keepdims=True) + 1e-06)
    return inverse, values * inverse


def unit_back(unit, inverse, grad):
    return (grad - unit * jnp.sum(unit * grad, axis=1, keepdims=True)) * inverse


def contract(a, b, dims):
    return lax.dot_general(a, b, (dims, ((), ())), preferred_element_type=F32)


def kernel(
    pic_hbm, cap_hbm, sharp_ref, off_ref,
    both_out, loss_out,
    pic, cap, ibuf, jbuf, cbuf, ctbuf, pacc, tacc, lacc,
    pb, xr1, x2, rb, qr, ys, yr,
    ts, tr, vs, vr,
    ls, lx, rl, lq,
    hop,
    in_sem, i_s, i_r, t_s, t_r, d_s, d_r, x1_s, x1_r, x2_s, x2_r, y_s, y_r, yc_s, yc_r,
    ly_s, ly_r, lx_s, lx_r, e_s, e_r, v_s, v_r, g_s, g_r,
):
    dp, split = lax.axis_index("dp"), lax.axis_index("split")
    x = lax.rem(dp, NX)
    yl = lax.rem(dp // NX, 2)
    z = dp // (2 * NX)
    yh, core = split // 2, lax.rem(split, 2)
    y = 2 * yh + yl
    other = 1 - core
    first = core == 0
    second = core == 1

    def at(px, py, pz, pc):
        px, py, pz = lax.rem(px, NX), lax.rem(py, NY), lax.rem(pz, NZ)
        return ((pz * 2 + lax.rem(py, 2)) * NX + px, (py // 2) * 2 + pc)

    sibling = at(x, y, z, other)
    x_up, x_down, x_far = (at(x + k, y, z, core) for k in (1, 3, 2))
    z_up, z_down = at(x, y, z + 1, core), at(x, y, z + 7, core)
    y_up1, y_down1 = at(x, y + 1, z, 1), at(x, y + 3, z, 1)

    own_text = pl.multiple_of(yh * HALF, HALF)
    fetch_text = pltpu.make_async_copy(cap_hbm.at[pl.ds(own_text, HALF)], cap, in_sem.at[0])
    fetch_image = pltpu.make_async_copy(pic_hbm, pic, in_sem.at[1])
    fetch_text.start()
    fetch_image.start()

    barrier = pltpu.get_barrier_semaphore()
    partners = [sibling, x_up, x_down, x_far, z_up, z_down]
    partners += [at(x, y + k, z, c) for k in (1, 2, 3) for c in (0, 1)]
    for partner in partners:
        pl.semaphore_signal(barrier, inc=1, device_id=partner, device_id_type=MESH)

    pending = []

    def copy(src, dst, send, recv, to):
        return pltpu.make_async_remote_copy(
            src_ref=src, dst_ref=dst, send_sem=send[0].at[send[1:]], recv_sem=recv, device_id=to, device_id_type=MESH
        )

    def note(cond, src, ssem):
        rows = 0 if src.dtype == F32 else src.shape[0] * (src.shape[1] if len(src.shape) == 3 else 1)
        pending.append((cond, rows, ssem))

    def sent(rows, ssem):
        ref = ibuf.at[pl.ds(0, rows)] if rows else ls.at[0]
        copy(ref, ref, ssem, e_r.at[0], sibling).wait_send()

    branch = [None]

    def on(cond):
        def run(body):
            branch[0] = cond
            pl.when(cond)(body)
            branch[0] = None

        return run

    def send(src, dst, ssem, rsem, to):
        copy(src, dst, ssem, rsem, to).start()
        note(branch[0], src, ssem)

    def send_when(cond, *copies):
        @pl.when(cond)
        def _():
            for one in copies:
                copy(*one).start()

        for one in copies:
            note(cond, one[0], one[2])

    def drain(of=None):
        later = [entry for entry in pending if of is not None and not any(entry[2][0] is sem for sem in of)]
        pending[:] = [entry for entry in pending if not any(entry is k for k in later)]
        for cond in (None, first, second):
            some = [entry[1:] for entry in pending if entry[0] is cond]
            if cond is None:
                for entry in some:
                    sent(*entry)
            elif some:

                @pl.when(cond)
                def _():
                    for entry in some:
                        sent(*entry)

        pending[:] = later + [entry for entry in pending if not any(entry[0] is k for k in (None, first, second))]

    def landed(dst, rsem):
        copy(dst, dst, (e_s, 0), rsem, sibling).wait_recv()


    fetch_text.wait()
    jbuf[0:HALF, :] = unit_rows(cap[...])[1].astype(BF16)
    pl.semaphore_wait(barrier, len(partners))

    def irows(slot, piece):
        return ibuf.at[pl.ds(slot * ROWS + piece * QUARTER, QUARTER)]

    def jrows(slot, c, start=0, count=QUARTER):
        return jbuf.at[pl.ds(pl.multiple_of(slot * HALF + c * QUARTER + start, EIGHTH), count)]

    def text_piece(slot, piece):
        return jrows(slot, core, piece * EIGHTH, EIGHTH)

    def text_send(side, d, piece, source, target):
        send(
            text_piece(source, piece),
            text_piece(target, piece),
            (t_s, side, d, piece),
            t_r.at[side, d, piece],
            z_down if side else z_up,
        )

    for piece in (0, 1):
        text_send(0, 0, piece, 0, 2)
        text_send(1, 0, piece, 0, 1)

    def to_y(slot, piece):
        target = y_up1 if piece < 2 else y_down1
        return (irows(slot, piece), irows(slot, piece), (i_s, 2 + slot, piece), i_r.at[slot, piece], target)

    def to_x(source, slot, piece, kind):
        target = x_up if slot == 1 or (slot == 3 and piece < 2) else x_down
        return (irows(source, piece), irows(slot, piece), (i_s, kind, piece), i_r.at[slot, piece], target)

    fetch_image.wait()

    @pl.when(first)
    def _():
        ibuf[0:ROWS, :] = unit_rows(pic[...])[1].astype(BF16)

    send_when(
        first,
        to_x(0, 1, 0, 0), to_x(0, 2, 2, 1), to_y(0, 0), to_y(0, 2),
        to_x(0, 1, 1, 0), to_x(0, 2, 3, 1), to_y(0, 1), to_y(0, 3),
        to_x(0, 1, 2, 0), to_x(0, 2, 0, 1), to_x(0, 1, 3, 0), to_x(0, 2, 1, 1),
    )

    def pass_near(up, down, onward):
        landed(irows(1, up), i_r.at[1, up])
        if onward:
            send(*to_x(1, 3, up, 6))
        send(*to_y(1, up))
        landed(irows(2, down), i_r.at[2, down])
        if onward:
            send(*to_x(2, 3, down, 6))
        send(*to_y(2, down))

    def pass_far(*pieces):
        for piece in pieces:
            landed(irows(3, piece), i_r.at[3, piece])
            send(*to_y(3, piece))

    def images_in(*slots):
        for slot in slots:
            for piece in range(4):
                landed(irows(slot, piece), i_r.at[slot, piece])

    for zeroed in (lacc,):

        def clear(n, carry):
            rows = pl.ds(pl.multiple_of(n * QUARTER, QUARTER), QUARTER)
            zeroed[rows, :] = jnp.zeros((QUARTER, zeroed.shape[1]), F32)
            return carry

        lax.fori_loop(0, 16, clear, 0)

    def swap(slot):
        send(jrows(slot, core), jrows(slot, core), (d_s, slot), d_r.at[slot], sibling)

    def swapped(*slots):
        for slot in slots:
            landed(jrows(slot, other), d_r.at[slot])

    def text_hop(d, pieces=(0, 1)):
        for piece in pieces:
            for side in (0, 1):
                if d == 4:
                    if piece == side:
                        landed(text_piece(7, piece), t_r.at[side, 3, piece])
                    continue
                here = 2 * d - side
                landed(text_piece(here, piece), t_r.at[side, d - 1, piece])
                if d < 3:
                    text_send(side, d, piece, here, here + 2)
                elif piece == side:
                    text_send(side, 3, piece, here, 7)
        if pieces[-1] == 0:
            return
        if d < 4:
            swap(2 * d - 1)
            swap(2 * d)
        else:
            swap(7)

    sharp, off = sharp_ref[0], off_ref[0]
    log2_e = 1.4426950408889634
    sharp2, off2 = sharp * log2_e, off * log2_e

    def logits_block(i, j, diagonal=False):
        ri, rj = slice(i * ROWS, (i + 1) * ROWS), slice(j * ROWS, (j + 1) * ROWS)
        logits = sharp2 * contract(ibuf[ri, :], jbuf[rj, :], ((1,), (1,))) + off2
        if diagonal:
            row = lax.broadcasted_iota(jnp.int32, (ROWS, ROWS), 0)
            col = lax.broadcasted_iota(jnp.int32, (ROWS, ROWS), 1)
            same = jnp.logical_and(row == col + yh * HALF, col < HALF)
            logits = jnp.where(same, -logits, logits)
        grown = jnp.exp2(logits)
        total = 1.0 + grown
        rough = pl.reciprocal(total, approx=True)
        inverse = rough * (2.0 - total * rough)
        coef = grown * inverse
        lost = (grown - (total - 1.0)) * inverse
        lacc[ri, :] += jnp.log(total[:, :HALF] * total[:, HALF:]) + (lost[:, :HALF] + lost[:, HALF:])
        if diagonal:
            coef = jnp.where(same, -coef, coef)
        coef = coef.astype(BF16)
        cbuf[ri, rj] = coef
        ctbuf[rj, ri] = coef.T

    def product(out, left, right, m, k0, k1):
        rows, depth = slice(m * ROWS, (m + 1) * ROWS), slice(k0 * ROWS, k1 * ROWS)
        a = left[rows, depth]
        for n in range(0, WIDTH, 256):
            columns = slice(n, min(n + 256, WIDTH))
            result = contract(a, right[depth, columns], ((1,), (0,)))
            out[rows, columns] = result if k0 == 0 else out[rows, columns] + result

    def image_product(i, j0, j1):
        product(pacc, cbuf, jbuf, i, j0, j1)

    def text_product(j, i0, i1):
        product(tacc, ctbuf, ibuf, j, i0, i1)

    up_hi = lax.rem(y + 1, NY) // 2
    turns = (
        other * 2 * (1 - yh) + core * 2 * up_hi,
        core * (2 * up_hi + 1),
        other * 2 * yh + core * 2 * (1 - up_hi),
        core * (2 * (1 - up_hi) + 1),
    )

    def hand_over(slot):
        for side, q, to in ((0, 2 * yh + 1, y_up1), (1, 2 * (1 - yh) + 1, y_down1)):
            rows = pl.ds(pl.multiple_of(slot * ROWS + q * QUARTER, QUARTER), QUARTER)
            ys[side, slot] = pacc[rows, :].astype(BF16)
            send(ys.at[side, slot], yr.at[side, slot], (yc_s, side, slot), yc_r.at[side, slot], to)

    def handed(slot):
        rows = part_rows(slot, 3)
        for side in (0, 1):
            landed(yr.at[side, slot], yc_r.at[side, slot])
        pacc[rows, :] += yr[0, slot].astype(F32) + yr[1, slot].astype(F32)

    def seat(k):
        return pl.ds(k * QUARTER, QUARTER)

    def part_rows(slot, k):
        return pl.ds(pl.multiple_of(slot * ROWS + turns[k] * QUARTER, QUARTER), QUARTER)

    def far_turn(k):
        pb[0, seat(k), :] = pacc[part_rows(3, k), :].astype(BF16)
        send(pb.at[0, seat(k)], xr1.at[seat(k)], (x1_s, k), x1_r.at[k], x_up if k < 2 else x_down)

    def near_turn(slot, k):
        side = 0 if slot == 2 else 1
        rows = pacc[part_rows(slot, k), :]
        if (k < 2) == (slot == 2):
            landed(xr1.at[seat(k)], x1_r.at[k])
            rows = rows + xr1[seat(k), :].astype(F32)
        pb[1 + side, seat(k), :] = rows.astype(BF16)
        send(
            pb.at[1 + side, seat(k)],
            x2.at[side, seat(k)],
            (x2_s, side, k),
            x2_r.at[side, k],
            x_down if side else x_up,
        )

    def text_over(low, count):
        for slot in range(low, low + count):
            mine = pl.ds(pl.multiple_of(slot * HALF + other * QUARTER, QUARTER), QUARTER)
            ts[slot] = tacc[mine, :].astype(BF16)
        slots = pl.ds(low, count)
        send(ts.at[slots], tr.at[slots], (e_s, low), e_r.at[low], sibling)

    def text_came(low, count):
        landed(tr.at[pl.ds(low, count)], e_r.at[low])

    def piece_rows(piece):
        return pl.ds(piece * EIGHTH, EIGHTH)

    def text_sum(slot, piece):
        start = slot * HALF + core * QUARTER + piece * EIGHTH
        return tacc[pl.ds(pl.multiple_of(start, EIGHTH), EIGHTH), :] + tr[slot, piece_rows(piece), :].astype(F32)

    def text_back(d, steps=(0, 1)):
        for step in steps:
            for side in (0, 1):
                piece = step if side else 1 - step
                if d == 4 and piece != side:
                    continue
                rows = text_sum(7 if d == 4 else 2 * d - 1 + side, piece)
                part = piece_rows(piece)
                if d < 3 or (d == 3 and piece == side):
                    landed(vr.at[side, d, part], v_r.at[side, d, piece])
                    rows = rows + vr[side, d, part, :].astype(F32)
                vs[side, d - 1, part, :] = rows.astype(BF16)
                send(
                    vs.at[side, d - 1, part],
                    vr.at[side, d - 1, part],
                    (v_s, side, d - 1, piece),
                    v_r.at[side, d - 1, piece],
                    z_down if side else z_up,
                )

    @on(first)
    def _():
        text_hop(1, (0,))
        pass_near(0, 2, True)
        text_hop(1, (1,))
        pass_near(1, 3, True)
        swapped(1)
        logits_block(0, 0, True)
        pass_near(2, 0, False)
        text_hop(2, (0,))
        text_hop(2, (1,))
        pass_near(3, 1, False)
        swapped(2, 3)
        logits_block(0, 1)
        pass_far(0, 2)
        logits_block(1, 0)
        logits_block(2, 0)
        image_product(0, 0, 2)
        text_hop(3)
        pass_far(1, 3)
        logits_block(1, 1)
        logits_block(2, 1)
        image_product(1, 0, 2)
        logits_block(3, 0)
        image_product(2, 0, 2)
        logits_block(3, 1)
        swapped(4, 5)
        text_hop(4)
        text_product(0, 0, 4)
        logits_block(0, 2)
        text_product(1, 0, 4)
        logits_block(1, 2)
        image_product(3, 0, 2)
        logits_block(2, 2)
        logits_block(3, 2)
        text_product(2, 0, 4)
        text_over(0, 4)
        text_over(4, 2)
        swapped(6, 7)
        logits_block(3, 3)
        logits_block(1, 3)
        image_product(3, 2, 4)
        logits_block(2, 3)
        logits_block(0, 3)
        text_product(3, 0, 4)
        text_over(6, 2)
        image_product(1, 2, 4)
        far_turn(0)
        far_turn(2)
        hand_over(3)
        near_turn(1, 0)
        hand_over(1)
        image_product(2, 2, 4)
        near_turn(2, 2)
        hand_over(2)
        image_product(0, 2, 4)
        hand_over(0)
        text_came(6, 2)
        text_back(4)
        text_came(4, 2)
        text_back(3, (0,))

    @on(second)
    def _():
        text_hop(1)
        images_in(0)
        swapped(1)
        logits_block(0, 0)
        text_hop(2)
        swapped(2, 3)
        logits_block(0, 1)
        text_hop(3)
        swapped(4, 5)
        logits_block(0, 2)
        image_product(0, 0, 3)
        text_hop(4)
        images_in(1, 2)
        logits_block(1, 0)
        logits_block(2, 0)
        logits_block(1, 1)
        text_product(0, 0, 3)
        logits_block(2, 1)
        logits_block(1, 2)
        text_product(1, 0, 3)
        logits_block(2, 2)
        swapped(6, 7)
        logits_block(1, 3)
        text_product(2, 0, 3)
        logits_block(2, 3)
        image_product(1, 0, 4)
        logits_block(0, 3)
        image_product(2, 0, 4)
        text_product(3, 0, 3)
        near_turn(1, 0)
        near_turn(2, 2)
        near_turn(1, 1)
        images_in(3)
        logits_block(3, 3)
        logits_block(3, 2)
        text_product(3, 3, 4)
        text_over(6, 2)
        logits_block(3, 1)
        text_product(2, 3, 4)
        text_over(4, 2)
        logits_block(3, 0)
        text_product(1, 3, 4)
        text_came(6, 2)
        text_back(4)
        text_product(0, 3, 4)
        text_over(0, 4)
        image_product(3, 0, 4)
        far_turn(0)
        far_turn(2)
        far_turn(1)
        text_came(4, 2)
        text_back(3, (0,))
        handed(3)
        far_turn(3)
        handed(2)
        near_turn(2, 3)
        image_product(0, 3, 4)

    near_turn(2, 0)
    near_turn(1, 2)
    text_back(3, (1,))

    ones = jnp.ones((8, HALF), F32)
    for i in range(4):
        ls[i] = lax.dot_general(
            ones,
            lacc[i * ROWS : (i + 1) * ROWS, :],
            (((1,), (1,)), ((), ())),
            precision=lax.Precision.HIGHEST,
            preferred_element_type=F32,
        )
    send(ls.at[2], lx.at[0], (lx_s, 0), lx_r.at[0], x_up)
    send(ls.at[1], lx.at[1], (lx_s, 1), lx_r.at[1], x_down)
    send(ls.at[3], lx.at[2], (lx_s, 2), lx_r.at[2], x_far)

    text_came(0, 4)
    text_back(2, (0,))

    @on(second)
    def _():
        near_turn(2, 1)
        handed(1)
        near_turn(1, 3)

    text_back(2, (1,))
    text_back(1, (0,))

    source = yh + 2 * core
    block_yl = lax.rem(yl + core, 2)

    def owner_of(q):
        to = at(x, 2 * (q // 2) + block_yl, z, q % 2)
        return to, jnp.logical_and(dp == to[0], split == to[1])

    for k in range(3):
        landed(lx.at[k], lx_r.at[k])
    rl[...] = ls[0] + lx[0] + lx[1] + lx[2]
    for q in range(4):
        to, own = owner_of(q)
        send_when(jnp.logical_not(own), (rl, lq.at[source], (ly_s, q), ly_r.at[source], to))

        @pl.when(own)
        def _():
            lq[source] = rl[...]

    text_back(1, (1,))
    drain((i_s, t_s, d_s))

    y_up0, y_down0 = at(x, y + 1, z, 0), at(x, y + 3, z, 0)

    def image_sum(k):
        landed(x2.at[0, seat(k)], x2_r.at[0, k])
        landed(x2.at[1, seat(k)], x2_r.at[1, k])
        return pacc[part_rows(0, k), :] + (x2[0, seat(k), :].astype(F32) + x2[1, seat(k), :].astype(F32))

    def image_out(k, box, to):
        total = image_sum(k)
        if core_of[0] == 1 and k == 0:
            landed(qr.at[3], y_r.at[3])
            total = total + qr[3].astype(F32)
        rb[seat(k), :] = total.astype(BF16)
        send(rb.at[seat(k)], qr.at[box], (y_s, k), y_r.at[box], to)

    core_of = [0]

    @on(first)
    def _():
        image_out(0, 3, y_up1)
        qr[0] = image_sum(2).astype(BF16)

    core_of[0] = 1

    @on(second)
    def _():
        qr[0] = jnp.zeros((QUARTER, WIDTH), BF16)
        image_out(2, 2, y_down0)
        image_out(0, 1, y_up0)

    mine = yh * 2 + core
    outs = (both_out.at[pl.ds(0, ROWS)], both_out.at[pl.ds(ROWS, ROWS)])

    def quarter_rows(q, start=0, count=QUARTER):
        return pl.ds(pl.multiple_of(q * QUARTER + start, EIGHTH), count)

    my_rows = quarter_rows(mine)
    y_up, y_down = at(x, y + 1, z, core), at(x, y + 3, z, core)

    def gather_out(kind, grad, values):
        inverse, unit = unit_rows(values)
        out = outs[kind]
        out[my_rows, :] = unit_back(unit, inverse, sharp * grad).astype(BF16)
        low, high = out.at[quarter_rows(mine, 0, EIGHTH)], out.at[quarter_rows(mine, EIGHTH, EIGHTH)]
        send(low, hop.at[kind, 0], (g_s, kind, 0), g_r.at[kind, 0], y_up)
        send(high, hop.at[kind, 1], (g_s, kind, 1), g_r.at[kind, 1], y_down)
        send(out.at[my_rows], out.at[my_rows], (g_s, kind, 2), g_r.at[kind, 2], sibling)

    def gather_on(kind):
        out = outs[kind]
        landed(hop.at[kind, 0], g_r.at[kind, 0])
        there = out.at[quarter_rows(2 * (1 - up_hi) + core, 0, EIGHTH)]
        send(hop.at[kind, 0], there, (g_s, kind, 3), g_r.at[kind, 3], y_up)
        landed(hop.at[kind, 1], g_r.at[kind, 1])
        there = out.at[quarter_rows(2 * up_hi + core, EIGHTH, EIGHTH)]
        send(hop.at[kind, 1], there, (g_s, kind, 4), g_r.at[kind, 4], y_down)

    def gather_over(kind):
        for half in (0, 1):
            here = outs[kind].at[quarter_rows((1 - yh) * 2 + core, half * EIGHTH, EIGHTH)]
            landed(here, g_r.at[kind, 3 + half])
            send(here, here, (g_s, kind, 5 + half), g_r.at[kind, 5 + half], sibling)

    def gather_end(kind):
        landed(outs[kind].at[quarter_rows(yh * 2 + other)], g_r.at[kind, 2])
        for half in (0, 1):
            here = outs[kind].at[quarter_rows((1 - yh) * 2 + other, half * EIGHTH, EIGHTH)]
            landed(here, g_r.at[kind, 5 + half])

    grads = []
    for piece in (0, 1):
        grad = text_sum(0, piece)
        for side in (0, 1):
            landed(vr.at[side, 0, piece_rows(piece)], v_r.at[side, 0, piece])
            grad = grad + vr[side, 0, piece_rows(piece), :].astype(F32)
        grads.append(grad)
    grad = jnp.concatenate(grads, axis=0)
    gather_out(1, grad, cap[pl.ds(pl.multiple_of(core * QUARTER, QUARTER), QUARTER), :])

    @on(second)
    def _():
        image_out(1, 1, y_up1)
        handed(0)
        image_out(3, 2, y_down1)

    gather_on(1)

    for k in range(4):
        here = jnp.logical_and(first, yh == k)

        @pl.when(jnp.logical_not(here))
        def _():
            landed(lq.at[k], ly_r.at[k])

    loss_out[...] = ((lq[0] + lq[1]) + (lq[2] + lq[3])) * (1.0 / PAIRS)

    landed(qr.at[1], y_r.at[1])
    landed(qr.at[2], y_r.at[2])
    grad = qr[0].astype(F32) + (qr[1].astype(F32) + qr[2].astype(F32))
    gather_out(0, grad, pic[my_rows, :])
    gather_over(1)
    drain()
    gather_on(0)
    gather_over(0)
    gather_end(1)
    gather_end(0)

    drain()
    for cond, rows, ssem in pending:

        @pl.when(cond)
        def _():
            sent(rows, ssem)


def per_device(picture_vectors, caption_vectors, sharpness_entry, offset_shift):
    dma = pltpu.SemaphoreType.DMA
    vmem = pl.BlockSpec(memory_space=pltpu.VMEM)
    smem = pl.BlockSpec(memory_space=pltpu.SMEM)
    hbm = pl.BlockSpec(memory_space=pltpu.HBM)
    both, loss = pl.pallas_call(
        kernel,
        out_shape=(
            jax.ShapeDtypeStruct((2 * ROWS, WIDTH), BF16),
            jax.ShapeDtypeStruct((8, ROWS), F32),
        ),
        in_specs=[hbm, hbm, smem, smem],
        out_specs=(vmem, vmem),
        scratch_shapes=[
            pltpu.VMEM((ROWS, WIDTH), BF16),
            pltpu.VMEM((HALF, WIDTH), BF16),
            pltpu.VMEM((4 * ROWS, WIDTH), BF16),
            pltpu.VMEM((8 * HALF, WIDTH), BF16),
            pltpu.VMEM((4 * ROWS, 8 * HALF), BF16),
            pltpu.VMEM((8 * HALF, 4 * ROWS), BF16),
            pltpu.VMEM((4 * ROWS, WIDTH), F32),
            pltpu.VMEM((8 * HALF, WIDTH), F32),
            pltpu.VMEM((4 * ROWS, HALF), F32),
            pltpu.VMEM((3, ROWS, WIDTH), BF16),
            pltpu.VMEM((ROWS, WIDTH), BF16),
            pltpu.VMEM((2, ROWS, WIDTH), BF16),
            pltpu.VMEM((ROWS, WIDTH), BF16),
            pltpu.VMEM((4, QUARTER, WIDTH), BF16),
            pltpu.VMEM((2, 4, QUARTER, WIDTH), BF16),
            pltpu.VMEM((2, 4, QUARTER, WIDTH), BF16),
            pltpu.VMEM((8, QUARTER, WIDTH), BF16),
            pltpu.VMEM((8, QUARTER, WIDTH), BF16),
            pltpu.VMEM((2, 4, QUARTER, WIDTH), BF16),
            pltpu.VMEM((2, 4, QUARTER, WIDTH), BF16),
            pltpu.VMEM((4, 8, ROWS), F32),
            pltpu.VMEM((3, 8, ROWS), F32),
            pltpu.VMEM((8, ROWS), F32),
            pltpu.VMEM((4, 8, ROWS), F32),
            pltpu.VMEM((2, 2, EIGHTH, WIDTH), BF16),
            dma((2,)),
            dma((7, 4)), dma((4, 4)),
            dma((2, 4, 2)), dma((2, 4, 2)),
            dma((8,)), dma((8,)),
            dma((4,)), dma((4,)),
            dma((2, 4)), dma((2, 4)),
            dma((4,)), dma((4,)),
            dma((2, 4)), dma((2, 4)),
            dma((4,)), dma((4,)),
            dma((3,)), dma((3,)),
            dma((8,)), dma((8,)),
            dma((2, 4, 2)), dma((2, 4, 2)),
            dma((2, 7)), dma((2, 7)),
        ],
        compiler_params=pltpu.CompilerParams(
            collective_id=0, has_side_effects=True, vmem_limit_bytes=48 * 1024 * 1024
        ),
        cost_estimate=pl.CostEstimate(flops=7_300_000_000, bytes_accessed=4_000_000, transcendentals=3_000_000),
    )(
        pltpu.with_memory_space_constraint(picture_vectors, pltpu.HBM),
        pltpu.with_memory_space_constraint(caption_vectors, pltpu.HBM),
        sharpness_entry,
        offset_shift,
    )
    return both[:ROWS].astype(F32), both[ROWS:].astype(F32), loss[0]


def solution(mesh):
    placed = (P("dp", None), P("dp", None), P(), P())
    return jax.shard_map(
        per_device,
        mesh=mesh,
        in_specs=placed,
        out_specs=(P("dp", None), P("dp", None), P("dp")),
        check_vma=False,
    )
```

```python
import jax
import jax.numpy as jnp
from jax import lax
from jax.experimental import pallas as pl
from jax.experimental.pallas import tpu as pltpu
from jax.sharding import PartitionSpec as P

MESH = pl.DeviceIdType.MESH
F32 = jnp.float32
BF16 = jnp.bfloat16

NX, NY, NZ = 4, 4, 8
ROWS, WIDTH = 256, 1152
HALF, QUARTER, EIGHTH = 128, 64, 32
PAIRS = 16384


def unit_rows(values):
    values = values.astype(F32)
    inverse = lax.rsqrt(jnp.sum(values * values, axis=1, keepdims=True) + 1e-06)
    return inverse, values * inverse


def unit_back(unit, inverse, grad):
    return (grad - unit * jnp.sum(unit * grad, axis=1, keepdims=True)) * inverse


def contract(a, b, dims):
    return lax.dot_general(a, b, (dims, ((), ())), preferred_element_type=F32)


def kernel(
    pic_hbm, cap_hbm, sharp_ref, off_ref,
    both_out, loss_out,
    pic, cap, ibuf, jbuf, cbuf, ctbuf, pacc, tacc, lacc,
    pb, xr1, x2, rb, qr, ys, yr,
    ts, tr, vs, vr,
    ls, lx, rl, lq,
    hop,
    in_sem, i_s, i_r, t_s, t_r, d_s, d_r, x1_s, x1_r, x2_s, x2_r, y_s, y_r, yc_s, yc_r,
    ly_s, ly_r, lx_s, lx_r, e_s, e_r, v_s, v_r, g_s, g_r,
):
    dp, split = lax.axis_index("dp"), lax.axis_index("split")
    x = lax.rem(dp, NX)
    yl = lax.rem(dp // NX, 2)
    z = dp // (2 * NX)
    yh, core = split // 2, lax.rem(split, 2)
    y = 2 * yh + yl
    other = 1 - core
    first = core == 0
    second = core == 1

    def at(px, py, pz, pc):
        px, py, pz = lax.rem(px, NX), lax.rem(py, NY), lax.rem(pz, NZ)
        return ((pz * 2 + lax.rem(py, 2)) * NX + px, (py // 2) * 2 + pc)

    sibling = at(x, y, z, other)
    x_up, x_down, x_far = (at(x + k, y, z, core) for k in (1, 3, 2))
    z_up, z_down = at(x, y, z + 1, core), at(x, y, z + 7, core)
    y_up1, y_down1 = at(x, y + 1, z, 1), at(x, y + 3, z, 1)

    own_text = pl.multiple_of(yh * HALF, HALF)
    fetch_text = pltpu.make_async_copy(cap_hbm.at[pl.ds(own_text, HALF)], cap, in_sem.at[0])
    fetch_image = pltpu.make_async_copy(pic_hbm, pic, in_sem.at[1])
    fetch_text.start()
    fetch_image.start()

    barrier = pltpu.get_barrier_semaphore()
    partners = [sibling, x_up, x_down, x_far, z_up, z_down]
    partners += [at(x, y + k, z, c) for k in (1, 2, 3) for c in (0, 1)]
    for partner in partners:
        pl.semaphore_signal(barrier, inc=1, device_id=partner, device_id_type=MESH)

    pending = []

    def copy(src, dst, send, recv, to):
        return pltpu.make_async_remote_copy(
            src_ref=src, dst_ref=dst, send_sem=send[0].at[send[1:]], recv_sem=recv, device_id=to, device_id_type=MESH
        )

    def note(cond, src, ssem):
        rows = 0 if src.dtype == F32 else src.shape[0] * (src.shape[1] if len(src.shape) == 3 else 1)
        pending.append((cond, rows, ssem))

    def sent(rows, ssem):
        ref = ibuf.at[pl.ds(0, rows)] if rows else ls.at[0]
        copy(ref, ref, ssem, e_r.at[0], sibling).wait_send()

    branch = [None]

    def on(cond):
        def run(body):
            branch[0] = cond
            pl.when(cond)(body)
            branch[0] = None

        return run

    def send(src, dst, ssem, rsem, to):
        copy(src, dst, ssem, rsem, to).start()
        note(branch[0], src, ssem)

    def send_when(cond, *copies):
        @pl.when(cond)
        def _():
            for one in copies:
                copy(*one).start()

        for one in copies:
            note(cond, one[0], one[2])

    def drain(of=None):
        later = [entry for entry in pending if of is not None and not any(entry[2][0] is sem for sem in of)]
        pending[:] = [entry for entry in pending if not any(entry is k for k in later)]
        for cond in (None, first, second):
            some = [entry[1:] for entry in pending if entry[0] is cond]
            if cond is None:
                for entry in some:
                    sent(*entry)
            elif some:

                @pl.when(cond)
                def _():
                    for entry in some:
                        sent(*entry)

        pending[:] = later + [entry for entry in pending if not any(entry[0] is k for k in (None, first, second))]

    def landed(dst, rsem):
        copy(dst, dst, (e_s, 0), rsem, sibling).wait_recv()


    fetch_text.wait()
    jbuf[0:HALF, :] = unit_rows(cap[...])[1].astype(BF16)
    pl.semaphore_wait(barrier, len(partners))

    def irows(slot, piece):
        return ibuf.at[pl.ds(slot * ROWS + piece * QUARTER, QUARTER)]

    def jrows(slot, c, start=0, count=QUARTER):
        return jbuf.at[pl.ds(pl.multiple_of(slot * HALF + c * QUARTER + start, EIGHTH), count)]

    def text_piece(slot, piece):
        return jrows(slot, core, piece * EIGHTH, EIGHTH)

    def text_send(side, d, piece, source, target):
        send(
            text_piece(source, piece),
            text_piece(target, piece),
            (t_s, side, d, piece),
            t_r.at[side, d, piece],
            z_down if side else z_up,
        )

    for piece in (0, 1):
        text_send(0, 0, piece, 0, 2)
        text_send(1, 0, piece, 0, 1)

    def to_y(slot, piece):
        target = y_up1 if piece < 2 else y_down1
        return (irows(slot, piece), irows(slot, piece), (i_s, 2 + slot, piece), i_r.at[slot, piece], target)

    def to_x(source, slot, piece, kind):
        target = x_up if slot == 1 or (slot == 3 and piece < 2) else x_down
        return (irows(source, piece), irows(slot, piece), (i_s, kind, piece), i_r.at[slot, piece], target)

    fetch_image.wait()

    @pl.when(first)
    def _():
        ibuf[0:ROWS, :] = unit_rows(pic[...])[1].astype(BF16)

    send_when(
        first,
        to_x(0, 1, 0, 0), to_x(0, 2, 2, 1), to_y(0, 0), to_y(0, 2),
        to_x(0, 1, 1, 0), to_x(0, 2, 3, 1), to_y(0, 1), to_y(0, 3),
        to_x(0, 1, 2, 0), to_x(0, 2, 0, 1), to_x(0, 1, 3, 0), to_x(0, 2, 1, 1),
    )

    def pass_near(up, down, onward):
        landed(irows(1, up), i_r.at[1, up])
        if onward:
            send(*to_x(1, 3, up, 6))
        send(*to_y(1, up))
        landed(irows(2, down), i_r.at[2, down])
        if onward:
            send(*to_x(2, 3, down, 6))
        send(*to_y(2, down))

    def pass_far(*pieces):
        for piece in pieces:
            landed(irows(3, piece), i_r.at[3, piece])
            send(*to_y(3, piece))

    def images_in(*slots):
        for slot in slots:
            for piece in range(4):
                landed(irows(slot, piece), i_r.at[slot, piece])

    for zeroed in (lacc,):

        def clear(n, carry):
            rows = pl.ds(pl.multiple_of(n * QUARTER, QUARTER), QUARTER)
            zeroed[rows, :] = jnp.zeros((QUARTER, zeroed.shape[1]), F32)
            return carry

        lax.fori_loop(0, 16, clear, 0)

    def swap(slot):
        send(jrows(slot, core), jrows(slot, core), (d_s, slot), d_r.at[slot], sibling)

    def swapped(*slots):
        for slot in slots:
            landed(jrows(slot, other), d_r.at[slot])

    def text_hop(d, pieces=(0, 1)):
        for piece in pieces:
            for side in (0, 1):
                if d == 4:
                    if piece == side:
                        landed(text_piece(7, piece), t_r.at[side, 3, piece])
                    continue
                here = 2 * d - side
                landed(text_piece(here, piece), t_r.at[side, d - 1, piece])
                if d < 3:
                    text_send(side, d, piece, here, here + 2)
                elif piece == side:
                    text_send(side, 3, piece, here, 7)
        if pieces[-1] == 0:
            return
        if d < 4:
            swap(2 * d - 1)
            swap(2 * d)
        else:
            swap(7)

    sharp, off = sharp_ref[0], off_ref[0]
    log2_e = 1.4426950408889634
    sharp2, off2 = sharp * log2_e, off * log2_e

    def logits_block(i, j, diagonal=False):
        ri, rj = slice(i * ROWS, (i + 1) * ROWS), slice(j * ROWS, (j + 1) * ROWS)
        logits = sharp2 * contract(ibuf[ri, :], jbuf[rj, :], ((1,), (1,))) + off2
        if diagonal:
            row = lax.broadcasted_iota(jnp.int32, (ROWS, ROWS), 0)
            col = lax.broadcasted_iota(jnp.int32, (ROWS, ROWS), 1)
            same = jnp.logical_and(row == col + yh * HALF, col < HALF)
            logits = jnp.where(same, -logits, logits)
        grown = jnp.exp2(logits)
        total = 1.0 + grown
        rough = pl.reciprocal(total, approx=True)
        inverse = rough * (2.0 - total * rough)
        coef = grown * inverse
        lost = (grown - (total - 1.0)) * inverse
        lacc[ri, :] += jnp.log(total[:, :HALF] * total[:, HALF:]) + (lost[:, :HALF] + lost[:, HALF:])
        if diagonal:
            coef = jnp.where(same, -coef, coef)
        coef = coef.astype(BF16)
        cbuf[ri, rj] = coef
        ctbuf[rj, ri] = coef.T

    def product(out, left, right, m, k0, k1):
        rows, depth = slice(m * ROWS, (m + 1) * ROWS), slice(k0 * ROWS, k1 * ROWS)
        a = left[rows, depth]
        for n in range(0, WIDTH, 256):
            columns = slice(n, min(n + 256, WIDTH))
            result = contract(a, right[depth, columns], ((1,), (0,)))
            out[rows, columns] = result if k0 == 0 else out[rows, columns] + result

    def image_product(i, j0, j1):
        product(pacc, cbuf, jbuf, i, j0, j1)

    def text_product(j, i0, i1):
        product(tacc, ctbuf, ibuf, j, i0, i1)

    up_hi = lax.rem(y + 1, NY) // 2
    turns = (
        other * 2 * (1 - yh) + core * 2 * up_hi,
        core * (2 * up_hi + 1),
        other * 2 * yh + core * 2 * (1 - up_hi),
        core * (2 * (1 - up_hi) + 1),
    )

    def hand_over(slot):
        for side, q, to in ((0, 2 * yh + 1, y_up1), (1, 2 * (1 - yh) + 1, y_down1)):
            rows = pl.ds(pl.multiple_of(slot * ROWS + q * QUARTER, QUARTER), QUARTER)
            ys[side, slot] = pacc[rows, :].astype(BF16)
            send(ys.at[side, slot], yr.at[side, slot], (yc_s, side, slot), yc_r.at[side, slot], to)

    def handed(slot):
        rows = part_rows(slot, 3)
        for side in (0, 1):
            landed(yr.at[side, slot], yc_r.at[side, slot])
        pacc[rows, :] += yr[0, slot].astype(F32) + yr[1, slot].astype(F32)

    def seat(k):
        return pl.ds(k * QUARTER, QUARTER)

    def part_rows(slot, k):
        return pl.ds(pl.multiple_of(slot * ROWS + turns[k] * QUARTER, QUARTER), QUARTER)

    def far_turn(k):
        pb[0, seat(k), :] = pacc[part_rows(3, k), :].astype(BF16)
        send(pb.at[0, seat(k)], xr1.at[seat(k)], (x1_s, k), x1_r.at[k], x_up if k < 2 else x_down)

    def near_turn(slot, k):
        side = 0 if slot == 2 else 1
        rows = pacc[part_rows(slot, k), :]
        if (k < 2) == (slot == 2):
            landed(xr1.at[seat(k)], x1_r.at[k])
            rows = rows + xr1[seat(k), :].astype(F32)
        pb[1 + side, seat(k), :] = rows.astype(BF16)
        send(
            pb.at[1 + side, seat(k)],
            x2.at[side, seat(k)],
            (x2_s, side, k),
            x2_r.at[side, k],
            x_down if side else x_up,
        )

    def text_over(low, count):
        for slot in range(low, low + count):
            mine = pl.ds(pl.multiple_of(slot * HALF + other * QUARTER, QUARTER), QUARTER)
            ts[slot] = tacc[mine, :].astype(BF16)
        slots = pl.ds(low, count)
        send(ts.at[slots], tr.at[slots], (e_s, low), e_r.at[low], sibling)

    def text_came(low, count):
        landed(tr.at[pl.ds(low, count)], e_r.at[low])

    def piece_rows(piece):
        return pl.ds(piece * EIGHTH, EIGHTH)

    def text_sum(slot, piece):
        start = slot * HALF + core * QUARTER + piece * EIGHTH
        return tacc[pl.ds(pl.multiple_of(start, EIGHTH), EIGHTH), :] + tr[slot, piece_rows(piece), :].astype(F32)

    def text_back(d, steps=(0, 1)):
        for step in steps:
            for side in (0, 1):
                piece = step if side else 1 - step
                if d == 4 and piece != side:
                    continue
                rows = text_sum(7 if d == 4 else 2 * d - 1 + side, piece)
                part = piece_rows(piece)
                if d < 3 or (d == 3 and piece == side):
                    landed(vr.at[side, d, part], v_r.at[side, d, piece])
                    rows = rows + vr[side, d, part, :].astype(F32)
                vs[side, d - 1, part, :] = rows.astype(BF16)
                send(
                    vs.at[side, d - 1, part],
                    vr.at[side, d - 1, part],
                    (v_s, side, d - 1, piece),
                    v_r.at[side, d - 1, piece],
                    z_down if side else z_up,
                )

    @on(first)
    def _():
        text_hop(1, (0,))
        pass_near(0, 2, True)
        text_hop(1, (1,))
        pass_near(1, 3, True)
        swapped(1)
        logits_block(0, 0, True)
        pass_near(2, 0, False)
        text_hop(2, (0,))
        text_hop(2, (1,))
        pass_near(3, 1, False)
        swapped(2, 3)
        logits_block(0, 1)
        pass_far(0, 2)
        logits_block(1, 0)
        logits_block(2, 0)
        image_product(0, 0, 2)
        text_hop(3)
        pass_far(1, 3)
        logits_block(1, 1)
        logits_block(2, 1)
        image_product(1, 0, 2)
        logits_block(3, 0)
        image_product(2, 0, 2)
        logits_block(3, 1)
        swapped(4, 5)
        text_hop(4)
        text_product(0, 0, 4)
        logits_block(0, 2)
        text_product(1, 0, 4)
        logits_block(1, 2)
        image_product(3, 0, 2)
        logits_block(2, 2)
        logits_block(3, 2)
        text_product(2, 0, 4)
        text_over(0, 4)
        text_over(4, 2)
        swapped(6, 7)
        logits_block(3, 3)
        logits_block(1, 3)
        image_product(3, 2, 4)
        far_turn(0)
        far_turn(2)
        hand_over(3)
        logits_block(2, 3)
        logits_block(0, 3)
        text_product(3, 0, 4)
        text_over(6, 2)
        image_product(1, 2, 4)
        near_turn(1, 0)
        hand_over(1)
        image_product(2, 2, 4)
        near_turn(2, 2)
        hand_over(2)
        image_product(0, 2, 4)
        hand_over(0)
        text_came(6, 2)
        text_back(4)
        text_came(4, 2)
        text_back(3, (0,))

    @on(second)
    def _():
        text_hop(1)
        images_in(0)
        swapped(1)
        logits_block(0, 0)
        text_hop(2)
        swapped(2, 3)
        logits_block(0, 1)
        text_hop(3)
        swapped(4, 5)
        logits_block(0, 2)
        image_product(0, 0, 3)
        text_hop(4)
        images_in(1, 2)
        logits_block(1, 0)
        logits_block(2, 0)
        logits_block(1, 1)
        text_product(0, 0, 3)
        logits_block(2, 1)
        logits_block(1, 2)
        text_product(1, 0, 3)
        logits_block(2, 2)
        swapped(6, 7)
        logits_block(1, 3)
        text_product(2, 0, 3)
        logits_block(2, 3)
        image_product(1, 0, 4)
        logits_block(0, 3)
        image_product(2, 0, 4)
        text_product(3, 0, 3)
        near_turn(1, 0)
        near_turn(2, 2)
        near_turn(1, 1)
        images_in(3)
        logits_block(3, 3)
        logits_block(3, 2)
        text_product(3, 3, 4)
        logits_block(3, 1)
        text_over(6, 2)
        logits_block(3, 0)
        image_product(3, 0, 4)
        far_turn(0)
        far_turn(2)
        far_turn(1)
        text_came(6, 2)
        text_back(4)
        text_product(2, 3, 4)
        text_over(4, 2)
        text_product(1, 3, 4)
        text_product(0, 3, 4)
        text_over(0, 4)
        handed(3)
        far_turn(3)
        text_came(4, 2)
        text_back(3, (0,))
        handed(2)
        near_turn(2, 3)
        image_product(0, 3, 4)

    near_turn(2, 0)
    near_turn(1, 2)
    text_back(3, (1,))

    ones = jnp.ones((8, HALF), F32)
    for i in range(4):
        ls[i] = lax.dot_general(
            ones,
            lacc[i * ROWS : (i + 1) * ROWS, :],
            (((1,), (1,)), ((), ())),
            precision=lax.Precision.HIGHEST,
            preferred_element_type=F32,
        )
    send(ls.at[2], lx.at[0], (lx_s, 0), lx_r.at[0], x_up)
    send(ls.at[1], lx.at[1], (lx_s, 1), lx_r.at[1], x_down)
    send(ls.at[3], lx.at[2], (lx_s, 2), lx_r.at[2], x_far)

    text_came(0, 4)
    text_back(2, (0,))

    @on(second)
    def _():
        near_turn(2, 1)
        handed(1)
        near_turn(1, 3)

    text_back(2, (1,))
    text_back(1, (0,))

    y_up0, y_down0 = at(x, y + 1, z, 0), at(x, y + 3, z, 0)

    def image_sum(k):
        landed(x2.at[0, seat(k)], x2_r.at[0, k])
        landed(x2.at[1, seat(k)], x2_r.at[1, k])
        return pacc[part_rows(0, k), :] + (x2[0, seat(k), :].astype(F32) + x2[1, seat(k), :].astype(F32))

    def image_out(k, box, to):
        total = image_sum(k)
        if core_of[0] == 1 and k == 0:
            landed(qr.at[3], y_r.at[3])
            total = total + qr[3].astype(F32)
        rb[seat(k), :] = total.astype(BF16)
        send(rb.at[seat(k)], qr.at[box], (y_s, k), y_r.at[box], to)

    core_of = [0]

    @on(first)
    def _():
        image_out(0, 3, y_up1)

    core_of[0] = 1

    @on(second)
    def _():
        image_out(2, 2, y_down0)

    text_back(1, (1,))

    @on(first)
    def _():
        qr[0] = image_sum(2).astype(BF16)

    @on(second)
    def _():
        qr[0] = jnp.zeros((QUARTER, WIDTH), BF16)
        image_out(0, 1, y_up0)

    source = yh + 2 * core
    block_yl = lax.rem(yl + core, 2)

    def owner_of(q):
        to = at(x, 2 * (q // 2) + block_yl, z, q % 2)
        return to, jnp.logical_and(dp == to[0], split == to[1])

    for k in range(3):
        landed(lx.at[k], lx_r.at[k])
    rl[...] = ls[0] + lx[0] + lx[1] + lx[2]
    for q in range(4):
        to, own = owner_of(q)
        send_when(jnp.logical_not(own), (rl, lq.at[source], (ly_s, q), ly_r.at[source], to))

        @pl.when(own)
        def _():
            lq[source] = rl[...]

    drain((i_s, t_s, d_s))
    mine = yh * 2 + core
    outs = (both_out.at[pl.ds(0, ROWS)], both_out.at[pl.ds(ROWS, ROWS)])

    def quarter_rows(q, start=0, count=QUARTER):
        return pl.ds(pl.multiple_of(q * QUARTER + start, EIGHTH), count)

    my_rows = quarter_rows(mine)
    y_up, y_down = at(x, y + 1, z, core), at(x, y + 3, z, core)

    def gather_out(kind, grad, values):
        inverse, unit = unit_rows(values)
        out = outs[kind]
        out[my_rows, :] = unit_back(unit, inverse, sharp * grad).astype(BF16)
        low, high = out.at[quarter_rows(mine, 0, EIGHTH)], out.at[quarter_rows(mine, EIGHTH, EIGHTH)]
        send(low, hop.at[kind, 0], (g_s, kind, 0), g_r.at[kind, 0], y_up)
        send(high, hop.at[kind, 1], (g_s, kind, 1), g_r.at[kind, 1], y_down)
        send(out.at[my_rows], out.at[my_rows], (g_s, kind, 2), g_r.at[kind, 2], sibling)

    def gather_on(kind):
        out = outs[kind]
        landed(hop.at[kind, 0], g_r.at[kind, 0])
        there = out.at[quarter_rows(2 * (1 - up_hi) + core, 0, EIGHTH)]
        send(hop.at[kind, 0], there, (g_s, kind, 3), g_r.at[kind, 3], y_up)
        landed(hop.at[kind, 1], g_r.at[kind, 1])
        there = out.at[quarter_rows(2 * up_hi + core, EIGHTH, EIGHTH)]
        send(hop.at[kind, 1], there, (g_s, kind, 4), g_r.at[kind, 4], y_down)

    def gather_over(kind):
        for half in (0, 1):
            here = outs[kind].at[quarter_rows((1 - yh) * 2 + core, half * EIGHTH, EIGHTH)]
            landed(here, g_r.at[kind, 3 + half])
            send(here, here, (g_s, kind, 5 + half), g_r.at[kind, 5 + half], sibling)

    def gather_end(kind):
        landed(outs[kind].at[quarter_rows(yh * 2 + other)], g_r.at[kind, 2])
        for half in (0, 1):
            here = outs[kind].at[quarter_rows((1 - yh) * 2 + other, half * EIGHTH, EIGHTH)]
            landed(here, g_r.at[kind, 5 + half])

    grads = []
    for piece in (0, 1):
        grad = text_sum(0, piece)
        for side in (0, 1):
            landed(vr.at[side, 0, piece_rows(piece)], v_r.at[side, 0, piece])
            grad = grad + vr[side, 0, piece_rows(piece), :].astype(F32)
        grads.append(grad)
    grad = jnp.concatenate(grads, axis=0)
    gather_out(1, grad, cap[pl.ds(pl.multiple_of(core * QUARTER, QUARTER), QUARTER), :])

    @on(second)
    def _():
        image_out(1, 1, y_up1)
        handed(0)
        image_out(3, 2, y_down1)

    gather_on(1)

    for k in range(4):
        here = jnp.logical_and(first, yh == k)

        @pl.when(jnp.logical_not(here))
        def _():
            landed(lq.at[k], ly_r.at[k])

    loss_out[...] = ((lq[0] + lq[1]) + (lq[2] + lq[3])) * (1.0 / PAIRS)

    landed(qr.at[1], y_r.at[1])
    landed(qr.at[2], y_r.at[2])
    grad = qr[0].astype(F32) + (qr[1].astype(F32) + qr[2].astype(F32))
    gather_out(0, grad, pic[my_rows, :])
    gather_over(1)
    drain()
    gather_on(0)
    gather_over(0)
    gather_end(1)
    gather_end(0)

    drain()
    for cond, rows, ssem in pending:

        @pl.when(cond)
        def _():
            sent(rows, ssem)


def per_device(picture_vectors, caption_vectors, sharpness_entry, offset_shift):
    dma = pltpu.SemaphoreType.DMA
    vmem = pl.BlockSpec(memory_space=pltpu.VMEM)
    smem = pl.BlockSpec(memory_space=pltpu.SMEM)
    hbm = pl.BlockSpec(memory_space=pltpu.HBM)
    both, loss = pl.pallas_call(
        kernel,
        out_shape=(
            jax.ShapeDtypeStruct((2 * ROWS, WIDTH), BF16),
            jax.ShapeDtypeStruct((8, ROWS), F32),
        ),
        in_specs=[hbm, hbm, smem, smem],
        out_specs=(vmem, vmem),
        scratch_shapes=[
            pltpu.VMEM((ROWS, WIDTH), BF16),
            pltpu.VMEM((HALF, WIDTH), BF16),
            pltpu.VMEM((4 * ROWS, WIDTH), BF16),
            pltpu.VMEM((8 * HALF, WIDTH), BF16),
            pltpu.VMEM((4 * ROWS, 8 * HALF), BF16),
            pltpu.VMEM((8 * HALF, 4 * ROWS), BF16),
            pltpu.VMEM((4 * ROWS, WIDTH), F32),
            pltpu.VMEM((8 * HALF, WIDTH), F32),
            pltpu.VMEM((4 * ROWS, HALF), F32),
            pltpu.VMEM((3, ROWS, WIDTH), BF16),
            pltpu.VMEM((ROWS, WIDTH), BF16),
            pltpu.VMEM((2, ROWS, WIDTH), BF16),
            pltpu.VMEM((ROWS, WIDTH), BF16),
            pltpu.VMEM((4, QUARTER, WIDTH), BF16),
            pltpu.VMEM((2, 4, QUARTER, WIDTH), BF16),
            pltpu.VMEM((2, 4, QUARTER, WIDTH), BF16),
            pltpu.VMEM((8, QUARTER, WIDTH), BF16),
            pltpu.VMEM((8, QUARTER, WIDTH), BF16),
            pltpu.VMEM((2, 4, QUARTER, WIDTH), BF16),
            pltpu.VMEM((2, 4, QUARTER, WIDTH), BF16),
            pltpu.VMEM((4, 8, ROWS), F32),
            pltpu.VMEM((3, 8, ROWS), F32),
            pltpu.VMEM((8, ROWS), F32),
            pltpu.VMEM((4, 8, ROWS), F32),
            pltpu.VMEM((2, 2, EIGHTH, WIDTH), BF16),
            dma((2,)),
            dma((7, 4)), dma((4, 4)),
            dma((2, 4, 2)), dma((2, 4, 2)),
            dma((8,)), dma((8,)),
            dma((4,)), dma((4,)),
            dma((2, 4)), dma((2, 4)),
            dma((4,)), dma((4,)),
            dma((2, 4)), dma((2, 4)),
            dma((4,)), dma((4,)),
            dma((3,)), dma((3,)),
            dma((8,)), dma((8,)),
            dma((2, 4, 2)), dma((2, 4, 2)),
            dma((2, 7)), dma((2, 7)),
        ],
        compiler_params=pltpu.CompilerParams(
            collective_id=0, has_side_effects=True, vmem_limit_bytes=48 * 1024 * 1024
        ),
        cost_estimate=pl.CostEstimate(flops=7_300_000_000, bytes_accessed=4_000_000, transcendentals=3_000_000),
    )(
        pltpu.with_memory_space_constraint(picture_vectors, pltpu.HBM),
        pltpu.with_memory_space_constraint(caption_vectors, pltpu.HBM),
        sharpness_entry,
        offset_shift,
    )
    return both[:ROWS].astype(F32), both[ROWS:].astype(F32), loss[0]


def solution(mesh):
    placed = (P("dp", None), P("dp", None), P(), P())
    return jax.shard_map(
        per_device,
        mesh=mesh,
        in_specs=placed,
        out_specs=(P("dp", None), P("dp", None), P("dp")),
        check_vma=False,
    )
```

```python
import jax
import jax.numpy as jnp
from jax import lax
from jax.experimental import pallas as pl
from jax.experimental.pallas import tpu as pltpu
from jax.sharding import PartitionSpec as P

MESH = pl.DeviceIdType.MESH
F32 = jnp.float32
BF16 = jnp.bfloat16

NX, NY, NZ = 4, 4, 8
ROWS, WIDTH = 256, 1152
HALF, QUARTER, EIGHTH = 128, 64, 32
PAIRS = 16384


def unit_rows(values):
    values = values.astype(F32)
    inverse = lax.rsqrt(jnp.sum(values * values, axis=1, keepdims=True) + 1e-06)
    return inverse, values * inverse


def unit_back(unit, inverse, grad):
    return (grad - unit * jnp.sum(unit * grad, axis=1, keepdims=True)) * inverse


def contract(a, b, dims):
    return lax.dot_general(a, b, (dims, ((), ())), preferred_element_type=F32)


def kernel(
    pic_hbm, cap_hbm, sharp_ref, off_ref,
    both_out, loss_out,
    pic, cap, ibuf, jbuf, cbuf, ctbuf, pacc, tacc, lacc,
    pb, xr1, x2, rb, qr, ys, yr,
    ts, tr, vs, vr,
    ls, lx, rl, lq,
    hop,
    in_sem, i_s, i_r, t_s, t_r, d_s, d_r, x1_s, x1_r, x2_s, x2_r, y_s, y_r, yc_s, yc_r,
    ly_s, ly_r, lx_s, lx_r, e_s, e_r, v_s, v_r, g_s, g_r,
):
    dp, split = lax.axis_index("dp"), lax.axis_index("split")
    x = lax.rem(dp, NX)
    yl = lax.rem(dp // NX, 2)
    z = dp // (2 * NX)
    yh, core = split // 2, lax.rem(split, 2)
    y = 2 * yh + yl
    other = 1 - core
    first = core == 0
    second = core == 1

    def at(px, py, pz, pc):
        px, py, pz = lax.rem(px, NX), lax.rem(py, NY), lax.rem(pz, NZ)
        return ((pz * 2 + lax.rem(py, 2)) * NX + px, (py // 2) * 2 + pc)

    sibling = at(x, y, z, other)
    x_up, x_down, x_far = (at(x + k, y, z, core) for k in (1, 3, 2))
    z_up, z_down = at(x, y, z + 1, core), at(x, y, z + 7, core)
    y_up1, y_down1 = at(x, y + 1, z, 1), at(x, y + 3, z, 1)

    own_text = pl.multiple_of(yh * HALF, HALF)
    fetch_text = pltpu.make_async_copy(cap_hbm.at[pl.ds(own_text, HALF)], cap, in_sem.at[0])
    fetch_image = pltpu.make_async_copy(pic_hbm, pic, in_sem.at[1])
    fetch_text.start()
    fetch_image.start()

    barrier = pltpu.get_barrier_semaphore()
    partners = [sibling, x_up, x_down, x_far, z_up, z_down]
    partners += [at(x, y + k, z, c) for k in (1, 2, 3) for c in (0, 1)]
    for partner in partners:
        pl.semaphore_signal(barrier, inc=1, device_id=partner, device_id_type=MESH)

    pending = []

    def copy(src, dst, send, recv, to):
        return pltpu.make_async_remote_copy(
            src_ref=src, dst_ref=dst, send_sem=send[0].at[send[1:]], recv_sem=recv, device_id=to, device_id_type=MESH
        )

    def note(cond, src, ssem):
        rows = 0 if src.dtype == F32 else src.shape[0] * (src.shape[1] if len(src.shape) == 3 else 1)
        pending.append((cond, rows, ssem))

    def sent(rows, ssem):
        ref = ibuf.at[pl.ds(0, rows)] if rows else ls.at[0]
        copy(ref, ref, ssem, e_r.at[0], sibling).wait_send()

    branch = [None]

    def on(cond):
        def run(body):
            branch[0] = cond
            pl.when(cond)(body)
            branch[0] = None

        return run

    def send(src, dst, ssem, rsem, to):
        copy(src, dst, ssem, rsem, to).start()
        note(branch[0], src, ssem)

    def send_when(cond, *copies):
        @pl.when(cond)
        def _():
            for one in copies:
                copy(*one).start()

        for one in copies:
            note(cond, one[0], one[2])

    def drain(of=None):
        later = [entry for entry in pending if of is not None and not any(entry[2][0] is sem for sem in of)]
        pending[:] = [entry for entry in pending if not any(entry is k for k in later)]
        for cond in (None, first, second):
            some = [entry[1:] for entry in pending if entry[0] is cond]
            if cond is None:
                for entry in some:
                    sent(*entry)
            elif some:

                @pl.when(cond)
                def _():
                    for entry in some:
                        sent(*entry)

        pending[:] = later + [entry for entry in pending if not any(entry[0] is k for k in (None, first, second))]

    def landed(dst, rsem):
        copy(dst, dst, (e_s, 0), rsem, sibling).wait_recv()


    fetch_text.wait()
    jbuf[0:HALF, :] = unit_rows(cap[...])[1].astype(BF16)
    pl.semaphore_wait(barrier, len(partners))

    def irows(slot, piece):
        return ibuf.at[pl.ds(slot * ROWS + piece * QUARTER, QUARTER)]

    def jrows(slot, c, start=0, count=QUARTER):
        return jbuf.at[pl.ds(pl.multiple_of(slot * HALF + c * QUARTER + start, EIGHTH), count)]

    def text_piece(slot, piece):
        return jrows(slot, core, piece * EIGHTH, EIGHTH)

    def text_send(side, d, piece, source, target):
        send(
            text_piece(source, piece),
            text_piece(target, piece),
            (t_s, side, d, piece),
            t_r.at[side, d, piece],
            z_down if side else z_up,
        )

    for piece in (0, 1):
        text_send(0, 0, piece, 0, 2)
        text_send(1, 0, piece, 0, 1)

    def to_y(slot, piece):
        target = y_up1 if piece < 2 else y_down1
        return (irows(slot, piece), irows(slot, piece), (i_s, 2 + slot, piece), i_r.at[slot, piece], target)

    def to_x(source, slot, piece, kind):
        target = x_up if slot == 1 or (slot == 3 and piece < 2) else x_down
        return (irows(source, piece), irows(slot, piece), (i_s, kind, piece), i_r.at[slot, piece], target)

    fetch_image.wait()

    @pl.when(first)
    def _():
        ibuf[0:ROWS, :] = unit_rows(pic[...])[1].astype(BF16)

    send_when(
        first,
        to_x(0, 1, 0, 0), to_x(0, 2, 2, 1), to_y(0, 0), to_y(0, 2),
        to_x(0, 1, 1, 0), to_x(0, 2, 3, 1), to_y(0, 1), to_y(0, 3),
        to_x(0, 1, 2, 0), to_x(0, 2, 0, 1), to_x(0, 1, 3, 0), to_x(0, 2, 1, 1),
    )

    def pass_near(up, down, onward):
        landed(irows(1, up), i_r.at[1, up])
        if onward:
            send(*to_x(1, 3, up, 6))
        send(*to_y(1, up))
        landed(irows(2, down), i_r.at[2, down])
        if onward:
            send(*to_x(2, 3, down, 6))
        send(*to_y(2, down))

    def pass_far():
        for piece in (0, 2):
            landed(irows(3, piece), i_r.at[3, piece])
            send(*to_y(3, piece))

    def images_in(slot, *pieces):
        for piece in pieces or range(4):
            landed(irows(slot, piece), i_r.at[slot, piece])

    for zeroed in (lacc,):

        def clear(n, carry):
            rows = pl.ds(pl.multiple_of(n * QUARTER, QUARTER), QUARTER)
            zeroed[rows, :] = jnp.zeros((QUARTER, zeroed.shape[1]), F32)
            return carry

        lax.fori_loop(0, 16, clear, 0)

    def swap(slot):
        send(jrows(slot, core), jrows(slot, core), (d_s, slot), d_r.at[slot], sibling)

    def swapped(*slots):
        for slot in slots:
            landed(jrows(slot, other), d_r.at[slot])

    def text_hop(d, pieces=(0, 1)):
        for piece in pieces:
            for side in (0, 1):
                if d == 4:
                    if piece == side:
                        landed(text_piece(7, piece), t_r.at[side, 3, piece])
                    continue
                here = 2 * d - side
                landed(text_piece(here, piece), t_r.at[side, d - 1, piece])
                if d < 3:
                    text_send(side, d, piece, here, here + 2)
                elif piece == side:
                    text_send(side, 3, piece, here, 7)
        if pieces[-1] == 0:
            return
        if d < 4:
            swap(2 * d - 1)
            swap(2 * d)
        else:
            swap(7)

    sharp, off = sharp_ref[0], off_ref[0]
    log2_e = 1.4426950408889634
    sharp2, off2 = sharp * log2_e, off * log2_e

    def logits_block(i, j, diagonal=False):
        ri, rj = slice(i * ROWS, (i + 1) * ROWS), slice(j * ROWS, (j + 1) * ROWS)
        logits = sharp2 * contract(ibuf[ri, :], jbuf[rj, :], ((1,), (1,))) + off2
        if diagonal:
            row = lax.broadcasted_iota(jnp.int32, (ROWS, ROWS), 0)
            col = lax.broadcasted_iota(jnp.int32, (ROWS, ROWS), 1)
            same = jnp.logical_and(row == col + yh * HALF, col < HALF)
            logits = jnp.where(same, -logits, logits)
        grown = jnp.exp2(logits)
        total = 1.0 + grown
        rough = pl.reciprocal(total, approx=True)
        inverse = rough * (2.0 - total * rough)
        coef = grown * inverse
        lost = (grown - (total - 1.0)) * inverse
        lacc[ri, :] += jnp.log(total[:, :HALF] * total[:, HALF:]) + (lost[:, :HALF] + lost[:, HALF:])
        if diagonal:
            coef = jnp.where(same, -coef, coef)
        coef = coef.astype(BF16)
        cbuf[ri, rj] = coef
        ctbuf[rj, ri] = coef.T

    def product(out, left, right, m, k0, k1):
        rows, depth = slice(m * ROWS, (m + 1) * ROWS), slice(k0 * ROWS, k1 * ROWS)
        a = left[rows, depth]
        for n in range(0, WIDTH, 256):
            columns = slice(n, min(n + 256, WIDTH))
            result = contract(a, right[depth, columns], ((1,), (0,)))
            out[rows, columns] = result if k0 == 0 else out[rows, columns] + result

    def image_product(i, j0, j1):
        product(pacc, cbuf, jbuf, i, j0, j1)

    def text_product(j, i0, i1):
        product(tacc, ctbuf, ibuf, j, i0, i1)

    up_hi = lax.rem(y + 1, NY) // 2
    turns = (
        other * 2 * (1 - yh) + core * 2 * up_hi,
        core * (2 * up_hi + 1),
        other * 2 * yh + core * 2 * (1 - up_hi),
        core * (2 * (1 - up_hi) + 1),
    )

    def hand_over(slot):
        for side, q, to in ((0, 2 * yh + 1, y_up1), (1, 2 * (1 - yh) + 1, y_down1)):
            rows = pl.ds(pl.multiple_of(slot * ROWS + q * QUARTER, QUARTER), QUARTER)
            ys[side, slot] = pacc[rows, :].astype(BF16)
            send(ys.at[side, slot], yr.at[side, slot], (yc_s, side, slot), yc_r.at[side, slot], to)

    def handed(slot):
        rows = part_rows(slot, 3)
        for side in (0, 1):
            landed(yr.at[side, slot], yc_r.at[side, slot])
        pacc[rows, :] += yr[0, slot].astype(F32) + yr[1, slot].astype(F32)

    def seat(k):
        return pl.ds(k * QUARTER, QUARTER)

    def part_rows(slot, k):
        return pl.ds(pl.multiple_of(slot * ROWS + turns[k] * QUARTER, QUARTER), QUARTER)

    def far_turn(k):
        pb[0, seat(k), :] = pacc[part_rows(3, k), :].astype(BF16)
        send(pb.at[0, seat(k)], xr1.at[seat(k)], (x1_s, k), x1_r.at[k], x_up if k < 2 else x_down)

    def near_turn(slot, k):
        side = 0 if slot == 2 else 1
        rows = pacc[part_rows(slot, k), :]
        if (k < 2) == (slot == 2):
            landed(xr1.at[seat(k)], x1_r.at[k])
            rows = rows + xr1[seat(k), :].astype(F32)
        pb[1 + side, seat(k), :] = rows.astype(BF16)
        send(
            pb.at[1 + side, seat(k)],
            x2.at[side, seat(k)],
            (x2_s, side, k),
            x2_r.at[side, k],
            x_down if side else x_up,
        )

    def text_over(low, count):
        for slot in range(low, low + count):
            mine = pl.ds(pl.multiple_of(slot * HALF + other * QUARTER, QUARTER), QUARTER)
            ts[slot] = tacc[mine, :].astype(BF16)
        slots = pl.ds(low, count)
        send(ts.at[slots], tr.at[slots], (e_s, low), e_r.at[low], sibling)

    def text_came(low, count):
        landed(tr.at[pl.ds(low, count)], e_r.at[low])

    def piece_rows(piece):
        return pl.ds(piece * EIGHTH, EIGHTH)

    def text_sum(slot, piece):
        start = slot * HALF + core * QUARTER + piece * EIGHTH
        return tacc[pl.ds(pl.multiple_of(start, EIGHTH), EIGHTH), :] + tr[slot, piece_rows(piece), :].astype(F32)

    def text_back(d, steps=(0, 1)):
        for step in steps:
            for side in (0, 1):
                piece = step if side else 1 - step
                if d == 4 and piece != side:
                    continue
                rows = text_sum(7 if d == 4 else 2 * d - 1 + side, piece)
                part = piece_rows(piece)
                if d < 3 or (d == 3 and piece == side):
                    landed(vr.at[side, d, part], v_r.at[side, d, piece])
                    rows = rows + vr[side, d, part, :].astype(F32)
                vs[side, d - 1, part, :] = rows.astype(BF16)
                send(
                    vs.at[side, d - 1, part],
                    vr.at[side, d - 1, part],
                    (v_s, side, d - 1, piece),
                    v_r.at[side, d - 1, piece],
                    z_down if side else z_up,
                )

    @on(first)
    def _():
        text_hop(1, (0,))
        pass_near(0, 2, True)
        text_hop(1, (1,))
        pass_near(1, 3, True)
        swapped(1)
        logits_block(0, 0, True)
        pass_near(2, 0, False)
        text_hop(2, (0,))
        text_hop(2, (1,))
        pass_near(3, 1, False)
        swapped(2, 3)
        logits_block(0, 1)
        pass_far()
        logits_block(1, 0)
        logits_block(2, 0)
        image_product(0, 0, 2)
        text_hop(3)
        images_in(3, 1, 3)
        logits_block(1, 1)
        logits_block(2, 1)
        image_product(1, 0, 2)
        logits_block(3, 0)
        image_product(2, 0, 2)
        logits_block(3, 1)
        swapped(4, 5)
        text_hop(4)
        text_product(0, 0, 4)
        logits_block(0, 2)
        text_product(1, 0, 4)
        logits_block(1, 2)
        image_product(3, 0, 2)
        logits_block(2, 2)
        logits_block(3, 2)
        text_product(2, 0, 4)
        text_over(0, 4)
        text_over(4, 2)
        swapped(6, 7)
        logits_block(3, 3)
        logits_block(1, 3)
        image_product(3, 2, 4)
        far_turn(0)
        far_turn(2)
        logits_block(2, 3)
        image_product(1, 2, 4)
        near_turn(1, 0)
        hand_over(3)
        hand_over(1)
        image_product(2, 2, 4)
        near_turn(2, 2)
        logits_block(0, 3)
        hand_over(2)
        text_product(3, 0, 4)
        text_over(6, 2)
        image_product(0, 2, 4)
        hand_over(0)
        text_came(6, 2)
        text_back(4)
        text_came(4, 2)
        text_back(3, (0,))

    @on(second)
    def _():
        text_hop(1)
        images_in(0)
        swapped(1)
        logits_block(0, 0)
        text_hop(2)
        swapped(2, 3)
        logits_block(0, 1)
        images_in(1, 1)
        send(*to_x(1, 3, 1, 6))
        images_in(2, 3)
        send(*to_x(2, 3, 3, 6))
        text_hop(3)
        swapped(4, 5)
        logits_block(0, 2)
        image_product(0, 0, 3)
        text_hop(4)
        images_in(1, 0, 2, 3)
        images_in(2, 0, 1, 2)
        logits_block(1, 0)
        logits_block(2, 0)
        logits_block(1, 1)
        text_product(0, 0, 3)
        logits_block(2, 1)
        logits_block(1, 2)
        text_product(1, 0, 3)
        logits_block(2, 2)
        swapped(6, 7)
        logits_block(1, 3)
        text_product(2, 0, 3)
        logits_block(2, 3)
        image_product(1, 0, 4)
        logits_block(0, 3)
        image_product(2, 0, 4)
        text_product(3, 0, 3)
        near_turn(1, 0)
        near_turn(2, 2)
        near_turn(1, 1)
        images_in(3)
        logits_block(3, 3)
        logits_block(3, 2)
        text_product(3, 3, 4)
        logits_block(3, 1)
        text_over(6, 2)
        logits_block(3, 0)
        image_product(3, 0, 4)
        far_turn(0)
        far_turn(2)
        far_turn(1)
        text_came(6, 2)
        text_back(4)
        text_product(2, 3, 4)
        text_over(4, 2)
        text_product(1, 3, 4)
        text_product(0, 3, 4)
        text_over(0, 4)
        handed(3)
        far_turn(3)
        text_came(4, 2)
        text_back(3, (0,))
        handed(2)
        near_turn(2, 3)
        image_product(0, 3, 4)

    near_turn(2, 0)
    near_turn(1, 2)
    text_back(3, (1,))

    ones = jnp.ones((8, HALF), F32)
    for i in range(4):
        ls[i] = lax.dot_general(
            ones,
            lacc[i * ROWS : (i + 1) * ROWS, :],
            (((1,), (1,)), ((), ())),
            precision=lax.Precision.HIGHEST,
            preferred_element_type=F32,
        )
    send(ls.at[2], lx.at[0], (lx_s, 0), lx_r.at[0], x_up)
    send(ls.at[1], lx.at[1], (lx_s, 1), lx_r.at[1], x_down)
    send(ls.at[3], lx.at[2], (lx_s, 2), lx_r.at[2], x_far)

    text_came(0, 4)
    text_back(2, (0,))

    @on(second)
    def _():
        near_turn(2, 1)
        handed(1)
        near_turn(1, 3)

    text_back(2, (1,))
    text_back(1, (0,))

    y_up0, y_down0 = at(x, y + 1, z, 0), at(x, y + 3, z, 0)

    def image_sum(k):
        landed(x2.at[0, seat(k)], x2_r.at[0, k])
        landed(x2.at[1, seat(k)], x2_r.at[1, k])
        return pacc[part_rows(0, k), :] + (x2[0, seat(k), :].astype(F32) + x2[1, seat(k), :].astype(F32))

    def image_out(k, box, to):
        total = image_sum(k)
        if core_of[0] == 1 and k == 0:
            landed(qr.at[3], y_r.at[3])
            total = total + qr[3].astype(F32)
        rb[seat(k), :] = total.astype(BF16)
        send(rb.at[seat(k)], qr.at[box], (y_s, k), y_r.at[box], to)

    core_of = [0]

    @on(first)
    def _():
        image_out(0, 3, y_up1)

    core_of[0] = 1

    @on(second)
    def _():
        image_out(2, 2, y_down0)

    text_back(1, (1,))

    @on(first)
    def _():
        qr[0] = image_sum(2).astype(BF16)

    @on(second)
    def _():
        qr[0] = jnp.zeros((QUARTER, WIDTH), BF16)
        image_out(0, 1, y_up0)

    source = yh + 2 * core
    block_yl = lax.rem(yl + core, 2)

    def owner_of(q):
        to = at(x, 2 * (q // 2) + block_yl, z, q % 2)
        return to, jnp.logical_and(dp == to[0], split == to[1])

    for k in range(3):
        landed(lx.at[k], lx_r.at[k])
    rl[...] = ls[0] + lx[0] + lx[1] + lx[2]
    for q in range(4):
        to, own = owner_of(q)
        send_when(jnp.logical_not(own), (rl, lq.at[source], (ly_s, q), ly_r.at[source], to))

        @pl.when(own)
        def _():
            lq[source] = rl[...]

    drain((i_s, t_s, d_s))
    mine = yh * 2 + core
    outs = (both_out.at[pl.ds(0, ROWS)], both_out.at[pl.ds(ROWS, ROWS)])

    def quarter_rows(q, start=0, count=QUARTER):
        return pl.ds(pl.multiple_of(q * QUARTER + start, EIGHTH), count)

    my_rows = quarter_rows(mine)
    y_up, y_down = at(x, y + 1, z, core), at(x, y + 3, z, core)

    def gather_out(kind, grad, values):
        inverse, unit = unit_rows(values)
        out = outs[kind]
        out[my_rows, :] = unit_back(unit, inverse, sharp * grad).astype(BF16)
        low, high = out.at[quarter_rows(mine, 0, EIGHTH)], out.at[quarter_rows(mine, EIGHTH, EIGHTH)]
        send(low, hop.at[kind, 0], (g_s, kind, 0), g_r.at[kind, 0], y_up)
        send(high, hop.at[kind, 1], (g_s, kind, 1), g_r.at[kind, 1], y_down)
        send(out.at[my_rows], out.at[my_rows], (g_s, kind, 2), g_r.at[kind, 2], sibling)

    def gather_on(kind):
        out = outs[kind]
        landed(hop.at[kind, 0], g_r.at[kind, 0])
        there = out.at[quarter_rows(2 * (1 - up_hi) + core, 0, EIGHTH)]
        send(hop.at[kind, 0], there, (g_s, kind, 3), g_r.at[kind, 3], y_up)
        landed(hop.at[kind, 1], g_r.at[kind, 1])
        there = out.at[quarter_rows(2 * up_hi + core, EIGHTH, EIGHTH)]
        send(hop.at[kind, 1], there, (g_s, kind, 4), g_r.at[kind, 4], y_down)

    def gather_over(kind):
        for half in (0, 1):
            here = outs[kind].at[quarter_rows((1 - yh) * 2 + core, half * EIGHTH, EIGHTH)]
            landed(here, g_r.at[kind, 3 + half])
            send(here, here, (g_s, kind, 5 + half), g_r.at[kind, 5 + half], sibling)

    def gather_end(kind):
        landed(outs[kind].at[quarter_rows(yh * 2 + other)], g_r.at[kind, 2])
        for half in (0, 1):
            here = outs[kind].at[quarter_rows((1 - yh) * 2 + other, half * EIGHTH, EIGHTH)]
            landed(here, g_r.at[kind, 5 + half])

    grads = []
    for piece in (0, 1):
        grad = text_sum(0, piece)
        for side in (0, 1):
            landed(vr.at[side, 0, piece_rows(piece)], v_r.at[side, 0, piece])
            grad = grad + vr[side, 0, piece_rows(piece), :].astype(F32)
        grads.append(grad)
    grad = jnp.concatenate(grads, axis=0)
    gather_out(1, grad, cap[pl.ds(pl.multiple_of(core * QUARTER, QUARTER), QUARTER), :])

    @on(second)
    def _():
        image_out(1, 1, y_up1)
        handed(0)
        image_out(3, 2, y_down1)

    gather_on(1)

    for k in range(4):
        here = jnp.logical_and(first, yh == k)

        @pl.when(jnp.logical_not(here))
        def _():
            landed(lq.at[k], ly_r.at[k])

    loss_out[...] = ((lq[0] + lq[1]) + (lq[2] + lq[3])) * (1.0 / PAIRS)

    landed(qr.at[1], y_r.at[1])
    landed(qr.at[2], y_r.at[2])
    grad = qr[0].astype(F32) + (qr[1].astype(F32) + qr[2].astype(F32))
    gather_out(0, grad, pic[my_rows, :])
    gather_over(1)
    drain()
    gather_on(0)
    gather_over(0)
    gather_end(1)
    gather_end(0)

    drain()
    for cond, rows, ssem in pending:

        @pl.when(cond)
        def _():
            sent(rows, ssem)


def per_device(picture_vectors, caption_vectors, sharpness_entry, offset_shift):
    dma = pltpu.SemaphoreType.DMA
    vmem = pl.BlockSpec(memory_space=pltpu.VMEM)
    smem = pl.BlockSpec(memory_space=pltpu.SMEM)
    hbm = pl.BlockSpec(memory_space=pltpu.HBM)
    both, loss = pl.pallas_call(
        kernel,
        out_shape=(
            jax.ShapeDtypeStruct((2 * ROWS, WIDTH), BF16),
            jax.ShapeDtypeStruct((8, ROWS), F32),
        ),
        in_specs=[hbm, hbm, smem, smem],
        out_specs=(vmem, vmem),
        scratch_shapes=[
            pltpu.VMEM((ROWS, WIDTH), BF16),
            pltpu.VMEM((HALF, WIDTH), BF16),
            pltpu.VMEM((4 * ROWS, WIDTH), BF16),
            pltpu.VMEM((8 * HALF, WIDTH), BF16),
            pltpu.VMEM((4 * ROWS, 8 * HALF), BF16),
            pltpu.VMEM((8 * HALF, 4 * ROWS), BF16),
            pltpu.VMEM((4 * ROWS, WIDTH), F32),
            pltpu.VMEM((8 * HALF, WIDTH), F32),
            pltpu.VMEM((4 * ROWS, HALF), F32),
            pltpu.VMEM((3, ROWS, WIDTH), BF16),
            pltpu.VMEM((ROWS, WIDTH), BF16),
            pltpu.VMEM((2, ROWS, WIDTH), BF16),
            pltpu.VMEM((ROWS, WIDTH), BF16),
            pltpu.VMEM((4, QUARTER, WIDTH), BF16),
            pltpu.VMEM((2, 4, QUARTER, WIDTH), BF16),
            pltpu.VMEM((2, 4, QUARTER, WIDTH), BF16),
            pltpu.VMEM((8, QUARTER, WIDTH), BF16),
            pltpu.VMEM((8, QUARTER, WIDTH), BF16),
            pltpu.VMEM((2, 4, QUARTER, WIDTH), BF16),
            pltpu.VMEM((2, 4, QUARTER, WIDTH), BF16),
            pltpu.VMEM((4, 8, ROWS), F32),
            pltpu.VMEM((3, 8, ROWS), F32),
            pltpu.VMEM((8, ROWS), F32),
            pltpu.VMEM((4, 8, ROWS), F32),
            pltpu.VMEM((2, 2, EIGHTH, WIDTH), BF16),
            dma((2,)),
            dma((7, 4)), dma((4, 4)),
            dma((2, 4, 2)), dma((2, 4, 2)),
            dma((8,)), dma((8,)),
            dma((4,)), dma((4,)),
            dma((2, 4)), dma((2, 4)),
            dma((4,)), dma((4,)),
            dma((2, 4)), dma((2, 4)),
            dma((4,)), dma((4,)),
            dma((3,)), dma((3,)),
            dma((8,)), dma((8,)),
            dma((2, 4, 2)), dma((2, 4, 2)),
            dma((2, 7)), dma((2, 7)),
        ],
        compiler_params=pltpu.CompilerParams(
            collective_id=0, has_side_effects=True, vmem_limit_bytes=48 * 1024 * 1024
        ),
        cost_estimate=pl.CostEstimate(flops=7_300_000_000, bytes_accessed=4_000_000, transcendentals=3_000_000),
    )(
        pltpu.with_memory_space_constraint(picture_vectors, pltpu.HBM),
        pltpu.with_memory_space_constraint(caption_vectors, pltpu.HBM),
        sharpness_entry,
        offset_shift,
    )
    return both[:ROWS].astype(F32), both[ROWS:].astype(F32), loss[0]


def solution(mesh):
    placed = (P("dp", None), P("dp", None), P(), P())
    return jax.shard_map(
        per_device,
        mesh=mesh,
        in_specs=placed,
        out_specs=(P("dp", None), P("dp", None), P("dp")),
        check_vma=False,
    )
```

```python
import jax
import jax.numpy as jnp
from jax import lax
from jax.experimental import pallas as pl
from jax.experimental.pallas import tpu as pltpu
from jax.sharding import PartitionSpec as P

MESH = pl.DeviceIdType.MESH
F32 = jnp.float32
BF16 = jnp.bfloat16

NX, NY, NZ = 4, 4, 8
ROWS, WIDTH = 256, 1152
HALF, QUARTER, EIGHTH, PIECE = 128, 64, 32, 16
PAIRS = 16384


def unit_rows(values):
    values = values.astype(F32)
    inverse = lax.rsqrt(jnp.sum(values * values, axis=1, keepdims=True) + 1e-06)
    return inverse, values * inverse


def unit_back(unit, inverse, grad):
    return (grad - unit * jnp.sum(unit * grad, axis=1, keepdims=True)) * inverse


def contract(a, b, dims):
    return lax.dot_general(a, b, (dims, ((), ())), preferred_element_type=F32)


def kernel(
    pic_hbm, cap_hbm, sharp_ref, off_ref,
    both_out, loss_out,
    pic, cap, ibuf, jbuf, cbuf, ctbuf, pacc, tacc, lacc,
    pb, xr1, x2, rb, qr, ys, yr,
    ts, tr, vs, vr,
    ls, lx, rl, lq,
    hop,
    in_sem, i_s, i_r, t_s, t_r, d_s, d_r, x1_s, x1_r, x2_s, x2_r, y_s, y_r, yc_s, yc_r,
    ly_s, ly_r, lx_s, lx_r, e_s, e_r, v_s, v_r, g_s, g_r,
):
    dp, split = lax.axis_index("dp"), lax.axis_index("split")
    x = lax.rem(dp, NX)
    yl = lax.rem(dp // NX, 2)
    z = dp // (2 * NX)
    yh, core = split // 2, lax.rem(split, 2)
    y = 2 * yh + yl
    other = 1 - core
    first = core == 0
    second = core == 1

    def at(px, py, pz, pc):
        px, py, pz = lax.rem(px, NX), lax.rem(py, NY), lax.rem(pz, NZ)
        return ((pz * 2 + lax.rem(py, 2)) * NX + px, (py // 2) * 2 + pc)

    sibling = at(x, y, z, other)
    x_up, x_down, x_far = (at(x + k, y, z, core) for k in (1, 3, 2))
    z_up, z_down = at(x, y, z + 1, core), at(x, y, z + 7, core)
    y_up1, y_down1 = at(x, y + 1, z, 1), at(x, y + 3, z, 1)

    own_text = pl.multiple_of(yh * HALF, HALF)
    fetch_text = pltpu.make_async_copy(cap_hbm.at[pl.ds(own_text, HALF)], cap, in_sem.at[0])
    fetch_image = pltpu.make_async_copy(pic_hbm, pic, in_sem.at[1])
    fetch_text.start()
    fetch_image.start()

    barrier = pltpu.get_barrier_semaphore()
    partners = [sibling, x_up, x_down, x_far, z_up, z_down]
    partners += [at(x, y + k, z, c) for k in (1, 2, 3) for c in (0, 1)]
    for partner in partners:
        pl.semaphore_signal(barrier, inc=1, device_id=partner, device_id_type=MESH)

    pending = []

    def copy(src, dst, send, recv, to):
        return pltpu.make_async_remote_copy(
            src_ref=src, dst_ref=dst, send_sem=send[0].at[send[1:]], recv_sem=recv, device_id=to, device_id_type=MESH
        )

    def note(cond, src, ssem):
        rows = 0 if src.dtype == F32 else src.shape[0] * (src.shape[1] if len(src.shape) == 3 else 1)
        pending.append((cond, rows, ssem))

    def sent(rows, ssem):
        ref = ibuf.at[pl.ds(0, rows)] if rows else ls.at[0]
        copy(ref, ref, ssem, e_r.at[0], sibling).wait_send()

    branch = [None]

    def on(cond):
        def run(body):
            branch[0] = cond
            pl.when(cond)(body)
            branch[0] = None

        return run

    def send(src, dst, ssem, rsem, to):
        copy(src, dst, ssem, rsem, to).start()
        note(branch[0], src, ssem)

    def send_when(cond, *copies):
        @pl.when(cond)
        def _():
            for one in copies:
                copy(*one).start()

        for one in copies:
            note(cond, one[0], one[2])

    def drain(of=None):
        later = [entry for entry in pending if of is not None and not any(entry[2][0] is sem for sem in of)]
        pending[:] = [entry for entry in pending if not any(entry is k for k in later)]
        for cond in (None, first, second):
            some = [entry[1:] for entry in pending if entry[0] is cond]
            if cond is None:
                for entry in some:
                    sent(*entry)
            elif some:

                @pl.when(cond)
                def _():
                    for entry in some:
                        sent(*entry)

        pending[:] = later + [entry for entry in pending if not any(entry[0] is k for k in (None, first, second))]

    def landed(dst, rsem):
        copy(dst, dst, (e_s, 0), rsem, sibling).wait_recv()


    fetch_text.wait()
    jbuf[0:HALF, :] = unit_rows(cap[...])[1].astype(BF16)
    pl.semaphore_wait(barrier, len(partners))

    def irows(slot, piece):
        return ibuf.at[pl.ds(slot * ROWS + piece * QUARTER, QUARTER)]

    def jrows(slot, c, start=0, count=QUARTER):
        return jbuf.at[pl.ds(pl.multiple_of(slot * HALF + c * QUARTER + start, PIECE), count)]

    def text_piece(slot, piece):
        return jrows(slot, core, piece * PIECE, PIECE)

    def text_send(side, d, piece, source, target):
        send(
            text_piece(source, piece),
            text_piece(target, piece),
            (t_s, side, d, piece),
            t_r.at[side, d, piece],
            z_down if side else z_up,
        )

    for piece in range(4):
        text_send(0, 0, piece, 0, 2)
        text_send(1, 0, piece, 0, 1)

    def to_y(slot, piece):
        target = y_up1 if piece < 2 else y_down1
        return (irows(slot, piece), irows(slot, piece), (i_s, 2 + slot, piece), i_r.at[slot, piece], target)

    def to_x(source, slot, piece, kind):
        target = x_up if slot == 1 or (slot == 3 and piece < 2) else x_down
        return (irows(source, piece), irows(slot, piece), (i_s, kind, piece), i_r.at[slot, piece], target)

    fetch_image.wait()

    @pl.when(first)
    def _():
        ibuf[0:ROWS, :] = unit_rows(pic[...])[1].astype(BF16)

    send_when(
        first,
        to_x(0, 1, 0, 0), to_x(0, 2, 2, 1), to_y(0, 0), to_y(0, 2),
        to_x(0, 1, 1, 0), to_x(0, 2, 3, 1), to_y(0, 1), to_y(0, 3),
        to_x(0, 1, 2, 0), to_x(0, 2, 0, 1), to_x(0, 1, 3, 0), to_x(0, 2, 1, 1),
    )

    def pass_near(up, down, onward):
        landed(irows(1, up), i_r.at[1, up])
        if onward:
            send(*to_x(1, 3, up, 6))
        send(*to_y(1, up))
        landed(irows(2, down), i_r.at[2, down])
        if onward:
            send(*to_x(2, 3, down, 6))
        send(*to_y(2, down))

    def pass_far(*pieces):
        for piece in pieces:
            landed(irows(3, piece), i_r.at[3, piece])
            send(*to_y(3, piece))

    def images_in(*slots):
        for slot in slots:
            for piece in range(4):
                landed(irows(slot, piece), i_r.at[slot, piece])

    for zeroed in (lacc,):

        def clear(n, carry):
            rows = pl.ds(pl.multiple_of(n * QUARTER, QUARTER), QUARTER)
            zeroed[rows, :] = jnp.zeros((QUARTER, zeroed.shape[1]), F32)
            return carry

        lax.fori_loop(0, 16, clear, 0)

    def swap(slot):
        send(jrows(slot, core), jrows(slot, core), (d_s, slot), d_r.at[slot], sibling)

    def swapped(*slots):
        for slot in slots:
            landed(jrows(slot, other), d_r.at[slot])

    def text_hop(d, pieces=(0, 1, 2, 3)):
        for piece in pieces:
            for side in (0, 1):
                if d == 4:
                    if piece // 2 == side:
                        landed(text_piece(7, piece), t_r.at[side, 3, piece])
                    continue
                here = 2 * d - side
                landed(text_piece(here, piece), t_r.at[side, d - 1, piece])
                if d < 3:
                    text_send(side, d, piece, here, here + 2)
                elif piece // 2 == side:
                    text_send(side, 3, piece, here, 7)
        if pieces[-1] != 3:
            return
        if d < 4:
            swap(2 * d - 1)
            swap(2 * d)
        else:
            swap(7)

    sharp, off = sharp_ref[0], off_ref[0]
    log2_e = 1.4426950408889634
    sharp2, off2 = sharp * log2_e, off * log2_e

    def logits_block(i, j, diagonal=False):
        ri, rj = slice(i * ROWS, (i + 1) * ROWS), slice(j * ROWS, (j + 1) * ROWS)
        logits = sharp2 * contract(ibuf[ri, :], jbuf[rj, :], ((1,), (1,))) + off2
        if diagonal:
            row = lax.broadcasted_iota(jnp.int32, (ROWS, ROWS), 0)
            col = lax.broadcasted_iota(jnp.int32, (ROWS, ROWS), 1)
            same = jnp.logical_and(row == col + yh * HALF, col < HALF)
            logits = jnp.where(same, -logits, logits)
        grown = jnp.exp2(logits)
        total = 1.0 + grown
        rough = pl.reciprocal(total, approx=True)
        inverse = rough * (2.0 - total * rough)
        coef = grown * inverse
        lost = (grown - (total - 1.0)) * inverse
        lacc[ri, :] += jnp.log(total[:, :HALF] * total[:, HALF:]) + (lost[:, :HALF] + lost[:, HALF:])
        if diagonal:
            coef = jnp.where(same, -coef, coef)
        coef = coef.astype(BF16)
        cbuf[ri, rj] = coef
        ctbuf[rj, ri] = coef.T

    def product(out, left, right, m, k0, k1):
        rows, depth = slice(m * ROWS, (m + 1) * ROWS), slice(k0 * ROWS, k1 * ROWS)
        a = left[rows, depth]
        for n in range(0, WIDTH, 256):
            columns = slice(n, min(n + 256, WIDTH))
            result = contract(a, right[depth, columns], ((1,), (0,)))
            out[rows, columns] = result if k0 == 0 else out[rows, columns] + result

    def image_product(i, j0, j1):
        product(pacc, cbuf, jbuf, i, j0, j1)

    def text_product(j, i0, i1):
        product(tacc, ctbuf, ibuf, j, i0, i1)

    up_hi = lax.rem(y + 1, NY) // 2
    turns = (
        other * 2 * (1 - yh) + core * 2 * up_hi,
        core * (2 * up_hi + 1),
        other * 2 * yh + core * 2 * (1 - up_hi),
        core * (2 * (1 - up_hi) + 1),
    )

    def hand_over(slot):
        for side, q, to in ((0, 2 * yh + 1, y_up1), (1, 2 * (1 - yh) + 1, y_down1)):
            rows = pl.ds(pl.multiple_of(slot * ROWS + q * QUARTER, QUARTER), QUARTER)
            ys[side, slot] = pacc[rows, :].astype(BF16)
            send(ys.at[side, slot], yr.at[side, slot], (yc_s, side, slot), yc_r.at[side, slot], to)

    def handed(slot):
        rows = part_rows(slot, 3)
        for side in (0, 1):
            landed(yr.at[side, slot], yc_r.at[side, slot])
        pacc[rows, :] += yr[0, slot].astype(F32) + yr[1, slot].astype(F32)

    def seat(k):
        return pl.ds(k * QUARTER, QUARTER)

    def part_rows(slot, k):
        return pl.ds(pl.multiple_of(slot * ROWS + turns[k] * QUARTER, QUARTER), QUARTER)

    def far_turn(k):
        pb[0, seat(k), :] = pacc[part_rows(3, k), :].astype(BF16)
        send(pb.at[0, seat(k)], xr1.at[seat(k)], (x1_s, k), x1_r.at[k], x_up if k < 2 else x_down)

    def near_turn(slot, k):
        side = 0 if slot == 2 else 1
        rows = pacc[part_rows(slot, k), :]
        if (k < 2) == (slot == 2):
            landed(xr1.at[seat(k)], x1_r.at[k])
            rows = rows + xr1[seat(k), :].astype(F32)
        pb[1 + side, seat(k), :] = rows.astype(BF16)
        send(
            pb.at[1 + side, seat(k)],
            x2.at[side, seat(k)],
            (x2_s, side, k),
            x2_r.at[side, k],
            x_down if side else x_up,
        )

    def text_over(low, count):
        for slot in range(low, low + count):
            mine = pl.ds(pl.multiple_of(slot * HALF + other * QUARTER, QUARTER), QUARTER)
            ts[slot] = tacc[mine, :].astype(BF16)
        slots = pl.ds(low, count)
        send(ts.at[slots], tr.at[slots], (e_s, low), e_r.at[low], sibling)

    def text_came(low, count):
        landed(tr.at[pl.ds(low, count)], e_r.at[low])

    def piece_rows(piece):
        return pl.ds(piece * PIECE, PIECE)

    def text_sum(slot, piece):
        start = slot * HALF + core * QUARTER + piece * PIECE
        return tacc[pl.ds(pl.multiple_of(start, PIECE), PIECE), :] + tr[slot, piece_rows(piece), :].astype(F32)

    def text_back(d, steps=(0, 1, 2, 3)):
        for step in steps:
            for side in (0, 1):
                piece = step if side else (step + 2) % 4
                if d == 4 and step < 2:
                    continue
                rows = text_sum(7 if d == 4 else 2 * d - 1 + side, piece)
                part = piece_rows(piece)
                if d < 3 or (d == 3 and step >= 2):
                    landed(vr.at[side, d, part], v_r.at[side, d, piece])
                    rows = rows + vr[side, d, part, :].astype(F32)
                vs[side, d - 1, part, :] = rows.astype(BF16)
                send(
                    vs.at[side, d - 1, part],
                    vr.at[side, d - 1, part],
                    (v_s, side, d - 1, piece),
                    v_r.at[side, d - 1, piece],
                    z_down if side else z_up,
                )

    @on(first)
    def _():
        text_hop(1, (0, 1))
        pass_near(0, 2, True)
        text_hop(1, (2, 3))
        pass_near(1, 3, True)
        swapped(1)
        logits_block(0, 0, True)
        pass_near(2, 0, False)
        text_hop(2)
        pass_near(3, 1, False)
        swapped(2, 3)
        logits_block(0, 1)
        pass_far(0, 2)
        logits_block(1, 0)
        logits_block(2, 0)
        image_product(0, 0, 2)
        text_hop(3)
        pass_far(1, 3)
        logits_block(1, 1)
        logits_block(2, 1)
        image_product(1, 0, 2)
        logits_block(3, 0)
        image_product(2, 0, 2)
        logits_block(3, 1)
        swapped(4, 5)
        text_hop(4)
        text_product(0, 0, 4)
        logits_block(0, 2)
        text_product(1, 0, 4)
        logits_block(1, 2)
        image_product(3, 0, 2)
        logits_block(2, 2)
        logits_block(3, 2)
        text_product(2, 0, 4)
        text_over(0, 4)
        text_over(4, 2)
        swapped(6, 7)
        logits_block(3, 3)
        logits_block(1, 3)
        image_product(3, 2, 4)
        far_turn(0)
        far_turn(2)
        hand_over(3)
        logits_block(2, 3)
        logits_block(0, 3)
        text_product(3, 0, 4)
        text_over(6, 2)
        image_product(1, 2, 4)
        near_turn(1, 0)
        hand_over(1)
        image_product(2, 2, 4)
        near_turn(2, 2)
        hand_over(2)
        image_product(0, 2, 4)
        hand_over(0)
        text_came(6, 2)
        text_back(4)
        text_came(4, 2)
        text_back(3, (0, 1))

    @on(second)
    def _():
        text_hop(1)
        images_in(0)
        swapped(1)
        logits_block(0, 0)
        text_hop(2)
        swapped(2, 3)
        logits_block(0, 1)
        text_hop(3)
        swapped(4, 5)
        logits_block(0, 2)
        image_product(0, 0, 3)
        text_hop(4)
        images_in(1, 2)
        logits_block(1, 0)
        logits_block(2, 0)
        logits_block(1, 1)
        text_product(0, 0, 3)
        logits_block(2, 1)
        logits_block(1, 2)
        text_product(1, 0, 3)
        logits_block(2, 2)
        swapped(6, 7)
        logits_block(1, 3)
        text_product(2, 0, 3)
        logits_block(2, 3)
        image_product(1, 0, 4)
        logits_block(0, 3)
        image_product(2, 0, 4)
        text_product(3, 0, 3)
        near_turn(1, 0)
        near_turn(2, 2)
        near_turn(1, 1)
        images_in(3)
        logits_block(3, 3)
        logits_block(3, 2)
        text_product(3, 3, 4)
        logits_block(3, 1)
        text_over(6, 2)
        logits_block(3, 0)
        image_product(3, 0, 4)
        far_turn(0)
        far_turn(2)
        far_turn(1)
        text_came(6, 2)
        text_back(4)
        text_product(2, 3, 4)
        text_over(4, 2)
        text_product(1, 3, 4)
        text_product(0, 3, 4)
        text_over(0, 4)
        handed(3)
        far_turn(3)
        text_came(4, 2)
        text_back(3, (0, 1))
        handed(2)
        near_turn(2, 3)
        image_product(0, 3, 4)

    near_turn(2, 0)
    near_turn(1, 2)
    text_back(3, (2, 3))

    ones = jnp.ones((8, HALF), F32)
    for i in range(4):
        ls[i] = lax.dot_general(
            ones,
            lacc[i * ROWS : (i + 1) * ROWS, :],
            (((1,), (1,)), ((), ())),
            precision=lax.Precision.HIGHEST,
            preferred_element_type=F32,
        )
    send(ls.at[2], lx.at[0], (lx_s, 0), lx_r.at[0], x_up)
    send(ls.at[1], lx.at[1], (lx_s, 1), lx_r.at[1], x_down)
    send(ls.at[3], lx.at[2], (lx_s, 2), lx_r.at[2], x_far)

    text_came(0, 4)
    text_back(2, (0, 1))

    @on(second)
    def _():
        near_turn(2, 1)
        handed(1)
        near_turn(1, 3)

    text_back(2, (2, 3))
    text_back(1, (0, 1))

    y_up0, y_down0 = at(x, y + 1, z, 0), at(x, y + 3, z, 0)

    def image_sum(k):
        landed(x2.at[0, seat(k)], x2_r.at[0, k])
        landed(x2.at[1, seat(k)], x2_r.at[1, k])
        return pacc[part_rows(0, k), :] + (x2[0, seat(k), :].astype(F32) + x2[1, seat(k), :].astype(F32))

    def image_out(k, box, to):
        total = image_sum(k)
        if core_of[0] == 1 and k == 0:
            landed(qr.at[3], y_r.at[3])
            total = total + qr[3].astype(F32)
        rb[seat(k), :] = total.astype(BF16)
        send(rb.at[seat(k)], qr.at[box], (y_s, k), y_r.at[box], to)

    core_of = [0]

    @on(first)
    def _():
        image_out(0, 3, y_up1)

    core_of[0] = 1

    @on(second)
    def _():
        image_out(2, 2, y_down0)

    text_back(1, (2, 3))

    @on(first)
    def _():
        qr[0] = image_sum(2).astype(BF16)

    @on(second)
    def _():
        qr[0] = jnp.zeros((QUARTER, WIDTH), BF16)
        image_out(0, 1, y_up0)

    source = yh + 2 * core
    block_yl = lax.rem(yl + core, 2)

    def owner_of(q):
        to = at(x, 2 * (q // 2) + block_yl, z, q % 2)
        return to, jnp.logical_and(dp == to[0], split == to[1])

    for k in range(3):
        landed(lx.at[k], lx_r.at[k])
    rl[...] = ls[0] + lx[0] + lx[1] + lx[2]
    for q in range(4):
        to, own = owner_of(q)
        send_when(jnp.logical_not(own), (rl, lq.at[source], (ly_s, q), ly_r.at[source], to))

        @pl.when(own)
        def _():
            lq[source] = rl[...]

    drain((i_s, t_s, d_s))
    mine = yh * 2 + core
    outs = (both_out.at[pl.ds(0, ROWS)], both_out.at[pl.ds(ROWS, ROWS)])

    def quarter_rows(q, start=0, count=QUARTER):
        return pl.ds(pl.multiple_of(q * QUARTER + start, EIGHTH), count)

    my_rows = quarter_rows(mine)
    y_up, y_down = at(x, y + 1, z, core), at(x, y + 3, z, core)

    def gather_out(kind, grad, values):
        inverse, unit = unit_rows(values)
        out = outs[kind]
        out[my_rows, :] = unit_back(unit, inverse, sharp * grad).astype(BF16)
        low, high = out.at[quarter_rows(mine, 0, EIGHTH)], out.at[quarter_rows(mine, EIGHTH, EIGHTH)]
        send(low, hop.at[kind, 0], (g_s, kind, 0), g_r.at[kind, 0], y_up)
        send(high, hop.at[kind, 1], (g_s, kind, 1), g_r.at[kind, 1], y_down)
        send(out.at[my_rows], out.at[my_rows], (g_s, kind, 2), g_r.at[kind, 2], sibling)

    def gather_on(kind):
        out = outs[kind]
        landed(hop.at[kind, 0], g_r.at[kind, 0])
        there = out.at[quarter_rows(2 * (1 - up_hi) + core, 0, EIGHTH)]
        send(hop.at[kind, 0], there, (g_s, kind, 3), g_r.at[kind, 3], y_up)
        landed(hop.at[kind, 1], g_r.at[kind, 1])
        there = out.at[quarter_rows(2 * up_hi + core, EIGHTH, EIGHTH)]
        send(hop.at[kind, 1], there, (g_s, kind, 4), g_r.at[kind, 4], y_down)

    def gather_over(kind):
        for half in (0, 1):
            here = outs[kind].at[quarter_rows((1 - yh) * 2 + core, half * EIGHTH, EIGHTH)]
            landed(here, g_r.at[kind, 3 + half])
            send(here, here, (g_s, kind, 5 + half), g_r.at[kind, 5 + half], sibling)

    def gather_end(kind):
        landed(outs[kind].at[quarter_rows(yh * 2 + other)], g_r.at[kind, 2])
        for half in (0, 1):
            here = outs[kind].at[quarter_rows((1 - yh) * 2 + other, half * EIGHTH, EIGHTH)]
            landed(here, g_r.at[kind, 5 + half])

    grads = []
    for piece in range(4):
        grad = text_sum(0, piece)
        for side in (0, 1):
            landed(vr.at[side, 0, piece_rows(piece)], v_r.at[side, 0, piece])
            grad = grad + vr[side, 0, piece_rows(piece), :].astype(F32)
        grads.append(grad)
    grad = jnp.concatenate(grads, axis=0)
    gather_out(1, grad, cap[pl.ds(pl.multiple_of(core * QUARTER, QUARTER), QUARTER), :])

    @on(second)
    def _():
        image_out(1, 1, y_up1)
        handed(0)
        image_out(3, 2, y_down1)

    gather_on(1)

    for k in range(4):
        here = jnp.logical_and(first, yh == k)

        @pl.when(jnp.logical_not(here))
        def _():
            landed(lq.at[k], ly_r.at[k])

    loss_out[...] = ((lq[0] + lq[1]) + (lq[2] + lq[3])) * (1.0 / PAIRS)

    landed(qr.at[1], y_r.at[1])
    landed(qr.at[2], y_r.at[2])
    grad = qr[0].astype(F32) + (qr[1].astype(F32) + qr[2].astype(F32))
    gather_out(0, grad, pic[my_rows, :])
    gather_over(1)
    drain()
    gather_on(0)
    gather_over(0)
    gather_end(1)
    gather_end(0)

    drain()
    for cond, rows, ssem in pending:

        @pl.when(cond)
        def _():
            sent(rows, ssem)


def per_device(picture_vectors, caption_vectors, sharpness_entry, offset_shift):
    dma = pltpu.SemaphoreType.DMA
    vmem = pl.BlockSpec(memory_space=pltpu.VMEM)
    smem = pl.BlockSpec(memory_space=pltpu.SMEM)
    hbm = pl.BlockSpec(memory_space=pltpu.HBM)
    both, loss = pl.pallas_call(
        kernel,
        out_shape=(
            jax.ShapeDtypeStruct((2 * ROWS, WIDTH), BF16),
            jax.ShapeDtypeStruct((8, ROWS), F32),
        ),
        in_specs=[hbm, hbm, smem, smem],
        out_specs=(vmem, vmem),
        scratch_shapes=[
            pltpu.VMEM((ROWS, WIDTH), BF16),
            pltpu.VMEM((HALF, WIDTH), BF16),
            pltpu.VMEM((4 * ROWS, WIDTH), BF16),
            pltpu.VMEM((8 * HALF, WIDTH), BF16),
            pltpu.VMEM((4 * ROWS, 8 * HALF), BF16),
            pltpu.VMEM((8 * HALF, 4 * ROWS), BF16),
            pltpu.VMEM((4 * ROWS, WIDTH), F32),
            pltpu.VMEM((8 * HALF, WIDTH), F32),
            pltpu.VMEM((4 * ROWS, HALF), F32),
            pltpu.VMEM((3, ROWS, WIDTH), BF16),
            pltpu.VMEM((ROWS, WIDTH), BF16),
            pltpu.VMEM((2, ROWS, WIDTH), BF16),
            pltpu.VMEM((ROWS, WIDTH), BF16),
            pltpu.VMEM((4, QUARTER, WIDTH), BF16),
            pltpu.VMEM((2, 4, QUARTER, WIDTH), BF16),
            pltpu.VMEM((2, 4, QUARTER, WIDTH), BF16),
            pltpu.VMEM((8, QUARTER, WIDTH), BF16),
            pltpu.VMEM((8, QUARTER, WIDTH), BF16),
            pltpu.VMEM((2, 4, QUARTER, WIDTH), BF16),
            pltpu.VMEM((2, 4, QUARTER, WIDTH), BF16),
            pltpu.VMEM((4, 8, ROWS), F32),
            pltpu.VMEM((3, 8, ROWS), F32),
            pltpu.VMEM((8, ROWS), F32),
            pltpu.VMEM((4, 8, ROWS), F32),
            pltpu.VMEM((2, 2, EIGHTH, WIDTH), BF16),
            dma((2,)),
            dma((7, 4)), dma((4, 4)),
            dma((2, 4, 4)), dma((2, 4, 4)),
            dma((8,)), dma((8,)),
            dma((4,)), dma((4,)),
            dma((2, 4)), dma((2, 4)),
            dma((4,)), dma((4,)),
            dma((2, 4)), dma((2, 4)),
            dma((4,)), dma((4,)),
            dma((3,)), dma((3,)),
            dma((8,)), dma((8,)),
            dma((2, 4, 4)), dma((2, 4, 4)),
            dma((2, 7)), dma((2, 7)),
        ],
        compiler_params=pltpu.CompilerParams(
            collective_id=0, has_side_effects=True, vmem_limit_bytes=48 * 1024 * 1024
        ),
        cost_estimate=pl.CostEstimate(flops=7_300_000_000, bytes_accessed=4_000_000, transcendentals=3_000_000),
    )(
        pltpu.with_memory_space_constraint(picture_vectors, pltpu.HBM),
        pltpu.with_memory_space_constraint(caption_vectors, pltpu.HBM),
        sharpness_entry,
        offset_shift,
    )
    return both[:ROWS].astype(F32), both[ROWS:].astype(F32), loss[0]


def solution(mesh):
    placed = (P("dp", None), P("dp", None), P(), P())
    return jax.shard_map(
        per_device,
        mesh=mesh,
        in_specs=placed,
        out_specs=(P("dp", None), P("dp", None), P("dp")),
        check_vma=False,
    )
```

```python
import jax
import jax.numpy as jnp
from jax import lax
from jax.experimental import pallas as pl
from jax.experimental.pallas import tpu as pltpu
from jax.sharding import PartitionSpec as P

MESH = pl.DeviceIdType.MESH
F32 = jnp.float32
BF16 = jnp.bfloat16

NX, NY, NZ = 4, 4, 8
ROWS, WIDTH = 256, 1152
HALF, QUARTER, EIGHTH = 128, 64, 32
PAIRS = 16384


def unit_rows(values):
    values = values.astype(F32)
    inverse = lax.rsqrt(jnp.sum(values * values, axis=1, keepdims=True) + 1e-06)
    return inverse, values * inverse


def unit_back(unit, inverse, grad):
    return (grad - unit * jnp.sum(unit * grad, axis=1, keepdims=True)) * inverse


def contract(a, b, dims):
    return lax.dot_general(a, b, (dims, ((), ())), preferred_element_type=F32)


def kernel(
    pic_hbm, cap_hbm, sharp_ref, off_ref,
    both_out, loss_out,
    pic, cap, ibuf, jbuf, cbuf, ctbuf, pacc, tacc, lacc,
    pb, xr1, x2, rb, qr, ys, yr,
    ts, tr, vs, vr,
    ls, lx, rl, lq,
    hop,
    in_sem, i_s, i_r, t_s, t_r, d_s, d_r, x1_s, x1_r, x2_s, x2_r, y_s, y_r, yc_s, yc_r,
    ly_s, ly_r, lx_s, lx_r, e_s, e_r, v_s, v_r, g_s, g_r,
):
    dp, split = lax.axis_index("dp"), lax.axis_index("split")
    x = lax.rem(dp, NX)
    yl = lax.rem(dp // NX, 2)
    z = dp // (2 * NX)
    yh, core = split // 2, lax.rem(split, 2)
    y = 2 * yh + yl
    other = 1 - core
    first = core == 0
    second = core == 1

    def at(px, py, pz, pc):
        px, py, pz = lax.rem(px, NX), lax.rem(py, NY), lax.rem(pz, NZ)
        return ((pz * 2 + lax.rem(py, 2)) * NX + px, (py // 2) * 2 + pc)

    sibling = at(x, y, z, other)
    x_up, x_down, x_far = (at(x + k, y, z, core) for k in (1, 3, 2))
    z_up, z_down = at(x, y, z + 1, core), at(x, y, z + 7, core)
    y_up1, y_down1 = at(x, y + 1, z, 1), at(x, y + 3, z, 1)

    own_text = pl.multiple_of(yh * HALF, HALF)
    fetch_text = pltpu.make_async_copy(cap_hbm.at[pl.ds(own_text, HALF)], cap, in_sem.at[0])
    fetch_image = pltpu.make_async_copy(pic_hbm, pic, in_sem.at[1])
    fetch_text.start()
    fetch_image.start()

    barrier = pltpu.get_barrier_semaphore()
    partners = [sibling, x_up, x_down, x_far, z_up, z_down]
    partners += [at(x, y + k, z, c) for k in (1, 2, 3) for c in (0, 1)]
    for partner in partners:
        pl.semaphore_signal(barrier, inc=1, device_id=partner, device_id_type=MESH)

    pending = []

    def copy(src, dst, send, recv, to):
        return pltpu.make_async_remote_copy(
            src_ref=src, dst_ref=dst, send_sem=send[0].at[send[1:]], recv_sem=recv, device_id=to, device_id_type=MESH
        )

    def note(cond, src, ssem):
        rows = 0 if src.dtype == F32 else src.shape[0] * (src.shape[1] if len(src.shape) == 3 else 1)
        pending.append((cond, rows, ssem))

    def sent(rows, ssem):
        ref = ibuf.at[pl.ds(0, rows)] if rows else ls.at[0]
        copy(ref, ref, ssem, e_r.at[0], sibling).wait_send()

    branch = [None]

    def on(cond):
        def run(body):
            branch[0] = cond
            pl.when(cond)(body)
            branch[0] = None

        return run

    def send(src, dst, ssem, rsem, to):
        copy(src, dst, ssem, rsem, to).start()
        note(branch[0], src, ssem)

    def send_when(cond, *copies):
        @pl.when(cond)
        def _():
            for one in copies:
                copy(*one).start()

        for one in copies:
            note(cond, one[0], one[2])

    def drain(of=None):
        later = [entry for entry in pending if of is not None and not any(entry[2][0] is sem for sem in of)]
        pending[:] = [entry for entry in pending if not any(entry is k for k in later)]
        for cond in (None, first, second):
            some = [entry[1:] for entry in pending if entry[0] is cond]
            if cond is None:
                for entry in some:
                    sent(*entry)
            elif some:

                @pl.when(cond)
                def _():
                    for entry in some:
                        sent(*entry)

        pending[:] = later + [entry for entry in pending if not any(entry[0] is k for k in (None, first, second))]

    def landed(dst, rsem):
        copy(dst, dst, (e_s, 0), rsem, sibling).wait_recv()


    fetch_text.wait()
    jbuf[0:HALF, :] = unit_rows(cap[...])[1].astype(BF16)
    pl.semaphore_wait(barrier, len(partners))

    def irows(slot, piece):
        return ibuf.at[pl.ds(slot * ROWS + piece * QUARTER, QUARTER)]

    def jrows(slot, c, start=0, count=QUARTER):
        return jbuf.at[pl.ds(pl.multiple_of(slot * HALF + c * QUARTER + start, EIGHTH), count)]

    def text_piece(slot, piece):
        return jrows(slot, core, piece * EIGHTH, EIGHTH)

    def text_send(side, d, piece, source, target):
        send(
            text_piece(source, piece),
            text_piece(target, piece),
            (t_s, side, d, piece),
            t_r.at[side, d, piece],
            z_down if side else z_up,
        )

    for piece in (0, 1):
        text_send(0, 0, piece, 0, 2)
        text_send(1, 0, piece, 0, 1)

    def to_y(slot, piece):
        target = y_up1 if piece < 2 else y_down1
        return (irows(slot, piece), irows(slot, piece), (i_s, 2 + slot, piece), i_r.at[slot, piece], target)

    def to_x(source, slot, piece, kind):
        target = x_up if slot == 1 or (slot == 3 and piece < 2) else x_down
        return (irows(source, piece), irows(slot, piece), (i_s, kind, piece), i_r.at[slot, piece], target)

    fetch_image.wait()

    @pl.when(first)
    def _():
        ibuf[0:ROWS, :] = unit_rows(pic[...])[1].astype(BF16)

    send_when(
        first,
        to_x(0, 1, 0, 0), to_x(0, 2, 2, 1), to_y(0, 0), to_y(0, 2),
        to_x(0, 1, 1, 0), to_x(0, 2, 3, 1), to_y(0, 1), to_y(0, 3),
        to_x(0, 1, 2, 0), to_x(0, 2, 0, 1), to_x(0, 1, 3, 0), to_x(0, 2, 1, 1),
    )

    def pass_near(up, down, onward):
        landed(irows(1, up), i_r.at[1, up])
        if onward:
            send(*to_x(1, 3, up, 6))
        send(*to_y(1, up))
        landed(irows(2, down), i_r.at[2, down])
        if onward:
            send(*to_x(2, 3, down, 6))
        send(*to_y(2, down))

    def pass_far(*pieces):
        for piece in pieces:
            landed(irows(3, piece), i_r.at[3, piece])
            send(*to_y(3, piece))

    def images_in(slot, *pieces):
        for piece in pieces or range(4):
            landed(irows(slot, piece), i_r.at[slot, piece])

    for zeroed in (lacc,):

        def clear(n, carry):
            rows = pl.ds(pl.multiple_of(n * QUARTER, QUARTER), QUARTER)
            zeroed[rows, :] = jnp.zeros((QUARTER, zeroed.shape[1]), F32)
            return carry

        lax.fori_loop(0, 16, clear, 0)

    def swap(slot):
        send(jrows(slot, core), jrows(slot, core), (d_s, slot), d_r.at[slot], sibling)

    def swapped(*slots):
        for slot in slots:
            landed(jrows(slot, other), d_r.at[slot])

    def text_hop(d, pieces=(0, 1)):
        for piece in pieces:
            for side in (0, 1):
                if d == 4:
                    if piece == side:
                        landed(text_piece(7, piece), t_r.at[side, 3, piece])
                    continue
                here = 2 * d - side
                landed(text_piece(here, piece), t_r.at[side, d - 1, piece])
                if d < 3:
                    text_send(side, d, piece, here, here + 2)
                elif piece == side:
                    text_send(side, 3, piece, here, 7)
        if pieces[-1] == 0:
            return
        if d < 4:
            swap(2 * d - 1)
            swap(2 * d)
        else:
            swap(7)

    sharp, off = sharp_ref[0], off_ref[0]
    log2_e = 1.4426950408889634
    sharp2, off2 = sharp * log2_e, off * log2_e

    def logits_block(i, j, diagonal=False, half=None):
        start = i * ROWS + (half or 0) * HALF
        ri = slice(start, start + (ROWS if half is None else HALF))
        rj = slice(j * ROWS, (j + 1) * ROWS)
        logits = sharp2 * contract(ibuf[ri, :], jbuf[rj, :], ((1,), (1,))) + off2
        if diagonal:
            row = lax.broadcasted_iota(jnp.int32, (ROWS, ROWS), 0)
            col = lax.broadcasted_iota(jnp.int32, (ROWS, ROWS), 1)
            same = jnp.logical_and(row == col + yh * HALF, col < HALF)
            logits = jnp.where(same, -logits, logits)
        grown = jnp.exp2(logits)
        total = 1.0 + grown
        rough = pl.reciprocal(total, approx=True)
        inverse = rough * (2.0 - total * rough)
        coef = grown * inverse
        lost = (grown - (total - 1.0)) * inverse
        lacc[ri, :] += jnp.log(total[:, :HALF] * total[:, HALF:]) + (lost[:, :HALF] + lost[:, HALF:])
        if diagonal:
            coef = jnp.where(same, -coef, coef)
        coef = coef.astype(BF16)
        cbuf[ri, rj] = coef
        ctbuf[rj, ri] = coef.T

    def product(out, left, right, m, k0, k1):
        rows, depth = slice(m * ROWS, (m + 1) * ROWS), slice(k0 * ROWS, k1 * ROWS)
        a = left[rows, depth]
        for n in range(0, WIDTH, 256):
            columns = slice(n, min(n + 256, WIDTH))
            result = contract(a, right[depth, columns], ((1,), (0,)))
            out[rows, columns] = result if k0 == 0 else out[rows, columns] + result

    def image_product(i, j0, j1):
        product(pacc, cbuf, jbuf, i, j0, j1)

    def text_product(j, i0, i1):
        product(tacc, ctbuf, ibuf, j, i0, i1)

    up_hi = lax.rem(y + 1, NY) // 2
    turns = (
        other * 2 * (1 - yh) + core * 2 * up_hi,
        core * (2 * up_hi + 1),
        other * 2 * yh + core * 2 * (1 - up_hi),
        core * (2 * (1 - up_hi) + 1),
    )

    def hand_over(slot):
        for side, q, to in ((0, 2 * yh + 1, y_up1), (1, 2 * (1 - yh) + 1, y_down1)):
            rows = pl.ds(pl.multiple_of(slot * ROWS + q * QUARTER, QUARTER), QUARTER)
            ys[side, slot] = pacc[rows, :].astype(BF16)
            send(ys.at[side, slot], yr.at[side, slot], (yc_s, side, slot), yc_r.at[side, slot], to)

    def handed(slot):
        rows = part_rows(slot, 3)
        for side in (0, 1):
            landed(yr.at[side, slot], yc_r.at[side, slot])
        pacc[rows, :] += yr[0, slot].astype(F32) + yr[1, slot].astype(F32)

    def seat(k):
        return pl.ds(k * QUARTER, QUARTER)

    def part_rows(slot, k):
        return pl.ds(pl.multiple_of(slot * ROWS + turns[k] * QUARTER, QUARTER), QUARTER)

    def far_turn(k):
        pb[0, seat(k), :] = pacc[part_rows(3, k), :].astype(BF16)
        send(pb.at[0, seat(k)], xr1.at[seat(k)], (x1_s, k), x1_r.at[k], x_up if k < 2 else x_down)

    def near_turn(slot, k):
        side = 0 if slot == 2 else 1
        rows = pacc[part_rows(slot, k), :]
        if (k < 2) == (slot == 2):
            landed(xr1.at[seat(k)], x1_r.at[k])
            rows = rows + xr1[seat(k), :].astype(F32)
        pb[1 + side, seat(k), :] = rows.astype(BF16)
        send(
            pb.at[1 + side, seat(k)],
            x2.at[side, seat(k)],
            (x2_s, side, k),
            x2_r.at[side, k],
            x_down if side else x_up,
        )

    def text_over(low, count):
        for slot in range(low, low + count):
            mine = pl.ds(pl.multiple_of(slot * HALF + other * QUARTER, QUARTER), QUARTER)
            ts[slot] = tacc[mine, :].astype(BF16)
        slots = pl.ds(low, count)
        send(ts.at[slots], tr.at[slots], (e_s, low), e_r.at[low], sibling)

    def text_came(low, count):
        landed(tr.at[pl.ds(low, count)], e_r.at[low])

    def piece_rows(piece):
        return pl.ds(piece * EIGHTH, EIGHTH)

    def text_sum(slot, piece):
        start = slot * HALF + core * QUARTER + piece * EIGHTH
        return tacc[pl.ds(pl.multiple_of(start, EIGHTH), EIGHTH), :] + tr[slot, piece_rows(piece), :].astype(F32)

    def text_back(d, steps=(0, 1)):
        for step in steps:
            for side in (0, 1):
                piece = step if side else 1 - step
                if d == 4 and piece != side:
                    continue
                rows = text_sum(7 if d == 4 else 2 * d - 1 + side, piece)
                part = piece_rows(piece)
                if d < 3 or (d == 3 and piece == side):
                    landed(vr.at[side, d, part], v_r.at[side, d, piece])
                    rows = rows + vr[side, d, part, :].astype(F32)
                vs[side, d - 1, part, :] = rows.astype(BF16)
                send(
                    vs.at[side, d - 1, part],
                    vr.at[side, d - 1, part],
                    (v_s, side, d - 1, piece),
                    v_r.at[side, d - 1, piece],
                    z_down if side else z_up,
                )

    @on(first)
    def _():
        text_hop(1, (0,))
        pass_near(0, 2, True)
        text_hop(1, (1,))
        pass_near(1, 3, True)
        swapped(1)
        logits_block(0, 0, True)
        pass_near(2, 0, False)
        text_hop(2, (0,))
        text_hop(2, (1,))
        pass_near(3, 1, False)
        swapped(2, 3)
        logits_block(0, 1)
        pass_far(0, 2)
        logits_block(1, 0)
        logits_block(2, 0)
        image_product(0, 0, 2)
        text_hop(3)
        pass_far(1, 3)
        logits_block(1, 1)
        logits_block(2, 1)
        image_product(1, 0, 2)
        logits_block(3, 0)
        image_product(2, 0, 2)
        logits_block(3, 1)
        swapped(4, 5)
        text_hop(4)
        text_product(0, 0, 4)
        logits_block(0, 2)
        text_product(1, 0, 4)
        logits_block(1, 2)
        image_product(3, 0, 2)
        logits_block(2, 2)
        logits_block(3, 2)
        text_product(2, 0, 4)
        text_over(0, 4)
        text_over(4, 2)
        swapped(6, 7)
        logits_block(3, 3)
        logits_block(1, 3)
        image_product(3, 2, 4)
        far_turn(0)
        far_turn(2)
        hand_over(3)
        logits_block(2, 3)
        logits_block(0, 3)
        text_product(3, 0, 4)
        text_over(6, 2)
        image_product(1, 2, 4)
        near_turn(1, 0)
        hand_over(1)
        image_product(2, 2, 4)
        near_turn(2, 2)
        hand_over(2)
        image_product(0, 2, 4)
        hand_over(0)
        text_came(6, 2)
        text_back(4)
        text_came(4, 2)
        text_back(3, (0,))

    @on(second)
    def _():
        text_hop(1)
        images_in(0)
        swapped(1)
        logits_block(0, 0)
        text_hop(2)
        swapped(2, 3)
        logits_block(0, 1)
        images_in(1, 0, 1)
        images_in(2, 2, 3)
        logits_block(1, 0, half=0)
        logits_block(2, 0, half=1)
        text_hop(3)
        logits_block(1, 1, half=0)
        logits_block(2, 1, half=1)
        swapped(4, 5)
        logits_block(0, 2)
        image_product(0, 0, 3)
        logits_block(1, 2, half=0)
        logits_block(2, 2, half=1)
        text_hop(4)
        images_in(1, 2, 3)
        images_in(2, 0, 1)
        logits_block(1, 0, half=1)
        logits_block(2, 0, half=0)
        logits_block(1, 1, half=1)
        text_product(0, 0, 3)
        logits_block(2, 1, half=0)
        logits_block(1, 2, half=1)
        text_product(1, 0, 3)
        logits_block(2, 2, half=0)
        swapped(6, 7)
        logits_block(1, 3)
        text_product(2, 0, 3)
        logits_block(2, 3)
        image_product(1, 0, 4)
        logits_block(0, 3)
        image_product(2, 0, 4)
        text_product(3, 0, 3)
        near_turn(1, 0)
        near_turn(2, 2)
        near_turn(1, 1)
        images_in(3)
        logits_block(3, 3)
        logits_block(3, 2)
        text_product(3, 3, 4)
        logits_block(3, 1)
        text_over(6, 2)
        logits_block(3, 0)
        image_product(3, 0, 4)
        far_turn(0)
        far_turn(2)
        far_turn(1)
        text_came(6, 2)
        text_back(4)
        text_product(2, 3, 4)
        text_over(4, 2)
        text_product(1, 3, 4)
        text_product(0, 3, 4)
        text_over(0, 4)
        handed(3)
        far_turn(3)
        text_came(4, 2)
        text_back(3, (0,))
        handed(2)
        near_turn(2, 3)
        image_product(0, 3, 4)

    near_turn(2, 0)
    near_turn(1, 2)
    text_back(3, (1,))

    ones = jnp.ones((8, HALF), F32)
    for i in range(4):
        ls[i] = lax.dot_general(
            ones,
            lacc[i * ROWS : (i + 1) * ROWS, :],
            (((1,), (1,)), ((), ())),
            precision=lax.Precision.HIGHEST,
            preferred_element_type=F32,
        )
    send(ls.at[2], lx.at[0], (lx_s, 0), lx_r.at[0], x_up)
    send(ls.at[1], lx.at[1], (lx_s, 1), lx_r.at[1], x_down)
    send(ls.at[3], lx.at[2], (lx_s, 2), lx_r.at[2], x_far)

    text_came(0, 4)
    text_back(2, (0,))

    @on(second)
    def _():
        near_turn(2, 1)
        handed(1)
        near_turn(1, 3)

    text_back(2, (1,))
    text_back(1, (0,))

    y_up0, y_down0 = at(x, y + 1, z, 0), at(x, y + 3, z, 0)

    def image_sum(k):
        landed(x2.at[0, seat(k)], x2_r.at[0, k])
        landed(x2.at[1, seat(k)], x2_r.at[1, k])
        return pacc[part_rows(0, k), :] + (x2[0, seat(k), :].astype(F32) + x2[1, seat(k), :].astype(F32))

    def image_out(k, box, to):
        total = image_sum(k)
        if core_of[0] == 1 and k == 0:
            landed(qr.at[3], y_r.at[3])
            total = total + qr[3].astype(F32)
        rb[seat(k), :] = total.astype(BF16)
        send(rb.at[seat(k)], qr.at[box], (y_s, k), y_r.at[box], to)

    core_of = [0]

    @on(first)
    def _():
        image_out(0, 3, y_up1)

    core_of[0] = 1

    @on(second)
    def _():
        image_out(2, 2, y_down0)

    text_back(1, (1,))

    @on(first)
    def _():
        qr[0] = image_sum(2).astype(BF16)

    @on(second)
    def _():
        qr[0] = jnp.zeros((QUARTER, WIDTH), BF16)
        image_out(0, 1, y_up0)

    source = yh + 2 * core
    block_yl = lax.rem(yl + core, 2)

    def owner_of(q):
        to = at(x, 2 * (q // 2) + block_yl, z, q % 2)
        return to, jnp.logical_and(dp == to[0], split == to[1])

    for k in range(3):
        landed(lx.at[k], lx_r.at[k])
    rl[...] = ls[0] + lx[0] + lx[1] + lx[2]
    for q in range(4):
        to, own = owner_of(q)
        send_when(jnp.logical_not(own), (rl, lq.at[source], (ly_s, q), ly_r.at[source], to))

        @pl.when(own)
        def _():
            lq[source] = rl[...]

    drain((i_s, t_s, d_s))
    mine = yh * 2 + core
    outs = (both_out.at[pl.ds(0, ROWS)], both_out.at[pl.ds(ROWS, ROWS)])

    def quarter_rows(q, start=0, count=QUARTER):
        return pl.ds(pl.multiple_of(q * QUARTER + start, EIGHTH), count)

    my_rows = quarter_rows(mine)
    y_up, y_down = at(x, y + 1, z, core), at(x, y + 3, z, core)

    def gather_out(kind, grad, values):
        inverse, unit = unit_rows(values)
        out = outs[kind]
        out[my_rows, :] = unit_back(unit, inverse, sharp * grad).astype(BF16)
        low, high = out.at[quarter_rows(mine, 0, EIGHTH)], out.at[quarter_rows(mine, EIGHTH, EIGHTH)]
        send(low, hop.at[kind, 0], (g_s, kind, 0), g_r.at[kind, 0], y_up)
        send(high, hop.at[kind, 1], (g_s, kind, 1), g_r.at[kind, 1], y_down)
        send(out.at[my_rows], out.at[my_rows], (g_s, kind, 2), g_r.at[kind, 2], sibling)

    def gather_on(kind):
        out = outs[kind]
        landed(hop.at[kind, 0], g_r.at[kind, 0])
        there = out.at[quarter_rows(2 * (1 - up_hi) + core, 0, EIGHTH)]
        send(hop.at[kind, 0], there, (g_s, kind, 3), g_r.at[kind, 3], y_up)
        landed(hop.at[kind, 1], g_r.at[kind, 1])
        there = out.at[quarter_rows(2 * up_hi + core, EIGHTH, EIGHTH)]
        send(hop.at[kind, 1], there, (g_s, kind, 4), g_r.at[kind, 4], y_down)

    def gather_over(kind):
        for half in (0, 1):
            here = outs[kind].at[quarter_rows((1 - yh) * 2 + core, half * EIGHTH, EIGHTH)]
            landed(here, g_r.at[kind, 3 + half])
            send(here, here, (g_s, kind, 5 + half), g_r.at[kind, 5 + half], sibling)

    def gather_end(kind):
        landed(outs[kind].at[quarter_rows(yh * 2 + other)], g_r.at[kind, 2])
        for half in (0, 1):
            here = outs[kind].at[quarter_rows((1 - yh) * 2 + other, half * EIGHTH, EIGHTH)]
            landed(here, g_r.at[kind, 5 + half])

    grads = []
    for piece in (0, 1):
        grad = text_sum(0, piece)
        for side in (0, 1):
            landed(vr.at[side, 0, piece_rows(piece)], v_r.at[side, 0, piece])
            grad = grad + vr[side, 0, piece_rows(piece), :].astype(F32)
        grads.append(grad)
    grad = jnp.concatenate(grads, axis=0)
    gather_out(1, grad, cap[pl.ds(pl.multiple_of(core * QUARTER, QUARTER), QUARTER), :])

    @on(second)
    def _():
        image_out(1, 1, y_up1)
        handed(0)
        image_out(3, 2, y_down1)

    gather_on(1)

    for k in range(4):
        here = jnp.logical_and(first, yh == k)

        @pl.when(jnp.logical_not(here))
        def _():
            landed(lq.at[k], ly_r.at[k])

    loss_out[...] = ((lq[0] + lq[1]) + (lq[2] + lq[3])) * (1.0 / PAIRS)

    drain((e_s, v_s, x1_s, x2_s, yc_s, lx_s))
    landed(qr.at[1], y_r.at[1])
    landed(qr.at[2], y_r.at[2])
    grad = qr[0].astype(F32) + (qr[1].astype(F32) + qr[2].astype(F32))
    gather_out(0, grad, pic[my_rows, :])
    gather_over(1)
    gather_on(0)
    drain()
    for cond, rows, ssem in pending:

        @pl.when(cond)
        def _():
            sent(rows, ssem)

    pending.clear()
    gather_end(1)
    gather_over(0)
    gather_end(0)
    drain()


def per_device(picture_vectors, caption_vectors, sharpness_entry, offset_shift):
    dma = pltpu.SemaphoreType.DMA
    vmem = pl.BlockSpec(memory_space=pltpu.VMEM)
    smem = pl.BlockSpec(memory_space=pltpu.SMEM)
    hbm = pl.BlockSpec(memory_space=pltpu.HBM)
    both, loss = pl.pallas_call(
        kernel,
        out_shape=(
            jax.ShapeDtypeStruct((2 * ROWS, WIDTH), BF16),
            jax.ShapeDtypeStruct((8, ROWS), F32),
        ),
        in_specs=[hbm, hbm, smem, smem],
        out_specs=(vmem, vmem),
        scratch_shapes=[
            pltpu.VMEM((ROWS, WIDTH), BF16),
            pltpu.VMEM((HALF, WIDTH), BF16),
            pltpu.VMEM((4 * ROWS, WIDTH), BF16),
            pltpu.VMEM((8 * HALF, WIDTH), BF16),
            pltpu.VMEM((4 * ROWS, 8 * HALF), BF16),
            pltpu.VMEM((8 * HALF, 4 * ROWS), BF16),
            pltpu.VMEM((4 * ROWS, WIDTH), F32),
            pltpu.VMEM((8 * HALF, WIDTH), F32),
            pltpu.VMEM((4 * ROWS, HALF), F32),
            pltpu.VMEM((3, ROWS, WIDTH), BF16),
            pltpu.VMEM((ROWS, WIDTH), BF16),
            pltpu.VMEM((2, ROWS, WIDTH), BF16),
            pltpu.VMEM((ROWS, WIDTH), BF16),
            pltpu.VMEM((4, QUARTER, WIDTH), BF16),
            pltpu.VMEM((2, 4, QUARTER, WIDTH), BF16),
            pltpu.VMEM((2, 4, QUARTER, WIDTH), BF16),
            pltpu.VMEM((8, QUARTER, WIDTH), BF16),
            pltpu.VMEM((8, QUARTER, WIDTH), BF16),
            pltpu.VMEM((2, 4, QUARTER, WIDTH), BF16),
            pltpu.VMEM((2, 4, QUARTER, WIDTH), BF16),
            pltpu.VMEM((4, 8, ROWS), F32),
            pltpu.VMEM((3, 8, ROWS), F32),
            pltpu.VMEM((8, ROWS), F32),
            pltpu.VMEM((4, 8, ROWS), F32),
            pltpu.VMEM((2, 2, EIGHTH, WIDTH), BF16),
            dma((2,)),
            dma((7, 4)), dma((4, 4)),
            dma((2, 4, 2)), dma((2, 4, 2)),
            dma((8,)), dma((8,)),
            dma((4,)), dma((4,)),
            dma((2, 4)), dma((2, 4)),
            dma((4,)), dma((4,)),
            dma((2, 4)), dma((2, 4)),
            dma((4,)), dma((4,)),
            dma((3,)), dma((3,)),
            dma((8,)), dma((8,)),
            dma((2, 4, 2)), dma((2, 4, 2)),
            dma((2, 7)), dma((2, 7)),
        ],
        compiler_params=pltpu.CompilerParams(
            collective_id=0, has_side_effects=True, vmem_limit_bytes=48 * 1024 * 1024
        ),
        cost_estimate=pl.CostEstimate(flops=7_300_000_000, bytes_accessed=4_000_000, transcendentals=3_000_000),
    )(
        pltpu.with_memory_space_constraint(picture_vectors, pltpu.HBM),
        pltpu.with_memory_space_constraint(caption_vectors, pltpu.HBM),
        sharpness_entry,
        offset_shift,
    )
    return both[:ROWS].astype(F32), both[ROWS:].astype(F32), loss[0]


def solution(mesh):
    placed = (P("dp", None), P("dp", None), P(), P())
    return jax.shard_map(
        per_device,
        mesh=mesh,
        in_specs=placed,
        out_specs=(P("dp", None), P("dp", None), P("dp")),
        check_vma=False,
    )
```

```python
import jax
import jax.numpy as jnp
from jax import lax
from jax.experimental import pallas as pl
from jax.experimental.pallas import tpu as pltpu
from jax.sharding import PartitionSpec as P

MESH = pl.DeviceIdType.MESH
F32 = jnp.float32
BF16 = jnp.bfloat16

NX, NY, NZ = 4, 4, 8
ROWS, WIDTH = 256, 1152
HALF, QUARTER, EIGHTH = 128, 64, 32
PAIRS = 16384


def unit_rows(values):
    values = values.astype(F32)
    inverse = lax.rsqrt(jnp.sum(values * values, axis=1, keepdims=True) + 1e-06)
    return inverse, values * inverse


def unit_back(unit, inverse, grad):
    return (grad - unit * jnp.sum(unit * grad, axis=1, keepdims=True)) * inverse


def contract(a, b, dims):
    return lax.dot_general(a, b, (dims, ((), ())), preferred_element_type=F32)


def kernel(
    pic_hbm, cap_hbm, sharp_ref, off_ref,
    both_out, loss_out,
    pic, cap, ibuf, jbuf, cbuf, ctbuf, pacc, tacc, lacc,
    pb, xr1, x2, rb, qr, ys, yr,
    ts, tr, vs, vr,
    ls, lx, rl, lq,
    hop,
    in_sem, i_s, i_r, t_s, t_r, d_s, d_r, x1_s, x1_r, x2_s, x2_r, y_s, y_r, yc_s, yc_r,
    ly_s, ly_r, lx_s, lx_r, e_s, e_r, v_s, v_r, g_s, g_r,
):
    dp, split = lax.axis_index("dp"), lax.axis_index("split")
    x = lax.rem(dp, NX)
    yl = lax.rem(dp // NX, 2)
    z = dp // (2 * NX)
    yh, core = split // 2, lax.rem(split, 2)
    y = 2 * yh + yl
    other = 1 - core
    first = core == 0
    second = core == 1

    def at(px, py, pz, pc):
        px, py, pz = lax.rem(px, NX), lax.rem(py, NY), lax.rem(pz, NZ)
        return ((pz * 2 + lax.rem(py, 2)) * NX + px, (py // 2) * 2 + pc)

    sibling = at(x, y, z, other)
    x_up, x_down, x_far = (at(x + k, y, z, core) for k in (1, 3, 2))
    z_up, z_down = at(x, y, z + 1, core), at(x, y, z + 7, core)
    y_up1, y_down1 = at(x, y + 1, z, 1), at(x, y + 3, z, 1)

    own_text = pl.multiple_of(yh * HALF, HALF)
    fetch_text = pltpu.make_async_copy(cap_hbm.at[pl.ds(own_text, HALF)], cap, in_sem.at[0])
    fetch_image = pltpu.make_async_copy(pic_hbm, pic, in_sem.at[1])
    fetch_text.start()
    fetch_image.start()

    barrier = pltpu.get_barrier_semaphore()
    partners = [sibling, x_up, x_down, x_far, z_up, z_down]
    partners += [at(x, y + k, z, c) for k in (1, 2, 3) for c in (0, 1)]
    for partner in partners:
        pl.semaphore_signal(barrier, inc=1, device_id=partner, device_id_type=MESH)

    pending = []

    def copy(src, dst, send, recv, to):
        return pltpu.make_async_remote_copy(
            src_ref=src, dst_ref=dst, send_sem=send[0].at[send[1:]], recv_sem=recv, device_id=to, device_id_type=MESH
        )

    def note(cond, src, ssem):
        rows = 0 if src.dtype == F32 else src.shape[0] * (src.shape[1] if len(src.shape) == 3 else 1)
        pending.append((cond, rows, ssem))

    def sent(rows, ssem):
        ref = ibuf.at[pl.ds(0, rows)] if rows else ls.at[0]
        copy(ref, ref, ssem, e_r.at[0], sibling).wait_send()

    branch = [None]

    def on(cond):
        def run(body):
            branch[0] = cond
            pl.when(cond)(body)
            branch[0] = None

        return run

    def send(src, dst, ssem, rsem, to):
        copy(src, dst, ssem, rsem, to).start()
        note(branch[0], src, ssem)

    def send_when(cond, *copies):
        @pl.when(cond)
        def _():
            for one in copies:
                copy(*one).start()

        for one in copies:
            note(cond, one[0], one[2])

    def drain(of=None):
        later = [entry for entry in pending if of is not None and not any(entry[2][0] is sem for sem in of)]
        pending[:] = [entry for entry in pending if not any(entry is k for k in later)]
        for cond in (None, first, second):
            some = [entry[1:] for entry in pending if entry[0] is cond]
            if cond is None:
                for entry in some:
                    sent(*entry)
            elif some:

                @pl.when(cond)
                def _():
                    for entry in some:
                        sent(*entry)

        pending[:] = later + [entry for entry in pending if not any(entry[0] is k for k in (None, first, second))]

    def landed(dst, rsem):
        copy(dst, dst, (e_s, 0), rsem, sibling).wait_recv()


    fetch_text.wait()
    jbuf[0:HALF, :] = unit_rows(cap[...])[1].astype(BF16)
    pl.semaphore_wait(barrier, len(partners))

    def irows(slot, piece):
        return ibuf.at[pl.ds(slot * ROWS + piece * QUARTER, QUARTER)]

    def jrows(slot, c, start=0, count=QUARTER):
        return jbuf.at[pl.ds(pl.multiple_of(slot * HALF + c * QUARTER + start, EIGHTH), count)]

    def text_piece(slot, piece):
        return jrows(slot, core, piece * EIGHTH, EIGHTH)

    def text_send(side, d, piece, source, target):
        send(
            text_piece(source, piece),
            text_piece(target, piece),
            (t_s, side, d, piece),
            t_r.at[side, d, piece],
            z_down if side else z_up,
        )

    for piece in (0, 1):
        text_send(0, 0, piece, 0, 2)
        text_send(1, 0, piece, 0, 1)

    def to_y(slot, piece):
        target = y_up1 if piece < 2 else y_down1
        return (irows(slot, piece), irows(slot, piece), (i_s, 2 + slot, piece), i_r.at[slot, piece], target)

    def to_x(source, slot, piece, kind):
        target = x_up if slot == 1 or (slot == 3 and piece < 2) else x_down
        return (irows(source, piece), irows(slot, piece), (i_s, kind, piece), i_r.at[slot, piece], target)

    fetch_image.wait()

    @pl.when(first)
    def _():
        ibuf[0:ROWS, :] = unit_rows(pic[...])[1].astype(BF16)

    send_when(
        first,
        to_x(0, 1, 0, 0), to_x(0, 2, 2, 1), to_y(0, 0), to_y(0, 2),
        to_x(0, 1, 1, 0), to_x(0, 2, 3, 1), to_y(0, 1), to_y(0, 3),
        to_x(0, 1, 2, 0), to_x(0, 2, 0, 1), to_x(0, 1, 3, 0), to_x(0, 2, 1, 1),
    )

    def pass_near(up, down, onward):
        landed(irows(1, up), i_r.at[1, up])
        if onward:
            send(*to_x(1, 3, up, 6))
        send(*to_y(1, up))
        landed(irows(2, down), i_r.at[2, down])
        if onward:
            send(*to_x(2, 3, down, 6))
        send(*to_y(2, down))

    def pass_far(*pieces):
        for piece in pieces:
            landed(irows(3, piece), i_r.at[3, piece])
            send(*to_y(3, piece))

    def images_in(slot, *pieces):
        for piece in pieces or range(4):
            landed(irows(slot, piece), i_r.at[slot, piece])

    for zeroed in (lacc,):

        def clear(n, carry):
            rows = pl.ds(pl.multiple_of(n * QUARTER, QUARTER), QUARTER)
            zeroed[rows, :] = jnp.zeros((QUARTER, zeroed.shape[1]), F32)
            return carry

        lax.fori_loop(0, 16, clear, 0)

    def swap(slot):
        send(jrows(slot, core), jrows(slot, core), (d_s, slot), d_r.at[slot], sibling)

    def swapped(*slots):
        for slot in slots:
            landed(jrows(slot, other), d_r.at[slot])

    def text_hop(d, pieces=(0, 1)):
        for piece in pieces:
            for side in (0, 1):
                if d == 4:
                    if piece == side:
                        landed(text_piece(7, piece), t_r.at[side, 3, piece])
                    continue
                here = 2 * d - side
                landed(text_piece(here, piece), t_r.at[side, d - 1, piece])
                if d < 3:
                    text_send(side, d, piece, here, here + 2)
                elif piece == side:
                    text_send(side, 3, piece, here, 7)
        if pieces[-1] == 0:
            return
        if d < 4:
            swap(2 * d - 1)
            swap(2 * d)
        else:
            swap(7)

    sharp, off = sharp_ref[0], off_ref[0]
    log2_e = 1.4426950408889634
    sharp2, off2 = sharp * log2_e, off * log2_e

    def logits_block(i, j, diagonal=False, half=None):
        start = i * ROWS + (half or 0) * HALF
        ri = slice(start, start + (ROWS if half is None else HALF))
        rj = slice(j * ROWS, (j + 1) * ROWS)
        logits = sharp2 * contract(ibuf[ri, :], jbuf[rj, :], ((1,), (1,))) + off2
        if diagonal:
            row = lax.broadcasted_iota(jnp.int32, (ROWS, ROWS), 0)
            col = lax.broadcasted_iota(jnp.int32, (ROWS, ROWS), 1)
            same = jnp.logical_and(row == col + yh * HALF, col < HALF)
            logits = jnp.where(same, -logits, logits)
        grown = jnp.exp2(logits)
        total = 1.0 + grown
        rough = pl.reciprocal(total, approx=True)
        inverse = rough * (2.0 - total * rough)
        coef = grown * inverse
        lost = (grown - (total - 1.0)) * inverse
        lacc[ri, :] += jnp.log(total[:, :HALF] * total[:, HALF:]) + (lost[:, :HALF] + lost[:, HALF:])
        if diagonal:
            coef = jnp.where(same, -coef, coef)
        coef = coef.astype(BF16)
        cbuf[ri, rj] = coef
        ctbuf[rj, ri] = coef.T

    def product(out, left, right, m, k0, k1):
        rows, depth = slice(m * ROWS, (m + 1) * ROWS), slice(k0 * ROWS, k1 * ROWS)
        a = left[rows, depth]
        for n in range(0, WIDTH, 256):
            columns = slice(n, min(n + 256, WIDTH))
            result = contract(a, right[depth, columns], ((1,), (0,)))
            out[rows, columns] = result if k0 == 0 else out[rows, columns] + result

    def image_product(i, j0, j1):
        product(pacc, cbuf, jbuf, i, j0, j1)

    def text_product(j, i0, i1):
        product(tacc, ctbuf, ibuf, j, i0, i1)

    up_hi = lax.rem(y + 1, NY) // 2
    turns = (
        other * 2 * (1 - yh) + core * 2 * up_hi,
        core * (2 * up_hi + 1),
        other * 2 * yh + core * 2 * (1 - up_hi),
        core * (2 * (1 - up_hi) + 1),
    )

    def hand_over(slot):
        for side, q, to in ((0, 2 * yh + 1, y_up1), (1, 2 * (1 - yh) + 1, y_down1)):
            rows = pl.ds(pl.multiple_of(slot * ROWS + q * QUARTER, QUARTER), QUARTER)
            ys[side, slot] = pacc[rows, :].astype(BF16)
            send(ys.at[side, slot], yr.at[side, slot], (yc_s, side, slot), yc_r.at[side, slot], to)

    def handed(slot):
        rows = part_rows(slot, 3)
        for side in (0, 1):
            landed(yr.at[side, slot], yc_r.at[side, slot])
        pacc[rows, :] += yr[0, slot].astype(F32) + yr[1, slot].astype(F32)

    def seat(k):
        return pl.ds(k * QUARTER, QUARTER)

    def part_rows(slot, k):
        return pl.ds(pl.multiple_of(slot * ROWS + turns[k] * QUARTER, QUARTER), QUARTER)

    def far_turn(k):
        pb[0, seat(k), :] = pacc[part_rows(3, k), :].astype(BF16)
        send(pb.at[0, seat(k)], xr1.at[seat(k)], (x1_s, k), x1_r.at[k], x_up if k < 2 else x_down)

    def near_turn(slot, k):
        side = 0 if slot == 2 else 1
        rows = pacc[part_rows(slot, k), :]
        if (k < 2) == (slot == 2):
            landed(xr1.at[seat(k)], x1_r.at[k])
            rows = rows + xr1[seat(k), :].astype(F32)
        pb[1 + side, seat(k), :] = rows.astype(BF16)
        send(
            pb.at[1 + side, seat(k)],
            x2.at[side, seat(k)],
            (x2_s, side, k),
            x2_r.at[side, k],
            x_down if side else x_up,
        )

    def text_over(low, count):
        for slot in range(low, low + count):
            mine = pl.ds(pl.multiple_of(slot * HALF + other * QUARTER, QUARTER), QUARTER)
            ts[slot] = tacc[mine, :].astype(BF16)
        slots = pl.ds(low, count)
        send(ts.at[slots], tr.at[slots], (e_s, low), e_r.at[low], sibling)

    def text_came(low, count):
        landed(tr.at[pl.ds(low, count)], e_r.at[low])

    def piece_rows(piece):
        return pl.ds(piece * EIGHTH, EIGHTH)

    def text_sum(slot, piece):
        start = slot * HALF + core * QUARTER + piece * EIGHTH
        return tacc[pl.ds(pl.multiple_of(start, EIGHTH), EIGHTH), :] + tr[slot, piece_rows(piece), :].astype(F32)

    def text_back(d, steps=(0, 1)):
        for step in steps:
            for side in (0, 1):
                piece = step if side else 1 - step
                if d == 4 and piece != side:
                    continue
                rows = text_sum(7 if d == 4 else 2 * d - 1 + side, piece)
                part = piece_rows(piece)
                if d < 3 or (d == 3 and piece == side):
                    landed(vr.at[side, d, part], v_r.at[side, d, piece])
                    rows = rows + vr[side, d, part, :].astype(F32)
                vs[side, d - 1, part, :] = rows.astype(BF16)
                send(
                    vs.at[side, d - 1, part],
                    vr.at[side, d - 1, part],
                    (v_s, side, d - 1, piece),
                    v_r.at[side, d - 1, piece],
                    z_down if side else z_up,
                )

    @on(first)
    def _():
        text_hop(1, (0,))
        pass_near(0, 2, True)
        text_hop(1, (1,))
        pass_near(1, 3, True)
        swapped(1)
        logits_block(0, 0, True)
        pass_near(2, 0, False)
        text_hop(2, (0,))
        text_hop(2, (1,))
        pass_near(3, 1, False)
        swapped(2, 3)
        logits_block(0, 1)
        pass_far(0, 2)
        logits_block(1, 0)
        logits_block(2, 0)
        image_product(0, 0, 2)
        text_hop(3)
        pass_far(1, 3)
        logits_block(1, 1)
        logits_block(2, 1)
        image_product(1, 0, 2)
        logits_block(3, 0)
        image_product(2, 0, 2)
        logits_block(3, 1)
        swapped(4, 5)
        text_hop(4)
        text_product(0, 0, 4)
        logits_block(0, 2)
        text_product(1, 0, 4)
        logits_block(1, 2)
        image_product(3, 0, 2)
        logits_block(2, 2)
        logits_block(3, 2)
        text_product(2, 0, 4)
        text_over(0, 4)
        text_over(4, 2)
        swapped(6, 7)
        logits_block(3, 3)
        logits_block(1, 3)
        image_product(3, 2, 4)
        far_turn(0)
        far_turn(2)
        hand_over(3)
        logits_block(2, 3)
        logits_block(0, 3)
        text_product(3, 0, 4)
        text_over(6, 2)
        image_product(1, 2, 4)
        near_turn(1, 0)
        hand_over(1)
        image_product(2, 2, 4)
        near_turn(2, 2)
        hand_over(2)
        image_product(0, 2, 4)
        hand_over(0)
        text_came(6, 2)
        text_back(4)
        text_came(4, 2)
        text_back(3, (0,))

    @on(second)
    def _():
        text_hop(1)
        images_in(0)
        swapped(1)
        logits_block(0, 0)
        text_hop(2)
        swapped(2, 3)
        logits_block(0, 1)
        images_in(1, 0, 1)
        images_in(2, 2, 3)
        logits_block(1, 0, half=0)
        logits_block(2, 0, half=1)
        text_hop(3)
        logits_block(1, 1, half=0)
        logits_block(2, 1, half=1)
        swapped(4, 5)
        logits_block(0, 2)
        image_product(0, 0, 3)
        logits_block(1, 2, half=0)
        logits_block(2, 2, half=1)
        text_hop(4)
        images_in(1, 2, 3)
        images_in(2, 0, 1)
        logits_block(1, 0, half=1)
        logits_block(2, 0, half=0)
        logits_block(1, 1, half=1)
        text_product(0, 0, 3)
        logits_block(2, 1, half=0)
        logits_block(1, 2, half=1)
        text_product(1, 0, 3)
        logits_block(2, 2, half=0)
        swapped(6, 7)
        logits_block(1, 3)
        text_product(2, 0, 3)
        logits_block(2, 3)
        image_product(1, 0, 4)
        logits_block(0, 3)
        image_product(2, 0, 4)
        text_product(3, 0, 3)
        near_turn(1, 0)
        near_turn(2, 2)
        near_turn(1, 1)
        images_in(3)
        logits_block(3, 3)
        logits_block(3, 2)
        text_product(3, 3, 4)
        logits_block(3, 1)
        text_over(6, 2)
        logits_block(3, 0)
        image_product(3, 0, 4)
        far_turn(0)
        far_turn(2)
        far_turn(1)
        text_came(6, 2)
        text_back(4)
        text_product(2, 3, 4)
        text_over(4, 2)
        text_product(1, 3, 4)
        text_product(0, 3, 4)
        text_over(0, 4)
        handed(3)
        far_turn(3)
        text_came(4, 2)
        text_back(3, (0,))
        handed(2)
        near_turn(2, 3)
        image_product(0, 3, 4)

    near_turn(2, 0)
    near_turn(1, 2)
    text_back(3, (1,))

    ones = jnp.ones((8, HALF), F32)
    for i in range(4):
        ls[i] = lax.dot_general(
            ones,
            lacc[i * ROWS : (i + 1) * ROWS, :],
            (((1,), (1,)), ((), ())),
            precision=lax.Precision.HIGHEST,
            preferred_element_type=F32,
        )
    send(ls.at[2], lx.at[0], (lx_s, 0), lx_r.at[0], x_up)
    send(ls.at[1], lx.at[1], (lx_s, 1), lx_r.at[1], x_down)
    send(ls.at[3], lx.at[2], (lx_s, 2), lx_r.at[2], x_far)

    text_came(0, 4)
    text_back(2, (0,))

    @on(second)
    def _():
        near_turn(2, 1)
        handed(1)
        near_turn(1, 3)

    text_back(2, (1,))
    text_back(1, (0,))

    y_up0, y_down0 = at(x, y + 1, z, 0), at(x, y + 3, z, 0)

    def image_sum(k):
        landed(x2.at[0, seat(k)], x2_r.at[0, k])
        landed(x2.at[1, seat(k)], x2_r.at[1, k])
        return pacc[part_rows(0, k), :] + (x2[0, seat(k), :].astype(F32) + x2[1, seat(k), :].astype(F32))

    def image_out(k, box, to):
        total = image_sum(k)
        if core_of[0] == 1 and k == 0:
            landed(qr.at[3], y_r.at[3])
            total = total + qr[3].astype(F32)
        rb[seat(k), :] = total.astype(BF16)
        send(rb.at[seat(k)], qr.at[box], (y_s, k), y_r.at[box], to)

    core_of = [0]

    @on(first)
    def _():
        image_out(0, 3, y_up1)

    core_of[0] = 1

    @on(second)
    def _():
        image_out(2, 2, y_down0)

    text_back(1, (1,))

    @on(first)
    def _():
        qr[0] = image_sum(2).astype(BF16)

    @on(second)
    def _():
        qr[0] = jnp.zeros((QUARTER, WIDTH), BF16)
        image_out(0, 1, y_up0)

    source = yh + 2 * core
    block_yl = lax.rem(yl + core, 2)

    def owner_of(q):
        to = at(x, 2 * (q // 2) + block_yl, z, q % 2)
        return to, jnp.logical_and(dp == to[0], split == to[1])

    for k in range(3):
        landed(lx.at[k], lx_r.at[k])
    rl[...] = ls[0] + lx[0] + lx[1] + lx[2]
    for q in range(4):
        to, own = owner_of(q)
        send_when(jnp.logical_not(own), (rl, lq.at[source], (ly_s, q), ly_r.at[source], to))

        @pl.when(own)
        def _():
            lq[source] = rl[...]

    drain((i_s, t_s, d_s))
    mine = yh * 2 + core
    outs = (both_out.at[pl.ds(0, ROWS)], both_out.at[pl.ds(ROWS, ROWS)])

    def quarter_rows(q, start=0, count=QUARTER):
        return pl.ds(pl.multiple_of(q * QUARTER + start, EIGHTH), count)

    my_rows, my_other = quarter_rows(mine), quarter_rows(yh * 2 + other)
    y_up, y_down, y_far = (at(x, y + k, z, core) for k in (1, 3, 2))

    def gather_out(kind, grad, values):
        inverse, unit = unit_rows(values)
        out = outs[kind]
        out[my_rows, :] = unit_back(unit, inverse, sharp * grad).astype(BF16)
        if kind == 0:
            send(out.at[my_rows], out.at[my_rows], (g_s, 0, 0), g_r.at[0, 3], y_far)
        else:
            low, high = out.at[quarter_rows(mine, 0, EIGHTH)], out.at[quarter_rows(mine, EIGHTH, EIGHTH)]
            send(low, hop.at[kind, 0], (g_s, kind, 0), g_r.at[kind, 0], y_up)
            send(high, hop.at[kind, 1], (g_s, kind, 1), g_r.at[kind, 1], y_down)
        send(out.at[my_rows], out.at[my_rows], (g_s, kind, 2), g_r.at[kind, 2], sibling)

    def gather_on(kind):
        out = outs[kind]
        landed(hop.at[kind, 0], g_r.at[kind, 0])
        there = out.at[quarter_rows(2 * (1 - up_hi) + core, 0, EIGHTH)]
        send(hop.at[kind, 0], there, (g_s, kind, 3), g_r.at[kind, 3], y_up)
        landed(hop.at[kind, 1], g_r.at[kind, 1])
        there = out.at[quarter_rows(2 * up_hi + core, EIGHTH, EIGHTH)]
        send(hop.at[kind, 1], there, (g_s, kind, 4), g_r.at[kind, 4], y_down)

    def gather_over(kind):
        for half in (0, 1):
            here = outs[kind].at[quarter_rows((1 - yh) * 2 + core, half * EIGHTH, EIGHTH)]
            landed(here, g_r.at[kind, 3 + half])
            send(here, here, (g_s, kind, 5 + half), g_r.at[kind, 5 + half], sibling)

    def gather_end(kind):
        landed(outs[kind].at[quarter_rows(yh * 2 + other)], g_r.at[kind, 2])
        for half in (0, 1):
            here = outs[kind].at[quarter_rows((1 - yh) * 2 + other, half * EIGHTH, EIGHTH)]
            landed(here, g_r.at[kind, 5 + half])

    grads = []
    for piece in (0, 1):
        grad = text_sum(0, piece)
        for side in (0, 1):
            landed(vr.at[side, 0, piece_rows(piece)], v_r.at[side, 0, piece])
            grad = grad + vr[side, 0, piece_rows(piece), :].astype(F32)
        grads.append(grad)
    grad = jnp.concatenate(grads, axis=0)
    gather_out(1, grad, cap[pl.ds(pl.multiple_of(core * QUARTER, QUARTER), QUARTER), :])

    @on(second)
    def _():
        image_out(1, 1, y_up1)
        handed(0)
        image_out(3, 2, y_down1)

    gather_on(1)

    for k in range(4):
        here = jnp.logical_and(first, yh == k)

        @pl.when(jnp.logical_not(here))
        def _():
            landed(lq.at[k], ly_r.at[k])

    loss_out[...] = ((lq[0] + lq[1]) + (lq[2] + lq[3])) * (1.0 / PAIRS)

    drain((e_s, v_s, x1_s, x2_s, yc_s, lx_s))
    landed(qr.at[1], y_r.at[1])
    landed(qr.at[2], y_r.at[2])
    grad = qr[0].astype(F32) + (qr[1].astype(F32) + qr[2].astype(F32))
    gather_out(0, grad, pic[my_rows, :])
    gather_over(1)
    drain()
    for cond, rows, ssem in pending:

        @pl.when(cond)
        def _():
            sent(rows, ssem)

    pending.clear()
    gather_end(1)
    far_rows, last_rows = quarter_rows((1 - yh) * 2 + core), quarter_rows((1 - yh) * 2 + other)
    landed(outs[0].at[far_rows], g_r.at[0, 3])
    send(outs[0].at[far_rows], outs[0].at[far_rows], (g_s, 0, 5), g_r.at[0, 5], sibling)
    landed(outs[0].at[my_other], g_r.at[0, 2])
    landed(outs[0].at[last_rows], g_r.at[0, 5])
    drain()


def per_device(picture_vectors, caption_vectors, sharpness_entry, offset_shift):
    dma = pltpu.SemaphoreType.DMA
    vmem = pl.BlockSpec(memory_space=pltpu.VMEM)
    smem = pl.BlockSpec(memory_space=pltpu.SMEM)
    hbm = pl.BlockSpec(memory_space=pltpu.HBM)
    both, loss = pl.pallas_call(
        kernel,
        out_shape=(
            jax.ShapeDtypeStruct((2 * ROWS, WIDTH), BF16),
            jax.ShapeDtypeStruct((8, ROWS), F32),
        ),
        in_specs=[hbm, hbm, smem, smem],
        out_specs=(vmem, vmem),
        scratch_shapes=[
            pltpu.VMEM((ROWS, WIDTH), BF16),
            pltpu.VMEM((HALF, WIDTH), BF16),
            pltpu.VMEM((4 * ROWS, WIDTH), BF16),
            pltpu.VMEM((8 * HALF, WIDTH), BF16),
            pltpu.VMEM((4 * ROWS, 8 * HALF), BF16),
            pltpu.VMEM((8 * HALF, 4 * ROWS), BF16),
            pltpu.VMEM((4 * ROWS, WIDTH), F32),
            pltpu.VMEM((8 * HALF, WIDTH), F32),
            pltpu.VMEM((4 * ROWS, HALF), F32),
            pltpu.VMEM((3, ROWS, WIDTH), BF16),
            pltpu.VMEM((ROWS, WIDTH), BF16),
            pltpu.VMEM((2, ROWS, WIDTH), BF16),
            pltpu.VMEM((ROWS, WIDTH), BF16),
            pltpu.VMEM((4, QUARTER, WIDTH), BF16),
            pltpu.VMEM((2, 4, QUARTER, WIDTH), BF16),
            pltpu.VMEM((2, 4, QUARTER, WIDTH), BF16),
            pltpu.VMEM((8, QUARTER, WIDTH), BF16),
            pltpu.VMEM((8, QUARTER, WIDTH), BF16),
            pltpu.VMEM((2, 4, QUARTER, WIDTH), BF16),
            pltpu.VMEM((2, 4, QUARTER, WIDTH), BF16),
            pltpu.VMEM((4, 8, ROWS), F32),
            pltpu.VMEM((3, 8, ROWS), F32),
            pltpu.VMEM((8, ROWS), F32),
            pltpu.VMEM((4, 8, ROWS), F32),
            pltpu.VMEM((2, 2, EIGHTH, WIDTH), BF16),
            dma((2,)),
            dma((7, 4)), dma((4, 4)),
            dma((2, 4, 2)), dma((2, 4, 2)),
            dma((8,)), dma((8,)),
            dma((4,)), dma((4,)),
            dma((2, 4)), dma((2, 4)),
            dma((4,)), dma((4,)),
            dma((2, 4)), dma((2, 4)),
            dma((4,)), dma((4,)),
            dma((3,)), dma((3,)),
            dma((8,)), dma((8,)),
            dma((2, 4, 2)), dma((2, 4, 2)),
            dma((2, 7)), dma((2, 7)),
        ],
        compiler_params=pltpu.CompilerParams(
            collective_id=0, has_side_effects=True, vmem_limit_bytes=48 * 1024 * 1024
        ),
        cost_estimate=pl.CostEstimate(flops=7_300_000_000, bytes_accessed=4_000_000, transcendentals=3_000_000),
    )(
        pltpu.with_memory_space_constraint(picture_vectors, pltpu.HBM),
        pltpu.with_memory_space_constraint(caption_vectors, pltpu.HBM),
        sharpness_entry,
        offset_shift,
    )
    return both[:ROWS].astype(F32), both[ROWS:].astype(F32), loss[0]


def solution(mesh):
    placed = (P("dp", None), P("dp", None), P(), P())
    return jax.shard_map(
        per_device,
        mesh=mesh,
        in_specs=placed,
        out_specs=(P("dp", None), P("dp", None), P("dp")),
        check_vma=False,
    )
```

```python
import jax
import jax.numpy as jnp
from jax import lax
from jax.experimental import pallas as pl
from jax.experimental.pallas import tpu as pltpu
from jax.sharding import PartitionSpec as P

MESH = pl.DeviceIdType.MESH
F32 = jnp.float32
BF16 = jnp.bfloat16

NX, NY, NZ = 4, 4, 8
ROWS, WIDTH = 256, 1152
HALF, QUARTER, EIGHTH = 128, 64, 32
PAIRS = 16384


def unit_rows(values):
    values = values.astype(F32)
    inverse = lax.rsqrt(jnp.sum(values * values, axis=1, keepdims=True) + 1e-06)
    return inverse, values * inverse


def unit_back(unit, inverse, grad):
    return (grad - unit * jnp.sum(unit * grad, axis=1, keepdims=True)) * inverse


def contract(a, b, dims):
    return lax.dot_general(a, b, (dims, ((), ())), preferred_element_type=F32)


def kernel(
    pic_hbm, cap_hbm, sharp_ref, off_ref,
    both_out, loss_out,
    pic, cap, ibuf, jbuf, cbuf, ctbuf, pacc, tacc, lacc,
    pb, xr1, x2, rb, qr, ys, yr,
    ts, tr, vs, vr,
    ls, lx, rl, lq,
    in_sem, i_s, i_r, t_s, t_r, d_s, d_r, x1_s, x1_r, x2_s, x2_r, y_s, y_r, yc_s, yc_r,
    ly_s, ly_r, lx_s, lx_r, e_s, e_r, v_s, v_r, g_s, g_r,
):
    dp, split = lax.axis_index("dp"), lax.axis_index("split")
    x = lax.rem(dp, NX)
    yl = lax.rem(dp // NX, 2)
    z = dp // (2 * NX)
    yh, core = split // 2, lax.rem(split, 2)
    y = 2 * yh + yl
    other = 1 - core
    first = core == 0
    second = core == 1

    def at(px, py, pz, pc):
        px, py, pz = lax.rem(px, NX), lax.rem(py, NY), lax.rem(pz, NZ)
        return ((pz * 2 + lax.rem(py, 2)) * NX + px, (py // 2) * 2 + pc)

    sibling = at(x, y, z, other)
    x_up, x_down, x_far = (at(x + k, y, z, core) for k in (1, 3, 2))
    z_up, z_down = at(x, y, z + 1, core), at(x, y, z + 7, core)
    y_up1, y_down1 = at(x, y + 1, z, 1), at(x, y + 3, z, 1)

    own_text = pl.multiple_of(yh * HALF, HALF)
    fetch_text = pltpu.make_async_copy(cap_hbm.at[pl.ds(own_text, HALF)], cap, in_sem.at[0])
    fetch_image = pltpu.make_async_copy(pic_hbm, pic, in_sem.at[1])
    fetch_text.start()
    fetch_image.start()

    barrier = pltpu.get_barrier_semaphore()
    partners = [sibling, x_up, x_down, x_far, z_up, z_down]
    partners += [at(x, y + k, z, c) for k in (1, 2, 3) for c in (0, 1)]
    for partner in partners:
        pl.semaphore_signal(barrier, inc=1, device_id=partner, device_id_type=MESH)

    pending = []

    def copy(src, dst, send, recv, to):
        return pltpu.make_async_remote_copy(
            src_ref=src, dst_ref=dst, send_sem=send[0].at[send[1:]], recv_sem=recv, device_id=to, device_id_type=MESH
        )

    def note(cond, src, ssem):
        rows = 0 if src.dtype == F32 else src.shape[0] * (src.shape[1] if len(src.shape) == 3 else 1)
        pending.append((cond, rows, ssem))

    def sent(rows, ssem):
        ref = ibuf.at[pl.ds(0, rows)] if rows else ls.at[0]
        copy(ref, ref, ssem, e_r.at[0], sibling).wait_send()

    branch = [None]

    def on(cond):
        def run(body):
            branch[0] = cond
            pl.when(cond)(body)
            branch[0] = None

        return run

    def send(src, dst, ssem, rsem, to):
        copy(src, dst, ssem, rsem, to).start()
        note(branch[0], src, ssem)

    def send_when(cond, *copies):
        @pl.when(cond)
        def _():
            for one in copies:
                copy(*one).start()

        for one in copies:
            note(cond, one[0], one[2])

    def drain(of=None):
        later = [entry for entry in pending if of is not None and not any(entry[2][0] is sem for sem in of)]
        pending[:] = [entry for entry in pending if not any(entry is k for k in later)]
        for cond in (None, first, second):
            some = [entry[1:] for entry in pending if entry[0] is cond]
            if cond is None:
                for entry in some:
                    sent(*entry)
            elif some:

                @pl.when(cond)
                def _():
                    for entry in some:
                        sent(*entry)

        pending[:] = later + [entry for entry in pending if not any(entry[0] is k for k in (None, first, second))]

    def landed(dst, rsem):
        copy(dst, dst, (e_s, 0), rsem, sibling).wait_recv()


    fetch_text.wait()
    jbuf[0:HALF, :] = unit_rows(cap[...])[1].astype(BF16)
    pl.semaphore_wait(barrier, len(partners))

    def irows(slot, piece):
        return ibuf.at[pl.ds(slot * ROWS + piece * QUARTER, QUARTER)]

    def jrows(slot, c, start=0, count=QUARTER):
        return jbuf.at[pl.ds(pl.multiple_of(slot * HALF + c * QUARTER + start, EIGHTH), count)]

    def text_piece(slot, piece):
        return jrows(slot, core, piece * EIGHTH, EIGHTH)

    def text_send(side, d, piece, source, target):
        send(
            text_piece(source, piece),
            text_piece(target, piece),
            (t_s, side, d, piece),
            t_r.at[side, d, piece],
            z_down if side else z_up,
        )

    for piece in (0, 1):
        text_send(0, 0, piece, 0, 2)
        text_send(1, 0, piece, 0, 1)

    def to_y(slot, piece):
        target = y_up1 if piece < 2 else y_down1
        return (irows(slot, piece), irows(slot, piece), (i_s, 2 + slot, piece), i_r.at[slot, piece], target)

    def to_x(source, slot, piece, kind):
        target = x_up if slot == 1 or (slot == 3 and piece < 2) else x_down
        return (irows(source, piece), irows(slot, piece), (i_s, kind, piece), i_r.at[slot, piece], target)

    fetch_image.wait()

    @pl.when(first)
    def _():
        ibuf[0:ROWS, :] = unit_rows(pic[...])[1].astype(BF16)

    send_when(
        first,
        to_x(0, 1, 0, 0), to_x(0, 2, 2, 1), to_y(0, 0), to_y(0, 2),
        to_x(0, 1, 1, 0), to_x(0, 2, 3, 1), to_y(0, 1), to_y(0, 3),
        to_x(0, 1, 2, 0), to_x(0, 2, 0, 1), to_x(0, 1, 3, 0), to_x(0, 2, 1, 1),
    )

    def pass_near(up, down, onward):
        landed(irows(1, up), i_r.at[1, up])
        if onward:
            send(*to_x(1, 3, up, 6))
        send(*to_y(1, up))
        landed(irows(2, down), i_r.at[2, down])
        if onward:
            send(*to_x(2, 3, down, 6))
        send(*to_y(2, down))

    def pass_far(*pieces):
        for piece in pieces:
            landed(irows(3, piece), i_r.at[3, piece])
            send(*to_y(3, piece))

    def images_in(slot, *pieces):
        for piece in pieces or range(4):
            landed(irows(slot, piece), i_r.at[slot, piece])

    for zeroed in (lacc,):

        def clear(n, carry):
            rows = pl.ds(pl.multiple_of(n * QUARTER, QUARTER), QUARTER)
            zeroed[rows, :] = jnp.zeros((QUARTER, zeroed.shape[1]), F32)
            return carry

        lax.fori_loop(0, 16, clear, 0)

    def swap(slot):
        send(jrows(slot, core), jrows(slot, core), (d_s, slot), d_r.at[slot], sibling)

    def swapped(*slots):
        for slot in slots:
            landed(jrows(slot, other), d_r.at[slot])

    def text_hop(d, pieces=(0, 1)):
        for piece in pieces:
            for side in (0, 1):
                if d == 4:
                    if piece == side:
                        landed(text_piece(7, piece), t_r.at[side, 3, piece])
                    continue
                here = 2 * d - side
                landed(text_piece(here, piece), t_r.at[side, d - 1, piece])
                if d < 3:
                    text_send(side, d, piece, here, here + 2)
                elif piece == side:
                    text_send(side, 3, piece, here, 7)
        if pieces[-1] == 0:
            return
        if d < 4:
            swap(2 * d - 1)
            swap(2 * d)
        else:
            swap(7)

    sharp, off = sharp_ref[0], off_ref[0]
    log2_e = 1.4426950408889634
    sharp2, off2 = sharp * log2_e, off * log2_e

    def logits_block(i, j, diagonal=False, half=None):
        start = i * ROWS + (half or 0) * HALF
        ri = slice(start, start + (ROWS if half is None else HALF))
        rj = slice(j * ROWS, (j + 1) * ROWS)
        logits = sharp2 * contract(ibuf[ri, :], jbuf[rj, :], ((1,), (1,))) + off2
        if diagonal:
            row = lax.broadcasted_iota(jnp.int32, (ROWS, ROWS), 0)
            col = lax.broadcasted_iota(jnp.int32, (ROWS, ROWS), 1)
            same = jnp.logical_and(row == col + yh * HALF, col < HALF)
            logits = jnp.where(same, -logits, logits)
        grown = jnp.exp2(logits)
        total = 1.0 + grown
        rough = pl.reciprocal(total, approx=True)
        inverse = rough * (2.0 - total * rough)
        coef = grown * inverse
        lost = (grown - (total - 1.0)) * inverse
        lacc[ri, :] += jnp.log(total[:, :HALF] * total[:, HALF:]) + (lost[:, :HALF] + lost[:, HALF:])
        if diagonal:
            coef = jnp.where(same, -coef, coef)
        coef = coef.astype(BF16)
        cbuf[ri, rj] = coef
        ctbuf[rj, ri] = coef.T

    def product(out, left, right, m, k0, k1):
        rows, depth = slice(m * ROWS, (m + 1) * ROWS), slice(k0 * ROWS, k1 * ROWS)
        a = left[rows, depth]
        for n in range(0, WIDTH, 256):
            columns = slice(n, min(n + 256, WIDTH))
            result = contract(a, right[depth, columns], ((1,), (0,)))
            out[rows, columns] = result if k0 == 0 else out[rows, columns] + result

    def image_product(i, j0, j1):
        product(pacc, cbuf, jbuf, i, j0, j1)

    def text_product(j, i0, i1):
        product(tacc, ctbuf, ibuf, j, i0, i1)

    up_hi = lax.rem(y + 1, NY) // 2
    turns = (
        other * 2 * (1 - yh) + core * 2 * up_hi,
        core * (2 * up_hi + 1),
        other * 2 * yh + core * 2 * (1 - up_hi),
        core * (2 * (1 - up_hi) + 1),
    )

    def hand_over(slot):
        for side, q, to in ((0, 2 * yh + 1, y_up1), (1, 2 * (1 - yh) + 1, y_down1)):
            rows = pl.ds(pl.multiple_of(slot * ROWS + q * QUARTER, QUARTER), QUARTER)
            ys[side, slot] = pacc[rows, :].astype(BF16)
            send(ys.at[side, slot], yr.at[side, slot], (yc_s, side, slot), yc_r.at[side, slot], to)

    def handed(slot):
        rows = part_rows(slot, 3)
        for side in (0, 1):
            landed(yr.at[side, slot], yc_r.at[side, slot])
        pacc[rows, :] += yr[0, slot].astype(F32) + yr[1, slot].astype(F32)

    def seat(k):
        return pl.ds(k * QUARTER, QUARTER)

    def part_rows(slot, k):
        return pl.ds(pl.multiple_of(slot * ROWS + turns[k] * QUARTER, QUARTER), QUARTER)

    def far_turn(k):
        pb[0, seat(k), :] = pacc[part_rows(3, k), :].astype(BF16)
        send(pb.at[0, seat(k)], xr1.at[seat(k)], (x1_s, k), x1_r.at[k], x_up if k < 2 else x_down)

    def near_turn(slot, k):
        side = 0 if slot == 2 else 1
        rows = pacc[part_rows(slot, k), :]
        if (k < 2) == (slot == 2):
            landed(xr1.at[seat(k)], x1_r.at[k])
            rows = rows + xr1[seat(k), :].astype(F32)
        pb[1 + side, seat(k), :] = rows.astype(BF16)
        send(
            pb.at[1 + side, seat(k)],
            x2.at[side, seat(k)],
            (x2_s, side, k),
            x2_r.at[side, k],
            x_down if side else x_up,
        )

    def text_over(low, count):
        for slot in range(low, low + count):
            mine = pl.ds(pl.multiple_of(slot * HALF + other * QUARTER, QUARTER), QUARTER)
            ts[slot] = tacc[mine, :].astype(BF16)
        slots = pl.ds(low, count)
        send(ts.at[slots], tr.at[slots], (e_s, low), e_r.at[low], sibling)

    def text_came(low, count):
        landed(tr.at[pl.ds(low, count)], e_r.at[low])

    def piece_rows(piece):
        return pl.ds(piece * EIGHTH, EIGHTH)

    def text_sum(slot, piece):
        start = slot * HALF + core * QUARTER + piece * EIGHTH
        return tacc[pl.ds(pl.multiple_of(start, EIGHTH), EIGHTH), :] + tr[slot, piece_rows(piece), :].astype(F32)

    def text_back(d, steps=(0, 1)):
        for step in steps:
            for side in (0, 1):
                piece = step if side else 1 - step
                if d == 4 and piece != side:
                    continue
                rows = text_sum(7 if d == 4 else 2 * d - 1 + side, piece)
                part = piece_rows(piece)
                if d < 3 or (d == 3 and piece == side):
                    landed(vr.at[side, d, part], v_r.at[side, d, piece])
                    rows = rows + vr[side, d, part, :].astype(F32)
                vs[side, d - 1, part, :] = rows.astype(BF16)
                send(
                    vs.at[side, d - 1, part],
                    vr.at[side, d - 1, part],
                    (v_s, side, d - 1, piece),
                    v_r.at[side, d - 1, piece],
                    z_down if side else z_up,
                )

    @on(first)
    def _():
        text_hop(1, (0,))
        pass_near(0, 2, True)
        text_hop(1, (1,))
        pass_near(1, 3, True)
        swapped(1)
        logits_block(0, 0, True)
        pass_near(2, 0, False)
        text_hop(2, (0,))
        text_hop(2, (1,))
        pass_near(3, 1, False)
        swapped(2, 3)
        logits_block(0, 1)
        pass_far(0, 2)
        logits_block(1, 0)
        logits_block(2, 0)
        image_product(0, 0, 2)
        text_hop(3)
        pass_far(1, 3)
        logits_block(1, 1)
        logits_block(2, 1)
        image_product(1, 0, 2)
        logits_block(3, 0)
        image_product(2, 0, 2)
        logits_block(3, 1)
        swapped(4, 5)
        text_hop(4)
        text_product(0, 0, 4)
        logits_block(0, 2)
        text_product(1, 0, 4)
        logits_block(1, 2)
        image_product(3, 0, 2)
        logits_block(2, 2)
        logits_block(3, 2)
        text_product(2, 0, 4)
        text_over(0, 4)
        text_over(4, 2)
        swapped(6, 7)
        logits_block(3, 3)
        logits_block(1, 3)
        image_product(3, 2, 4)
        far_turn(0)
        far_turn(2)
        hand_over(3)
        logits_block(2, 3)
        logits_block(0, 3)
        text_product(3, 0, 4)
        text_over(6, 2)
        image_product(1, 2, 4)
        near_turn(1, 0)
        hand_over(1)
        image_product(2, 2, 4)
        near_turn(2, 2)
        hand_over(2)
        image_product(0, 2, 4)
        hand_over(0)
        text_came(6, 2)
        text_back(4)
        text_came(4, 2)
        text_back(3, (0,))

    @on(second)
    def _():
        text_hop(1)
        images_in(0)
        swapped(1)
        logits_block(0, 0)
        text_hop(2)
        swapped(2, 3)
        logits_block(0, 1)
        images_in(1, 0, 1)
        images_in(2, 2, 3)
        logits_block(1, 0, half=0)
        logits_block(2, 0, half=1)
        text_hop(3)
        logits_block(1, 1, half=0)
        logits_block(2, 1, half=1)
        swapped(4, 5)
        logits_block(0, 2)
        image_product(0, 0, 3)
        logits_block(1, 2, half=0)
        logits_block(2, 2, half=1)
        text_hop(4)
        images_in(1, 2, 3)
        images_in(2, 0, 1)
        logits_block(1, 0, half=1)
        logits_block(2, 0, half=0)
        logits_block(1, 1, half=1)
        text_product(0, 0, 3)
        logits_block(2, 1, half=0)
        logits_block(1, 2, half=1)
        text_product(1, 0, 3)
        logits_block(2, 2, half=0)
        swapped(6, 7)
        logits_block(1, 3)
        text_product(2, 0, 3)
        logits_block(2, 3)
        image_product(1, 0, 4)
        logits_block(0, 3)
        image_product(2, 0, 4)
        text_product(3, 0, 3)
        near_turn(1, 0)
        near_turn(2, 2)
        near_turn(1, 1)
        images_in(3)
        logits_block(3, 3)
        logits_block(3, 2)
        text_product(3, 3, 4)
        logits_block(3, 1)
        text_over(6, 2)
        logits_block(3, 0)
        image_product(3, 0, 4)
        far_turn(0)
        far_turn(2)
        far_turn(1)
        text_came(6, 2)
        text_back(4)
        text_product(2, 3, 4)
        text_over(4, 2)
        text_product(1, 3, 4)
        text_product(0, 3, 4)
        text_over(0, 4)
        handed(3)
        far_turn(3)
        text_came(4, 2)
        text_back(3, (0,))
        handed(2)
        near_turn(2, 3)
        image_product(0, 3, 4)

    near_turn(2, 0)
    near_turn(1, 2)
    text_back(3, (1,))

    ones = jnp.ones((8, HALF), F32)
    for i in range(4):
        ls[i] = lax.dot_general(
            ones,
            lacc[i * ROWS : (i + 1) * ROWS, :],
            (((1,), (1,)), ((), ())),
            precision=lax.Precision.HIGHEST,
            preferred_element_type=F32,
        )
    send(ls.at[2], lx.at[0], (lx_s, 0), lx_r.at[0], x_up)
    send(ls.at[1], lx.at[1], (lx_s, 1), lx_r.at[1], x_down)
    send(ls.at[3], lx.at[2], (lx_s, 2), lx_r.at[2], x_far)

    text_came(0, 4)
    text_back(2, (0,))

    @on(second)
    def _():
        near_turn(2, 1)
        handed(1)
        near_turn(1, 3)

    text_back(2, (1,))
    text_back(1, (0,))

    y_up0, y_down0 = at(x, y + 1, z, 0), at(x, y + 3, z, 0)

    def image_sum(k):
        landed(x2.at[0, seat(k)], x2_r.at[0, k])
        landed(x2.at[1, seat(k)], x2_r.at[1, k])
        return pacc[part_rows(0, k), :] + (x2[0, seat(k), :].astype(F32) + x2[1, seat(k), :].astype(F32))

    def image_out(k, box, to):
        total = image_sum(k)
        rb[seat(k), :] = total.astype(BF16)
        send(rb.at[seat(k)], qr.at[box], (y_s, k), y_r.at[box], to)

    @on(first)
    def _():
        image_out(0, 3, at(x, y + 2, z, 0))

    @on(second)
    def _():
        image_out(2, 2, y_down0)
        image_out(0, 1, y_up0)

    text_back(1, (1,))

    @on(first)
    def _():
        qr[0] = image_sum(2).astype(BF16)

    @on(second)
    def _():
        qr[0] = jnp.zeros((QUARTER, WIDTH), BF16)
        qr[3] = jnp.zeros((QUARTER, WIDTH), BF16)

    source = yh + 2 * core
    block_yl = lax.rem(yl + core, 2)

    def owner_of(q):
        to = at(x, 2 * (q // 2) + block_yl, z, q % 2)
        return to, jnp.logical_and(dp == to[0], split == to[1])

    for k in range(3):
        landed(lx.at[k], lx_r.at[k])
    rl[...] = ls[0] + lx[0] + lx[1] + lx[2]
    for q in range(4):
        to, own = owner_of(q)
        send_when(jnp.logical_not(own), (rl, lq.at[source], (ly_s, q), ly_r.at[source], to))

        @pl.when(own)
        def _():
            lq[source] = rl[...]

    drain((i_s, t_s, d_s))
    mine = yh * 2 + core
    outs = (both_out.at[pl.ds(0, ROWS)], both_out.at[pl.ds(ROWS, ROWS)])

    def quarter_rows(q, start=0, count=QUARTER):
        return pl.ds(pl.multiple_of(q * QUARTER + start, EIGHTH), count)

    my_rows, my_other = quarter_rows(mine), quarter_rows(yh * 2 + other)
    y_far = at(x, y + 2, z, core)

    far_rows, last_rows = quarter_rows((1 - yh) * 2 + core), quarter_rows((1 - yh) * 2 + other)

    def gather_out(kind, grad, values):
        inverse, unit = unit_rows(values)
        out = outs[kind]
        out[my_rows, :] = unit_back(unit, inverse, sharp * grad).astype(BF16)
        here = out.at[my_rows]
        send(here, here, (g_s, kind, 0), g_r.at[kind, 0], y_far)
        send(here, here, (g_s, kind, 1), g_r.at[kind, 1], sibling)

    def gather_over(kind):
        here = outs[kind].at[far_rows]
        landed(here, g_r.at[kind, 0])
        send(here, here, (g_s, kind, 2), g_r.at[kind, 2], sibling)

    def gather_end(kind):
        landed(outs[kind].at[my_other], g_r.at[kind, 1])
        landed(outs[kind].at[last_rows], g_r.at[kind, 2])

    grads = []
    for piece in (0, 1):
        grad = text_sum(0, piece)
        for side in (0, 1):
            landed(vr.at[side, 0, piece_rows(piece)], v_r.at[side, 0, piece])
            grad = grad + vr[side, 0, piece_rows(piece), :].astype(F32)
        grads.append(grad)
    grad = jnp.concatenate(grads, axis=0)
    gather_out(1, grad, cap[pl.ds(pl.multiple_of(core * QUARTER, QUARTER), QUARTER), :])

    @on(second)
    def _():
        image_out(1, 1, y_up1)
        handed(0)
        image_out(3, 2, y_down1)

    for k in range(4):
        here = jnp.logical_and(first, yh == k)

        @pl.when(jnp.logical_not(here))
        def _():
            landed(lq.at[k], ly_r.at[k])

    loss_out[...] = ((lq[0] + lq[1]) + (lq[2] + lq[3])) * (1.0 / PAIRS)

    drain((e_s, v_s, x1_s, x2_s, yc_s, lx_s))
    landed(qr.at[1], y_r.at[1])
    landed(qr.at[2], y_r.at[2])

    @on(first)
    def _():
        landed(qr.at[3], y_r.at[3])

    grad = (qr[0].astype(F32) + qr[3].astype(F32)) + (qr[1].astype(F32) + qr[2].astype(F32))
    gather_out(0, grad, pic[my_rows, :])
    gather_over(1)
    drain()
    for cond, rows, ssem in pending:

        @pl.when(cond)
        def _():
            sent(rows, ssem)

    pending.clear()
    gather_over(0)
    gather_end(1)
    gather_end(0)
    drain()


def per_device(picture_vectors, caption_vectors, sharpness_entry, offset_shift):
    dma = pltpu.SemaphoreType.DMA
    vmem = pl.BlockSpec(memory_space=pltpu.VMEM)
    smem = pl.BlockSpec(memory_space=pltpu.SMEM)
    hbm = pl.BlockSpec(memory_space=pltpu.HBM)
    both, loss = pl.pallas_call(
        kernel,
        out_shape=(
            jax.ShapeDtypeStruct((2 * ROWS, WIDTH), BF16),
            jax.ShapeDtypeStruct((8, ROWS), F32),
        ),
        in_specs=[hbm, hbm, smem, smem],
        out_specs=(vmem, vmem),
        scratch_shapes=[
            pltpu.VMEM((ROWS, WIDTH), BF16),
            pltpu.VMEM((HALF, WIDTH), BF16),
            pltpu.VMEM((4 * ROWS, WIDTH), BF16),
            pltpu.VMEM((8 * HALF, WIDTH), BF16),
            pltpu.VMEM((4 * ROWS, 8 * HALF), BF16),
            pltpu.VMEM((8 * HALF, 4 * ROWS), BF16),
            pltpu.VMEM((4 * ROWS, WIDTH), F32),
            pltpu.VMEM((8 * HALF, WIDTH), F32),
            pltpu.VMEM((4 * ROWS, HALF), F32),
            pltpu.VMEM((3, ROWS, WIDTH), BF16),
            pltpu.VMEM((ROWS, WIDTH), BF16),
            pltpu.VMEM((2, ROWS, WIDTH), BF16),
            pltpu.VMEM((ROWS, WIDTH), BF16),
            pltpu.VMEM((4, QUARTER, WIDTH), BF16),
            pltpu.VMEM((2, 4, QUARTER, WIDTH), BF16),
            pltpu.VMEM((2, 4, QUARTER, WIDTH), BF16),
            pltpu.VMEM((8, QUARTER, WIDTH), BF16),
            pltpu.VMEM((8, QUARTER, WIDTH), BF16),
            pltpu.VMEM((2, 4, QUARTER, WIDTH), BF16),
            pltpu.VMEM((2, 4, QUARTER, WIDTH), BF16),
            pltpu.VMEM((4, 8, ROWS), F32),
            pltpu.VMEM((3, 8, ROWS), F32),
            pltpu.VMEM((8, ROWS), F32),
            pltpu.VMEM((4, 8, ROWS), F32),
            dma((2,)),
            dma((7, 4)), dma((4, 4)),
            dma((2, 4, 2)), dma((2, 4, 2)),
            dma((8,)), dma((8,)),
            dma((4,)), dma((4,)),
            dma((2, 4)), dma((2, 4)),
            dma((4,)), dma((4,)),
            dma((2, 4)), dma((2, 4)),
            dma((4,)), dma((4,)),
            dma((3,)), dma((3,)),
            dma((8,)), dma((8,)),
            dma((2, 4, 2)), dma((2, 4, 2)),
            dma((2, 3)), dma((2, 3)),
        ],
        compiler_params=pltpu.CompilerParams(
            collective_id=0, has_side_effects=True, vmem_limit_bytes=48 * 1024 * 1024
        ),
        cost_estimate=pl.CostEstimate(flops=7_300_000_000, bytes_accessed=4_000_000, transcendentals=3_000_000),
    )(
        pltpu.with_memory_space_constraint(picture_vectors, pltpu.HBM),
        pltpu.with_memory_space_constraint(caption_vectors, pltpu.HBM),
        sharpness_entry,
        offset_shift,
    )
    return both[:ROWS].astype(F32), both[ROWS:].astype(F32), loss[0]


def solution(mesh):
    placed = (P("dp", None), P("dp", None), P(), P())
    return jax.shard_map(
        per_device,
        mesh=mesh,
        in_specs=placed,
        out_specs=(P("dp", None), P("dp", None), P("dp")),
        check_vma=False,
    )
```
